32 devices in a mesh: head: 2 (over x), seq: 16 (over z, y, core).
Axes of the slice: x: 2, y: 2, z: 4, core: 2. Of those that a mesh axis runs over, the one named last changes fastest.
Arguments:
- inputs: bfloat16 [2, 4096, 768], P(None, ('seq', 'head')), may hold values from -6 to 6
- cotangent: bfloat16 [2, 4096, 768], P(None, ('seq', 'head')), may hold values from -6 to 6
- lengths: int32 [2, 1, 8], replicated, may hold values from 1 to 1024, 4096 in all within a row
- qkv_weight: float32 [2, 768, 2304], P(None, ('head', 'seq')), may hold values from -0.21875 to 0.21875
- qkv_first: float32 [2, 768, 2304], P(None, ('head', 'seq')), may hold values from -160 to 160
- qkv_second: float32 [2, 768, 2304], P(None, ('head', 'seq')), may hold values from 409.6 to 3276.8
- out_weight: float32 [2, 768, 768], P(None, ('head', 'seq')), may hold values from -0.875 to 0.875
- out_first: float32 [2, 768, 768], P(None, ('head', 'seq')), may hold values from -160 to 160
- out_second: float32 [2, 768, 768], P(None, ('head', 'seq')), may hold values from 409.6 to 3276.8
- up_weight: float32 [2, 768, 6144], P(None, ('head', 'seq')), may hold values from -0.21875 to 0.21875
- up_first: float32 [2, 768, 6144], P(None, ('head', 'seq')), may hold values from -160 to 160
- up_second: float32 [2, 768, 6144], P(None, ('head', 'seq')), may hold values from 409.6 to 3276.8
- down_weight: float32 [2, 3072, 768], P(None, ('head', 'seq')), may hold values from -0.109375 to 0.109375
- down_first: float32 [2, 3072, 768], P(None, ('head', 'seq')), may hold values from -160 to 160
- down_second: float32 [2, 3072, 768], P(None, ('head', 'seq')), may hold values from 409.6 to 3276.8
- norm_params: float32 [2, 768, 4], P(None, ('head', 'seq')), may hold values from -1.2 to 1.65, as said below
- norm_first: float32 [2, 768, 4], P(None, ('head', 'seq')), may hold values from -512 to 512
- norm_second: float32 [2, 768, 4], P(None, ('head', 'seq')), may hold values from 8192 to 32768
Outputs:
- outputs: float32 [2, 4096, 768], P(None, ('seq', 'head'))
- input_grad: float32 [2, 4096, 768], P(None, ('seq', 'head'))
- qkv_grad: float32 [2, 768, 2304], P(None, ('head', 'seq'))
- qkv_first_new: float32 [2, 768, 2304], P(None, ('head', 'seq'))
- qkv_second_new: float32 [2, 768, 2304], P(None, ('head', 'seq'))
- qkv_weight_new: float32 [2, 768, 2304], P(None, ('head', 'seq'))
- out_grad: float32 [2, 768, 768], P(None, ('head', 'seq'))
- out_first_new: float32 [2, 768, 768], P(None, ('head', 'seq'))
- out_second_new: float32 [2, 768, 768], P(None, ('head', 'seq'))
- out_weight_new: float32 [2, 768, 768], P(None, ('head', 'seq'))
- up_grad: float32 [2, 768, 6144], P(None, ('head', 'seq'))
- up_first_new: float32 [2, 768, 6144], P(None, ('head', 'seq'))
- up_second_new: float32 [2, 768, 6144], P(None, ('head', 'seq'))
- up_weight_new: float32 [2, 768, 6144], P(None, ('head', 'seq'))
- down_grad: float32 [2, 3072, 768], P(None, ('head', 'seq'))
- down_first_new: float32 [2, 3072, 768], P(None, ('head', 'seq'))
- down_second_new: float32 [2, 3072, 768], P(None, ('head', 'seq'))
- down_weight_new: float32 [2, 3072, 768], P(None, ('head', 'seq'))
- norm_grad: float32 [2, 768, 4], P(None, ('head', 'seq'))
- norm_first_new: float32 [2, 768, 4], P(None, ('head', 'seq'))
- norm_second_new: float32 [2, 768, 4], P(None, ('head', 'seq'))
- norm_params_new: float32 [2, 768, 4], P(None, ('head', 'seq'))
- qkv_copy: bfloat16 [2, 768, 2304], P(None, ('head', 'seq'))
- out_copy: bfloat16 [2, 768, 768], P(None, ('head', 'seq'))
- up_copy: bfloat16 [2, 768, 6144], P(None, ('head', 'seq'))
- down_copy: bfloat16 [2, 3072, 768], P(None, ('head', 'seq'))
The draws below stay inside these ranges and needn't reach their ends.
Inputs may be any that keep to these rules, and one draw needn't show every extreme that they name: Each row of 8 lengths sums to 4096, and its largest entry is 1024. `norm_params`: columns 0 and 2 are positive gains, columns 1 and 3 shifts of both signs.
All inputs are finite; a program needn't handle non-finite values.
Results may differ from the reference program's by a relative error of at most 0.03.
The reference program's roundings to bfloat16 on the way count: a program that leaves them out, or rounds other values in their place, can miss the bound.
Values may be sent and summed in bfloat16 or wider, within the bound.
A program may use at most 248 MiB of HBM per device.

```python
import math
import jax
import jax.numpy as jnp
import numpy as np
from jax import lax

D = 768
HEADS = 12
HEAD_DIM = 64
FF = 3072
LAYERS = 2
MB = 2
WINDOW = 1024
DOCS = 8
STEP = 10
TOKENS_MB = 4096
SEQ_LEN = 4096
DOC_MOST = 1024
NSEQ_MB = 1
TOK_ALL = 8192


def draw_norm_params(key, part):
    key = jax.random.fold_in(key, 11)
    gain_key, shift_key = jax.random.split(key)
    gains = jnp.exp(jax.random.uniform(gain_key, (LAYERS, D, 2), jnp.float32, -0.6, 0.45))
    shifts = jnp.clip(0.3 * jax.random.normal(shift_key, (LAYERS, D, 2), jnp.float32), -1.2, 1.2)
    return jnp.stack([gains[..., 0], shifts[..., 0], gains[..., 1], shifts[..., 1]], axis=-1)


def level_of(own_key, dims, cuts, least, high):
    level, own = 1.0, jax.random.fold_in(own_key, 6)
    for position, shards_of in cuts:
        heights = jnp.exp(jax.random.uniform(jax.random.fold_in(own, position), (shards_of,), jnp.float32, least / len(cuts), high / len(cuts)))
        level = level * jnp.repeat(heights, dims[position] // shards_of).reshape([-1 if axis == position else 1 for axis in range(len(dims))])
    return level


def profile(amount, total, limit, skew):
    loads = [(1 << 20) // math.isqrt(standing ** skew) + 1 for standing in range(2, amount + 1)]
    surplus, given = total - limit - (amount - 1), [1] * (amount - 1)
    while surplus > 0:
        candidates = [i for i in range(amount - 1) if given[i] < limit]
        mass, left = sum([loads[i] for i in candidates]), surplus
        for i in candidates:
            more = min(limit - given[i], max(1, left * loads[i] // mass), surplus)
            given[i] = given[i] + more
            surplus = surplus - more
    return np.array([limit] + given)


def uneven(key, number_of, total, limit, lean):
    if number_of == 2:
        one = jax.random.randint(key, (), max(1, total - limit), min(limit, total - 1) + 1)
        return jnp.stack([one, total - one])
    tallies = jnp.asarray(profile(number_of, total, limit, lean), jnp.int32)
    pairs = (number_of - 1) // 2
    giver, taker = tallies[1:1 + 2 * pairs:2], tallies[2:2 + 2 * pairs:2]
    margin = jnp.minimum(giver - 1, limit - taker)
    shifted = jax.random.randint(jax.random.fold_in(key, 1), (pairs,), 0, 1 << 20) % (margin + 1)
    tallies = tallies.at[1:1 + 2 * pairs:2].set(giver - shifted).at[2:2 + 2 * pairs:2].set(taker + shifted)
    return tallies[jax.random.permutation(jax.random.fold_in(key, 2), number_of)]


def noise(stream_key, dims, deviation, bound, pieces=(), kind=jnp.bfloat16):
    loudness = level_of(stream_key, dims, pieces, -0.22, 0.18) if pieces else 1.0
    values = jax.random.normal(stream_key, dims, jnp.float32) * deviation * loudness
    return jnp.minimum(jnp.maximum(values, -bound), bound).astype(kind)


def setup_inputs(seed: int = 0) -> dict:
    streams_of = jax.random.split(jax.random.key(seed), 19)
    inputs = noise(streams_of[0], (MB, TOKENS_MB, D), 1.0, 6.0, ((1, 32),))
    cotangent = noise(streams_of[1], (MB, TOKENS_MB, D), 1.0, 6.0, ((1, 32),))
    lengths = jax.vmap(lambda own: uneven(own, DOCS, SEQ_LEN, DOC_MOST, 2))(jax.random.split(streams_of[2], MB * NSEQ_MB)).reshape((MB, NSEQ_MB, DOCS)).astype(jnp.int32)
    qkv_weight = noise(streams_of[3], (LAYERS, D, 3 * D), D ** -0.5, 0.21875, ((1, 32),), jnp.float32)
    qkv_first = noise(streams_of[4], (LAYERS, D, 3 * D), (0.3 * TOK_ALL ** 0.5), 160.0, ((1, 32),), jnp.float32)
    qkv_second = jnp.clip(jnp.exp(math.log(3276.8) - 2.0794415 * jax.random.uniform(streams_of[5], (LAYERS, D, 3 * D), jnp.float32) ** level_of(streams_of[5], (LAYERS, D, 3 * D), ((1, 32),), -0.2, 0.2)), 409.6, 3276.8)
    out_weight = noise(streams_of[6], (LAYERS, D, D), (D // 16) ** -0.5, 0.875, ((1, 32),), jnp.float32)
    out_first = noise(streams_of[7], (LAYERS, D, D), (0.3 * TOK_ALL ** 0.5), 160.0, ((1, 32),), jnp.float32)
    out_second = jnp.clip(jnp.exp(math.log(3276.8) - 2.0794415 * jax.random.uniform(streams_of[8], (LAYERS, D, D), jnp.float32) ** level_of(streams_of[8], (LAYERS, D, D), ((1, 32),), -0.2, 0.2)), 409.6, 3276.8)
    up_weight = noise(streams_of[9], (LAYERS, D, 2 * FF), D ** -0.5, 0.21875, ((1, 32),), jnp.float32)
    up_first = noise(streams_of[10], (LAYERS, D, 2 * FF), (0.3 * TOK_ALL ** 0.5), 160.0, ((1, 32),), jnp.float32)
    up_second = jnp.clip(jnp.exp(math.log(3276.8) - 2.0794415 * jax.random.uniform(streams_of[11], (LAYERS, D, 2 * FF), jnp.float32) ** level_of(streams_of[11], (LAYERS, D, 2 * FF), ((1, 32),), -0.2, 0.2)), 409.6, 3276.8)
    down_weight = noise(streams_of[12], (LAYERS, FF, D), FF ** -0.5, 0.109375, ((1, 32),), jnp.float32)
    down_first = noise(streams_of[13], (LAYERS, FF, D), (0.3 * TOK_ALL ** 0.5), 160.0, ((1, 32),), jnp.float32)
    down_second = jnp.clip(jnp.exp(math.log(3276.8) - 2.0794415 * jax.random.uniform(streams_of[14], (LAYERS, FF, D), jnp.float32) ** level_of(streams_of[14], (LAYERS, FF, D), ((1, 32),), -0.2, 0.2)), 409.6, 3276.8)
    norm_params = draw_norm_params(jax.random.fold_in(streams_of[18], 71), 0)
    norm_first = noise(streams_of[16], (LAYERS, D, 4), (TOK_ALL ** 0.5), 512.0, ((1, 32),), jnp.float32)
    norm_second = jnp.clip(jnp.exp(math.log(32768.0) - 1.3862944 * jax.random.uniform(streams_of[17], (LAYERS, D, 4), jnp.float32) ** level_of(streams_of[17], (LAYERS, D, 4), ((1, 32),), -0.2, 0.2)), 8192.0, 32768.0)
    return {"inputs": inputs, "cotangent": cotangent, "lengths": lengths, "qkv_weight": qkv_weight, "qkv_first": qkv_first, "qkv_second": qkv_second, "out_weight": out_weight, "out_first": out_first, "out_second": out_second, "up_weight": up_weight, "up_first": up_first, "up_second": up_second, "down_weight": down_weight, "down_first": down_first, "down_second": down_second, "norm_params": norm_params, "norm_first": norm_first, "norm_second": norm_second}


highest = lax.Precision.HIGHEST
beta_one = 0.5
beta_two = 0.5
adam_eps = 1e-08
decay = 0.1
learn_rates = (0.03, 0.15, 0.03, 0.02, 0.2)

@jax.custom_vjp
def low(v):
    return lax.optimization_barrier(v.astype(jnp.bfloat16)).astype(jnp.float32)

@jax.custom_vjp
def low_back(v):
    return v

def low_keep(v):
    return (low(v), None)

def low_pass(kept, grad):
    return (grad,)

def back_keep(v):
    return (v, None)

def back_low(kept, grad):
    return (low(grad),)
low.defvjp(low_keep, low_pass)
low_back.defvjp(back_keep, back_low)

def layer_norm(summed, gain, shift):
    centre = lax.optimization_barrier(jnp.mean(summed, axis=-1, keepdims=True))
    centred = summed - centre
    variance = lax.optimization_barrier(jnp.mean(centred * centred, axis=-1, keepdims=True))
    return centred * lax.rsqrt(variance + 1e-12) * gain + shift

def geglu(gate, upper):
    return jax.nn.gelu(gate, approximate=False) * upper

def doc_index(positions, ends):
    return lax.optimization_barrier(jnp.sum((positions[:, None] >= ends[None, :]).astype(jnp.int32), axis=1)).astype(jnp.int32)

def one_block(query, keys_pad, values_pad, doc_ids, docs_pad, slopes, start):
    q_block = math.gcd(query.shape[0], 512)
    span = q_block + 2 * WINDOW
    q_part = lax.dynamic_slice_in_dim(query, start, q_block, 0)
    k_part = lax.dynamic_slice_in_dim(keys_pad, start, span, 0)
    v_part = lax.dynamic_slice_in_dim(values_pad, start, span, 0)
    q_doc = lax.dynamic_slice_in_dim(doc_ids, start, q_block, 0)
    k_doc = lax.dynamic_slice_in_dim(docs_pad, start, span, 0)
    q_pos = start + jnp.arange(q_block, dtype=jnp.int32)
    k_pos = start - WINDOW + jnp.arange(span, dtype=jnp.int32)
    raw = low_back(jnp.einsum('qhd,khd->hqk', q_part, k_part, precision=highest))
    distance = jnp.abs(q_pos[:, None] - k_pos[None, :])
    allowed = (q_doc[:, None] == k_doc[None, :]) & (distance < WINDOW)
    score = raw * HEAD_DIM ** (-0.5) - slopes[:, None, None] * distance.astype(jnp.float32)[None]
    score = jnp.where(allowed[None], score, -1e+30)
    attn_probs = jax.nn.softmax(score, axis=-1)
    return jnp.einsum('hqk,khd->qhd', low(attn_probs), v_part, precision=highest)

def attention(query, keys, values, doc_ids, slopes):
    total = query.shape[0]
    q_block = math.gcd(total, 512)
    padding = ((WINDOW, WINDOW), (0, 0), (0, 0))
    keys_pad = jnp.pad(keys, padding)
    values_pad = jnp.pad(values, padding)
    docs_pad = jnp.pad(doc_ids, (WINDOW, WINDOW), constant_values=-1)
    checked = jax.checkpoint(one_block)
    starts = jnp.arange(total // q_block, dtype=jnp.int32) * q_block
    blocks = lax.map(lambda start: checked(query, keys_pad, values_pad, doc_ids, docs_pad, slopes, start), starts)
    return blocks.reshape(total, HEADS, HEAD_DIM)

def layer(hidden, qkv_w, out_w, up_w, down_w, norm_w, doc_ids, slopes):
    total = hidden.shape[0]
    hidden_low = low(hidden)
    packed = low(low_back(jnp.dot(hidden_low, qkv_w, precision=highest)))
    packed = packed.reshape(total, 3, HEADS, HEAD_DIM)
    attended = attention(packed[:, 0], packed[:, 1], packed[:, 2], doc_ids, slopes)
    attn_low = low(low_back(attended)).reshape(total, D)
    mixed = hidden + low_back(jnp.dot(attn_low, out_w, precision=highest))
    normed = layer_norm(mixed, norm_w[:, 0], norm_w[:, 1])
    upper = low_back(jnp.dot(low(normed), up_w, precision=highest))
    act_low = low(geglu(upper[:, :FF], upper[:, FF:]))
    second = normed + low_back(jnp.dot(act_low, down_w, precision=highest))
    return layer_norm(second, norm_w[:, 2], norm_w[:, 3])

def network(params, hidden, doc_ids, slopes):
    for layer_index in range(LAYERS):
        hidden = layer(hidden, low(params[0][layer_index]), low(params[1][layer_index]), low(params[2][layer_index]), low(params[3][layer_index]), low(params[4][layer_index]), doc_ids, slopes)
    return hidden

def adamw(weight, first, second, grad, rate):
    first_new = beta_one * first + (1.0 - beta_one) * grad
    second_new = beta_two * second + (1.0 - beta_two) * grad * grad
    first_hat = first_new / (1.0 - beta_one ** STEP)
    second_hat = second_new / (1.0 - beta_two ** STEP)
    weight_new = weight - rate * (first_hat / (jnp.sqrt(second_hat) + adam_eps) + decay * weight)
    return (first_new, second_new, weight_new)

def reference(inputs, cotangent, lengths, qkv_weight, qkv_first, qkv_second, out_weight, out_first, out_second, up_weight, up_first, up_second, down_weight, down_first, down_second, norm_params, norm_first, norm_second):
    params = (qkv_weight, out_weight, up_weight, down_weight, norm_params)
    states = ((qkv_first, qkv_second), (out_first, out_second), (up_first, up_second), (down_first, down_second), (norm_first, norm_second))
    slopes = jnp.exp2(-8.0 * (jnp.arange(HEADS, dtype=jnp.int32) + 1).astype(jnp.float32) / HEADS)
    positions = jnp.arange(TOKENS_MB, dtype=jnp.int32)
    seq_starts = jnp.arange(NSEQ_MB, dtype=jnp.int32)[:, None] * SEQ_LEN
    totals = tuple((jnp.zeros(member.shape, jnp.float32) for member in params))
    outputs_list = []
    input_grads = []
    for batch_index in range(MB):
        ends = (jnp.cumsum(lengths[batch_index], axis=1).astype(jnp.int32) + seq_starts).reshape(-1)
        doc_ids = doc_index(positions, ends)

        def forward(weights, hidden):
            return network(weights, hidden, doc_ids, slopes)
        result, pullback = jax.vjp(forward, params, inputs[batch_index].astype(jnp.float32))
        weight_grads, input_grad = pullback(cotangent[batch_index].astype(jnp.float32))
        totals = tuple((total + piece for total, piece in zip(totals, weight_grads)))
        outputs_list.append(result)
        input_grads.append(input_grad)
    results = [jnp.stack(outputs_list), jnp.stack(input_grads)]
    new_weights = []
    for kind_index in range(5):
        first_new, second_new, weight_new = adamw(params[kind_index], states[kind_index][0], states[kind_index][1], totals[kind_index], learn_rates[kind_index])
        results += [totals[kind_index], first_new, second_new, weight_new]
        new_weights.append(weight_new)
    results += [member.astype(jnp.bfloat16) for member in new_weights[:4]]
    return tuple(results)
```

```python
import functools
import math

import jax
import jax.numpy as jnp
from jax import lax
from jax.experimental import pallas as pl
from jax.experimental.pallas import tpu as pltpu
from jax.sharding import PartitionSpec as P

D = 768
HEADS = 12
HEAD_DIM = 64
FF = 3072
LAYERS = 2
WINDOW = 1024
STEP = 10

beta_one = 0.5
beta_two = 0.5
adam_eps = 1e-08
decay = 0.1
learn_rates = (0.03, 0.15, 0.03, 0.02, 0.2)

MESH = pl.DeviceIdType.MESH
TILE = 256
LOG2E = math.log2(math.e)
NORM_PAD = 128

CORES = 2
AXES = ("x", "z", "y", "c")


def cost_of(microseconds):
    return pl.CostEstimate(flops=0, bytes_accessed=int(microseconds * 3.69e6), transcendentals=0)


def grid_sizes(seq_size):
    rows = 2 if seq_size <= 16 else 4
    return {"x": lax.axis_size("head"), "z": seq_size // (rows * CORES), "y": rows, "c": CORES}


def quotient(value, divisor, count):
    result = 0
    for step in range(1, count):
        result = result + jnp.where(value >= step * divisor, 1, 0)
    return result


def wrapped(value, size):
    return value - jnp.where(value >= size, size, 0)


def own_place(sizes):
    seq = lax.axis_index("seq")
    return {
        "x": lax.axis_index("head"),
        "z": lax.div(seq, sizes["y"] * sizes["c"]),
        "y": lax.rem(lax.div(seq, sizes["c"]), sizes["y"]),
        "c": lax.rem(seq, sizes["c"]),
    }


def device_of(place, sizes):
    seq = (place["z"] * sizes["y"] + place["y"]) * sizes["c"] + place["c"]
    return {"head": place["x"], "seq": seq}


def peer_at(place, axis, step, sizes):
    other = dict(place)
    other[axis] = lax.rem(place[axis] + step, sizes[axis])
    return other


def greet_axes(place, sizes):
    barrier = pltpu.get_barrier_semaphore()
    count = 0
    for axis in AXES:
        for step in range(1, sizes[axis]):
            pl.semaphore_signal(
                barrier,
                inc=1,
                device_id=device_of(peer_at(place, axis, step, sizes), sizes),
                device_id_type=MESH,
            )
            count += 1
    pl.semaphore_wait(barrier, count)


def region(place, full, window):
    return tuple(slice(None) if axis in full else place[axis] for axis in AXES) + window


ZXY = ("z", "x", "y")
ZYX = ("z", "y", "x")

def steps_of(kind, rows):
    def halves(first, second, start=0):
        return ((0, rows, start, first, ZXY), (0, rows, start + first, second, ZYX))

    if kind == "qkv":
        return [halves(384, 384, start) for start in range(0, 3 * D, 768)]
    if kind == "out":
        return [halves(384, 512)]
    if kind == "up":
        return [halves(768, 768, start) for start in range(0, 2 * FF, 1536)]
    if rows % 32:
        return [halves(384, 384)]
    half = rows // 2
    return [
        ((0, half, start, 384, ZXY), (half, half, start, 384, ZYX)) for start in range(0, D, 384)
    ]


HBM = pl.BlockSpec(memory_space=pl.ANY)
VMEM = pl.BlockSpec(memory_space=pltpu.VMEM)
SMEM = pl.BlockSpec(memory_space=pltpu.SMEM)


class Flow:
    def __init__(self, kinds, operands, sizes, ahead, lag):
        self.operands = list(operands)
        self.sizes = sizes
        self.ahead, self.lag = ahead, lag
        self.steps, self.pieces = [], []
        for array, kind in enumerate(kinds):
            for step in steps_of(kind, operands[array].shape[-2]):
                self.steps.append(range(len(self.pieces), len(self.pieces) + len(step)))
                self.pieces += [(array,) + piece for piece in step]
        most = sum(size - 1 for size in sizes.values())
        self.semaphores = [
            pltpu.SemaphoreType.DMA((len(self.pieces), most)),
            pltpu.SemaphoreType.DMA((len(self.pieces), most)),
            pltpu.SemaphoreType.DMA((len(self.pieces),)),
        ]

        if not self.pieces:
            self.ahead, self.semaphores = 0, []

    def bind(self, ins, outs, scratch):
        self.place = own_place(self.sizes)
        if self.pieces:
            self.ins, self.outs, self.buffers = ins, outs, scratch[:-3]
            self.send_sem, self.recv_sem, self.own_sem = scratch[-3:]

    def window(self, number):
        _, row, rows, column, columns, _ = self.pieces[number]
        return (pl.ds(row, rows), pl.ds(column, columns))

    def remote(self, number, axis, step, source, target):
        before = AXES[: AXES.index(axis)]
        slot = sum(self.sizes[one] - 1 for one in before) + step - 1
        return pltpu.make_async_remote_copy(
            src_ref=source,
            dst_ref=target,
            send_sem=self.send_sem.at[number, slot],
            recv_sem=self.recv_sem.at[number, slot],
            device_id=device_of(peer_at(self.place, axis, step, self.sizes), self.sizes),
            device_id_type=MESH,
        )

    def numbers(self, step):
        return self.steps[step] if 0 <= step < len(self.steps) else ()

    def start(self, step, phase):
        for number in self.numbers(step):
            if phase == 0:
                self.own_copy(number).start()
            for copy in self.copies(number, phase):
                copy.start()

    def begin(self):
        for step in range(self.ahead):
            self.start(step, 0)

    def arrive(self, step, phase):
        for number in self.numbers(step):
            if phase == 0:
                self.own_copy(number).wait()
            for copy in self.copies(number, phase):
                copy.wait_recv()
            self.take(number, phase)

    def turns(self):
        def turn(index):
            self.start(index + self.ahead, 0)
            for phase in (3, 2, 1, 0):
                self.arrive(index - self.lag * phase, phase)
                if phase < 3:
                    self.start(index - self.lag * phase, phase + 1)

        count = len(self.steps) + 3 * self.lag if self.steps else 0
        return [functools.partial(turn, index) for index in range(count)]

    def end(self):
        for number in range(len(self.pieces)):
            for phase in range(4):
                for copy in self.copies(number, phase):
                    copy.wait_send()


class Gather(Flow):
    def __init__(self, kinds, shards, sizes, ahead, lag):
        super().__init__(kinds, shards, sizes, ahead, lag)
        lead = tuple(sizes[axis] for axis in AXES)
        self.out_shape = [jax.ShapeDtypeStruct(lead + one.shape, one.dtype) for one in shards]
        self.out_specs = [HBM] * len(shards)
        self.scratch = self.semaphores

    def own_copy(self, number):
        array, window = self.pieces[number][0], self.window(number)
        return pltpu.make_async_copy(
            self.ins[array].at[window],
            self.outs[array].at[region(self.place, (), window)],
            self.own_sem.at[number],
        )

    def copies(self, number, phase):
        array, order, window = self.pieces[number][0], self.pieces[number][-1], self.window(number)
        axis = (order + ("c",))[phase]
        part = self.outs[array].at[region(self.place, order[:phase], window)]
        source = self.ins[array].at[window] if phase == 0 else part
        return [
            self.remote(number, axis, step, source, part) for step in range(1, self.sizes[axis])
        ]

    def take(self, number, phase):
        pass


class Scatter(Flow):
    def __init__(self, kinds, grads, sizes, ahead, lag):
        grads = [
            grad.reshape(tuple(sizes[axis] for axis in AXES) + (-1, grad.shape[-1]))
            for grad in grads
        ]
        super().__init__(kinds, grads, sizes, ahead, lag)
        self.out_shape = [jax.ShapeDtypeStruct(grad.shape[-2:], jnp.float32) for grad in grads]
        self.out_specs = [VMEM] * len(grads)
        self.scratch = []
        for _, _, rows, _, columns, order in self.pieces:

            def shape_of(full, rows=rows, columns=columns):
                return tuple(sizes[axis] for axis in AXES if axis in full) + (rows, columns)

            self.scratch += [pltpu.VMEM(shape_of(order), jnp.bfloat16)] * 2
            for phase in range(3):
                senders = sizes[order[2 - phase]] - 1
                self.scratch.append(
                    pltpu.VMEM((senders,) + shape_of(order[: 2 - phase]), jnp.bfloat16)
                )
        self.scratch += self.semaphores

    def own_copy(self, number):
        array = self.pieces[number][0]
        return pltpu.make_async_copy(
            self.ins[array].at[region(self.place, AXES[:3], self.window(number))],
            self.buffers[5 * number],
            self.own_sem.at[number],
        )

    def copies(self, number, phase):
        array, order = self.pieces[number][0], self.pieces[number][-1]
        axis = "c" if phase == 0 else order[3 - phase]
        found = []
        for step in range(1, self.sizes[axis]):
            peer = peer_at(self.place, axis, step, self.sizes)
            if phase == 0:
                source = self.ins[array].at[region(peer, AXES[:3], self.window(number))]
                target = self.buffers[5 * number + 1]
            else:
                full = order[: 3 - phase]
                where = tuple(slice(None) if one in full else peer[one] for one in AXES[:3])
                source = self.buffers[5 * number].at[where]
                target = self.buffers[5 * number + 1 + phase].at[step - 1]
            found.append(self.remote(number, axis, step, source, target))
        return found

    def take(self, number, phase):
        array, order = self.pieces[number][0], self.pieces[number][-1]
        total = self.buffers[5 * number]
        got = self.buffers[5 * number + 1 + phase]
        if phase == 0:
            total[...] = total[...] + got[...]
            return
        full = order[: 3 - phase]
        where = tuple(slice(None) if axis in full else self.place[axis] for axis in AXES[:3])
        value = total[where]
        senders = self.sizes[order[3 - phase]] - 1
        if phase == 3:
            value = value.astype(jnp.float32)
            for sender in range(senders):
                value = value + got[sender].astype(jnp.float32)
            self.outs[array][self.window(number)] = value
        else:
            for sender in range(senders):
                value = value + got[sender]
            total[where] = value


def run_flow(flow, collective_id, name):
    count = len(flow.operands)

    def kernel(*refs):
        flow.bind(refs[:count], refs[count : 2 * count], refs[2 * count :])
        greet_axes(flow.place, flow.sizes)
        flow.begin()
        for turn in flow.turns():
            turn()
        flow.end()

    return pl.pallas_call(
        kernel,
        out_shape=flow.out_shape,
        in_specs=[HBM] * count,
        out_specs=flow.out_specs,
        scratch_shapes=flow.scratch,
        compiler_params=pltpu.CompilerParams(
            collective_id=collective_id, has_side_effects=True, vmem_limit_bytes=40 << 20
        ),
        cost_estimate=cost_of(30),
        name=name,
    )(*flow.operands)


def unit_place(unit, sizes):
    chips = sizes["x"] * sizes["y"]
    inside = quotient(unit, sizes["z"], chips * sizes["c"])
    row = quotient(inside, sizes["x"], sizes["y"] * sizes["c"])
    core = quotient(inside, chips, sizes["c"])
    x = inside - row * sizes["x"]
    y = wrapped(row - core * sizes["y"] + x, sizes["y"])
    return {"x": x, "z": unit - inside * sizes["z"], "y": y, "c": core}


def own_unit(sizes):
    place = own_place(sizes)
    turned = lax.rem(place["y"] + sizes["y"] * sizes["x"] - place["x"], sizes["y"])
    inside = (place["c"] * sizes["y"] + turned) * sizes["x"] + place["x"]
    return inside * sizes["z"] + place["z"]


class Exchange:
    def __init__(self, sizes, batches, sequences):
        self.sizes = sizes
        self.batches = batches
        self.sequences = sequences
        self.heads = sizes["x"]
        self.devices = math.prod(sizes.values())
        self.units = batches * sequences * HEADS
        self.blocks = self.devices // sequences
        self.held = batches * HEADS
        assert self.units <= self.devices

    def my_block(self):
        return lax.axis_index("seq") * self.heads + lax.axis_index("head")

    def unit_for(self, slot, block):
        batch = quotient(slot, HEADS, self.batches)
        sequence = quotient(block, self.blocks, self.sequences)
        return (batch * self.sequences + sequence) * HEADS + slot - batch * HEADS

    def block_device(self, block):
        return {"head": lax.rem(block, self.heads), "seq": lax.div(block, self.heads)}

    def token_device(self, unit, slot):
        if self.sequences > 1:
            slot = slot + lax.rem(lax.div(unit, HEADS), self.sequences) * self.blocks
        return self.block_device(slot)

    def unit_device(self, slot, block):
        return device_of(unit_place(self.unit_for(slot, block), self.sizes), self.sizes)

    def slot_of(self, unit):
        batch = lax.div(unit, HEADS * self.sequences)
        return lax.min(batch * HEADS + lax.rem(unit, HEADS), self.held - 1)

    def is_me(self, device):
        return jnp.logical_and(
            device["head"] == lax.axis_index("head"), device["seq"] == lax.axis_index("seq")
        )

    def greet_all(self):
        barrier = pltpu.get_barrier_semaphore()

        def greet(step, carry):
            device = self.block_device(lax.rem(self.my_block() + step, self.devices))
            pl.semaphore_signal(barrier, inc=1, device_id=device, device_id_type=MESH)
            return carry

        lax.fori_loop(1, self.devices, greet, 0)
        pl.semaphore_wait(barrier, self.devices - 1)

    def send(self, source, target, send_sem, recv_sem, own_sem, device, wait):
        same = self.is_me(device)
        remote = pltpu.make_async_remote_copy(
            src_ref=source,
            dst_ref=target,
            send_sem=send_sem,
            recv_sem=recv_sem,
            device_id=device,
            device_id_type=MESH,
        )
        if not wait:
            pl.when(same)(pltpu.make_async_copy(source, target, own_sem).start)

        @pl.when(jnp.logical_not(same))
        def _():
            remote.wait_send() if wait else remote.start()

    def receive(self, target, recv_sem, own_sem, device):
        same = self.is_me(device)

        @pl.when(same)
        def _():
            pltpu.make_async_copy(target, target, own_sem).wait()

        @pl.when(jnp.logical_not(same))
        def _():
            pltpu.make_async_copy(target, target, recv_sem).wait()

    def to_units(self, source_at, target_at, send_sem, recv_sem, own_sem, wait, part=0, parts=1):
        block = self.my_block()
        spot = block - quotient(block, self.blocks, self.sequences) * self.blocks
        turned = lax.rem(block, self.held)

        def one(index, carry):
            slot = wrapped(index + turned, self.held)
            self.send(
                source_at(slot),
                target_at(spot),
                send_sem.at[index],
                recv_sem.at[spot],
                own_sem,
                self.unit_device(slot, block),
                wait,
            )
            return carry

        lax.fori_loop(part * self.held // parts, (part + 1) * self.held // parts, one, 0)

    def at_unit(self, target_at, recv_sem, own_sem):
        unit = own_unit(self.sizes)

        def one(spot, carry):
            self.receive(
                target_at(spot), recv_sem.at[spot], own_sem, self.token_device(unit, spot)
            )
            return carry

        lax.fori_loop(0, self.blocks, one, 0)

    def to_token(self, spot, source_at, target_at, send_sem, recv_sem, own_sem, wait):
        unit = own_unit(self.sizes)
        slot = self.slot_of(unit)
        self.send(
            source_at(spot),
            target_at(slot),
            send_sem.at[spot],
            recv_sem.at[slot],
            own_sem,
            self.token_device(unit, spot),
            wait,
        )

    def at_tokens(self, target_at, recv_sem, own_sem):
        block = self.my_block()

        def one(slot, carry):
            self.receive(
                target_at(slot), recv_sem.at[slot], own_sem, self.unit_device(slot, block)
            )
            return carry

        lax.fori_loop(0, self.held, one, 0)


PART = 128
PER = TILE // PART
GUARD = WINDOW // TILE
REACH = 2 * GUARD + 1
DOC_ROWS = 64
FAR = -1e30
FORWARD_AHEAD, FORWARD_FIRST, FORWARD_LAG = 3, 5, 2
BACKWARD_AHEAD, BACKWARD_FIRST, BACKWARD_LAG = 4, 4, 2


def unit_context(lengths, exchange, tokens):
    unit = own_unit(exchange.sizes)
    row = lax.min(lax.div(unit, HEADS), exchange.batches * exchange.sequences - 1)
    head = lax.rem(unit, HEADS)
    own = lax.dynamic_index_in_dim(lengths.reshape(-1, lengths.shape[-1]), row, 0, keepdims=False)
    ends = jnp.cumsum(own)
    place = jnp.arange(tokens, dtype=jnp.int32)
    document = jnp.sum((place[None, :] >= ends[:, None]).astype(jnp.int32), axis=0)
    inside = jnp.arange(DOC_ROWS, dtype=jnp.int32)[:, None] == document[None, :]
    real = jnp.arange(DOC_ROWS, dtype=jnp.int32)[:, None] < lengths.shape[-1]
    of_query = jnp.where(inside, FAR, 0.0)
    of_key = jnp.where(real & ~inside, 1.0, 0.0)
    blocks = tokens // PART
    shape = (DOC_ROWS, blocks, PART)
    slope = jnp.exp2(-8.0 * (head + 1).astype(jnp.float32) / HEADS)
    return (
        (slope * LOG2E).reshape(1),
        of_query.reshape(shape).transpose(1, 0, 2).astype(jnp.bfloat16),
        of_key.reshape(shape).transpose(1, 0, 2).astype(jnp.bfloat16),
    )


def side_by_side(ref, tile, rows):
    return jnp.concatenate([ref[tile * PER + part, rows, :] for part in range(PER)], axis=1)


ROW_Q, ROW_K, ROW_V = slice(0, 64), slice(64, 128), slice(128, 192)


def rows_at(tile):
    return pl.ds(pl.multiple_of(tile * TILE, TILE), TILE)


def part_at(block):
    return pl.ds(pl.multiple_of(block * PART, PART), PART)


def fill_biases(slope_ref, bias_ref):
    key = lax.broadcasted_iota(jnp.int32, (TILE, TILE), 0)
    query = lax.broadcasted_iota(jnp.int32, (TILE, TILE), 1)

    def one(step, carry):
        distance = jnp.abs(key - query + (step - GUARD) * TILE)
        bias = distance.astype(jnp.float32) * -slope_ref[0]
        bias_ref[step] = jnp.where(distance < WINDOW, bias, FAR)
        return carry

    lax.fori_loop(0, REACH, one, 0)


def fill_guards(unit_ref, key_ref, blocks):
    rows = GUARD * TILE
    feature = lax.broadcasted_iota(jnp.int32, (rows, PART), 1)
    away = jnp.where((feature >= 64) & (feature < 72), 1.0, 0.0).astype(jnp.bfloat16)
    for first in (0, rows + blocks * PART):
        key_ref[pl.ds(first, rows), :] = away
    for first in (0, GUARD * PER + blocks):
        unit_ref[pl.ds(first, GUARD * PER)] = jnp.zeros(
            (GUARD * PER,) + unit_ref.shape[1:], unit_ref.dtype
        )


def fill_keys(unit_ref, doc_ref, key_ref, blocks):
    def one(block, carry):
        there = block + GUARD * PER
        features = jnp.concatenate([unit_ref[there, ROW_K, :], doc_ref[block]], axis=0)
        key_ref[part_at(there), :] = features.T
        return carry

    lax.fori_loop(0, blocks, one, 0, unroll=4)


class Service:
    def __init__(self, flow, first, tiles):
        self.turns = flow.turns()
        self.first = first
        self.after = {}
        left = max(len(self.turns) - first, 0)
        for index in range(left):
            self.after.setdefault(index * tiles // left, []).append(self.turns[first + index])

    def begin(self, done=0):
        for turn in self.turns[done : self.first]:
            turn()

    def at(self, tile):
        for index, turns in self.after.items():

            @pl.when(tile == index)
            def _(turns=turns):
                for turn in turns:
                    turn()


def attention_forward(packed, exchange, context, collective_id, flow, first):
    blocks, held = exchange.blocks, exchange.held
    tiles = blocks // PER
    edge = GUARD * PER

    count = len(flow.operands)

    def kernel(slope_ref, query_doc_ref, key_doc_ref, packed_ref, *refs):
        out_ref, keep_ref, wide_ref, sum_ref = refs[count : count + 4]
        flow.bind(refs[:count], refs[count + 4 : 2 * count + 4], refs[2 * count + 14 :])
        (
            unit_ref,
            key_ref,
            bias_ref,
            score_ref,
            result_ref,
            to_sem,
            at_sem,
            back_sem,
            home_sem,
            own_sem,
        ) = refs[2 * count + 4 : 2 * count + 14]
        service = Service(flow, first, tiles)
        has_unit = own_unit(exchange.sizes) < exchange.units
        exchange.greet_all()

        def units(wait, part=0, parts=1):
            exchange.to_units(
                lambda slot: packed_ref.at[slot],
                lambda spot: unit_ref.at[edge + spot],
                to_sem,
                at_sem,
                own_sem.at[0],
                wait,
                part,
                parts,
            )

        def tokens(spot, wait):
            exchange.to_token(
                spot,
                lambda spot: result_ref.at[spot],
                lambda slot: out_ref.at[slot],
                back_sem,
                home_sem,
                own_sem.at[1],
                wait,
            )

        keep = pltpu.make_async_copy(unit_ref.at[pl.ds(edge, blocks)], keep_ref, own_sem.at[2])
        flow.begin()
        parts = 3 if first > 2 else 1
        units(False, 0, parts)

        @pl.when(has_unit)
        def _():
            fill_biases(slope_ref, bias_ref)
            fill_guards(unit_ref, key_ref, blocks)

        for part in range(1, parts):
            service.turns[part - 1]()
            units(False, part, parts)
        service.begin(parts - 1)

        @pl.when(has_unit)
        def _():
            exchange.at_unit(lambda spot: unit_ref.at[edge + spot], at_sem, own_sem.at[0])
            keep.start()
            fill_keys(unit_ref, key_doc_ref, key_ref, blocks)

        def one_tile(tile, carry):
            @pl.when(has_unit)
            def _():
                q_t = jnp.concatenate(
                    [
                        side_by_side(unit_ref, tile + GUARD, ROW_Q),
                        side_by_side(query_doc_ref, tile, slice(0, DOC_ROWS)),
                    ],
                    axis=0,
                )
                top = jnp.full((1, TILE), FAR, jnp.float32)
                for step in range(REACH):
                    raw = jnp.dot(
                        key_ref[rows_at(tile + step), :], q_t, preferred_element_type=jnp.float32
                    )
                    score = raw * (HEAD_DIM ** (-0.5) * LOG2E) + bias_ref[step]
                    score_ref[step] = score
                    top = jnp.maximum(top, jnp.max(score, axis=0, keepdims=True))
                total = jnp.zeros((1, TILE), jnp.float32)
                attended = jnp.zeros((HEAD_DIM, TILE), jnp.float32)
                for step in range(REACH):
                    probs = jnp.exp2(score_ref[step] - top)
                    total = total + jnp.sum(probs, axis=0, keepdims=True)
                    attended = attended + jnp.dot(
                        side_by_side(unit_ref, tile + step, ROW_V),
                        probs.astype(jnp.bfloat16),
                        preferred_element_type=jnp.float32,
                    )
                result = attended / total
                sum_ref[tile] = top + jnp.log2(total)
                for part in range(PER):
                    piece = result[:, part * PART : (part + 1) * PART]
                    wide_ref[tile * PER + part] = piece
                    result_ref[tile * PER + part] = piece.astype(jnp.bfloat16)
                    tokens(tile * PER + part, False)

            service.at(tile)
            return carry

        lax.fori_loop(0, tiles, one_tile, 0)
        units(True)

        exchange.at_tokens(lambda slot: out_ref.at[slot], home_sem, own_sem.at[1])

        @pl.when(has_unit)
        def _():
            def sent(spot, carry):
                tokens(spot, True)
                return carry

            lax.fori_loop(0, blocks, sent, 0)
            keep.wait()

        flow.end()

    return pl.pallas_call(
        kernel,
        out_shape=[
            jax.ShapeDtypeStruct((held, HEAD_DIM, PART), jnp.bfloat16),
            jax.ShapeDtypeStruct((blocks, 3 * HEAD_DIM, PART), jnp.bfloat16),
            jax.ShapeDtypeStruct((blocks, HEAD_DIM, PART), jnp.float32),
            jax.ShapeDtypeStruct((tiles, 1, TILE), jnp.float32),
        ]
        + flow.out_shape,
        in_specs=[SMEM, VMEM, VMEM, HBM] + [HBM] * count,
        out_specs=[HBM, HBM, VMEM, VMEM] + flow.out_specs,
        scratch_shapes=[
            pltpu.VMEM((blocks + 2 * edge, 3 * HEAD_DIM, PART), jnp.bfloat16),
            pltpu.VMEM(((blocks + 2 * edge) * PART, PART), jnp.bfloat16),
            pltpu.VMEM((REACH, TILE, TILE), jnp.float32),
            pltpu.VMEM((REACH, TILE, TILE), jnp.float32),
            pltpu.VMEM((blocks, HEAD_DIM, PART), jnp.bfloat16),
            pltpu.SemaphoreType.DMA((held,)),
            pltpu.SemaphoreType.DMA((blocks,)),
            pltpu.SemaphoreType.DMA((blocks,)),
            pltpu.SemaphoreType.DMA((held,)),
            pltpu.SemaphoreType.DMA((3,)),
        ]
        + flow.scratch,
        compiler_params=pltpu.CompilerParams(
            collective_id=collective_id, has_side_effects=True, vmem_limit_bytes=48 << 20
        ),
        cost_estimate=cost_of(60),
        name="attention_forward",
    )(*context, packed, *flow.operands)


def attention_backward(grad, unit_kept, exchange, context, collective_id, flow, first):
    blocks, held = exchange.blocks, exchange.held
    tiles = blocks // PER
    edge = GUARD * PER

    count = len(flow.operands)

    def kernel(
        slope_ref, query_doc_ref, key_doc_ref, wide_ref, sum_ref, grad_ref, kept_ref, *refs
    ):
        out_ref = refs[count]
        flow.bind(refs[:count], refs[count + 1 : 2 * count + 1], refs[2 * count + 13 :])
        (
            unit_ref,
            got_ref,
            key_ref,
            value_ref,
            bias_ref,
            total_ref,
            result_ref,
            to_sem,
            at_sem,
            back_sem,
            home_sem,
            own_sem,
        ) = refs[2 * count + 1 : 2 * count + 13]
        service = Service(flow, first, tiles)
        has_unit = own_unit(exchange.sizes) < exchange.units
        exchange.greet_all()

        def units(wait):
            exchange.to_units(
                lambda slot: grad_ref.at[slot],
                lambda spot: got_ref.at[spot],
                to_sem,
                at_sem,
                own_sem.at[0],
                wait,
            )

        def tokens(spot, wait):
            exchange.to_token(
                spot,
                lambda spot: result_ref.at[spot],
                lambda slot: out_ref.at[slot],
                back_sem,
                home_sem,
                own_sem.at[1],
                wait,
            )

        load = pltpu.make_async_copy(kept_ref, unit_ref.at[pl.ds(edge, blocks)], own_sem.at[2])
        flow.begin()
        units(False)

        @pl.when(has_unit)
        def _():
            load.start()
            fill_biases(slope_ref, bias_ref)
            fill_guards(unit_ref, key_ref, blocks)
            for first in (0, (edge + blocks) * PART):
                value_ref[pl.ds(first, edge * PART), :] = jnp.zeros(
                    (edge * PART, PART), value_ref.dtype
                )
            total_ref[...] = jnp.zeros_like(total_ref)
            load.wait()
            fill_keys(unit_ref, key_doc_ref, key_ref, blocks)

            def one(block, carry):
                there = block + edge
                value_ref[part_at(there), :] = unit_ref[there, 64:192, :].T
                return carry

            lax.fori_loop(0, blocks, one, 0, unroll=4)

        service.begin()

        @pl.when(has_unit)
        def _():
            exchange.at_unit(lambda spot: got_ref.at[spot], at_sem, own_sem.at[0])

        def finish(tile):
            for part in range(PER):
                block = tile * PER + part
                result_ref[block, 64:192, :] = total_ref[part_at(block + edge), :].T.astype(
                    jnp.bfloat16
                )
                tokens(block, False)

        def one_tile(tile, carry):
            @pl.when(has_unit)
            def _():
                q_part = side_by_side(unit_ref, tile + GUARD, ROW_Q)
                g_part = side_by_side(got_ref, tile, slice(0, 64))
                q_t = jnp.concatenate(
                    [q_part, side_by_side(query_doc_ref, tile, slice(0, DOC_ROWS))], axis=0
                )
                g_small = g_part * jnp.asarray(HEAD_DIM ** (-0.5), jnp.bfloat16)
                g_t = jnp.concatenate([jnp.zeros_like(g_small), g_small], axis=0)
                turned = jnp.concatenate([q_part, g_part], axis=0).T
                lane = lax.broadcasted_iota(jnp.int32, turned.shape, 1)
                none = jnp.zeros_like(turned)
                q_and_g = jnp.concatenate(
                    [jnp.where(lane < 64, turned, none), jnp.where(lane < 64, none, turned)],
                    axis=0,
                )
                wide_t = side_by_side(wide_ref, tile, slice(0, 64))
                mean = jnp.sum(g_small.astype(jnp.float32) * wide_t, axis=0, keepdims=True)
                sum_now = sum_ref[tile]
                grad_q = jnp.zeros((HEAD_DIM, TILE), jnp.float32)
                for step in range(REACH):
                    there = rows_at(tile + step)
                    raw = jnp.dot(key_ref[there, :], q_t, preferred_element_type=jnp.float32)
                    grad_probs = jnp.dot(
                        value_ref[there, :], g_t, preferred_element_type=jnp.float32
                    )
                    score = raw * (HEAD_DIM ** (-0.5) * LOG2E) + bias_ref[step]
                    probs = jnp.exp2(score - sum_now)
                    grad_raw = (probs * (grad_probs - mean)).astype(jnp.bfloat16)
                    total_ref[there, :] += jnp.dot(
                        jnp.concatenate([grad_raw, probs.astype(jnp.bfloat16)], axis=1),
                        q_and_g,
                        preferred_element_type=jnp.float32,
                    )
                    grad_q = grad_q + jnp.dot(
                        side_by_side(unit_ref, tile + step, ROW_K),
                        grad_raw,
                        preferred_element_type=jnp.float32,
                    )
                for part in range(PER):
                    result_ref[tile * PER + part, ROW_Q, :] = grad_q[
                        :, part * PART : (part + 1) * PART
                    ].astype(jnp.bfloat16)

                @pl.when(tile >= GUARD)
                def _():
                    finish(tile - GUARD)

            service.at(tile)
            return carry

        lax.fori_loop(0, tiles, one_tile, 0)
        units(True)

        @pl.when(has_unit)
        def _():
            def rest(tile, carry):
                finish(tile)
                return carry

            lax.fori_loop(max(tiles - GUARD, 0), tiles, rest, 0)

        exchange.at_tokens(lambda slot: out_ref.at[slot], home_sem, own_sem.at[1])

        @pl.when(has_unit)
        def _():
            def sent(spot, carry):
                tokens(spot, True)
                return carry

            lax.fori_loop(0, blocks, sent, 0)

        flow.end()

    return pl.pallas_call(
        kernel,
        out_shape=[jax.ShapeDtypeStruct((held, 3 * HEAD_DIM, PART), jnp.bfloat16)] + flow.out_shape,
        in_specs=[SMEM, VMEM, VMEM, VMEM, VMEM, HBM, HBM] + [HBM] * count,
        out_specs=[HBM] + flow.out_specs,
        scratch_shapes=[
            pltpu.VMEM((blocks + 2 * edge, 3 * HEAD_DIM, PART), jnp.bfloat16),
            pltpu.VMEM((blocks, HEAD_DIM, PART), jnp.bfloat16),
            pltpu.VMEM(((blocks + 2 * edge) * PART, PART), jnp.bfloat16),
            pltpu.VMEM(((blocks + 2 * edge) * PART, PART), jnp.bfloat16),
            pltpu.VMEM((REACH, TILE, TILE), jnp.float32),
            pltpu.VMEM(((blocks + 2 * edge) * PART, PART), jnp.float32),
            pltpu.VMEM((blocks, 3 * HEAD_DIM, PART), jnp.bfloat16),
            pltpu.SemaphoreType.DMA((held,)),
            pltpu.SemaphoreType.DMA((blocks,)),
            pltpu.SemaphoreType.DMA((blocks,)),
            pltpu.SemaphoreType.DMA((held,)),
            pltpu.SemaphoreType.DMA((3,)),
        ]
        + flow.scratch,
        compiler_params=pltpu.CompilerParams(
            collective_id=collective_id, has_side_effects=True, vmem_limit_bytes=60 << 20
        ),
        cost_estimate=cost_of(70),
        name="attention_backward",
    )(*context, *unit_kept[1:], grad, unit_kept[0], *flow.operands)


def layer_norm(summed, gain, shift):
    centre = jnp.mean(summed, axis=-1, keepdims=True)
    centred = summed - centre
    variance = jnp.mean(centred * centred, axis=-1, keepdims=True)
    return centred * lax.rsqrt(variance + 1e-12) * gain + shift


def geglu(gate, upper):
    return jax.nn.gelu(gate, approximate=False) * upper


def dot(a, b, a_axis, b_axis):
    return lax.dot_general(
        a, b, (((a_axis,), (b_axis,)), ((), ())), preferred_element_type=jnp.float32
    )


def layer_forward(hidden, qkv_w, others, kinds, shards, exchange, context, collective_id):
    batches = exchange.batches
    tokens = hidden.shape[0] // batches
    hidden_low = lax.optimization_barrier(hidden.astype(jnp.bfloat16))
    packed = dot(qkv_w, hidden_low, 0, 1).astype(jnp.bfloat16)
    packed = packed.reshape(3, HEADS, HEAD_DIM, batches, tokens)
    packed = packed.transpose(3, 1, 0, 2, 4).reshape(batches * HEADS, 3 * HEAD_DIM, tokens)
    attended, unit_packed, wide, sums, *gathered = attention_forward(
        packed,
        exchange,
        context,
        collective_id,
        Gather(kinds, shards, exchange.sizes, FORWARD_AHEAD, FORWARD_LAG),
        FORWARD_FIRST if kinds else 0,
    )
    out_w, up_w, down_w = others + [one.reshape(-1, one.shape[-1]) for one in gathered]
    norm_f = out_w[:, D : D + 4].astype(jnp.float32)
    out_w = out_w[:, :D]
    attn_t = attended.reshape(batches, D, tokens)
    attn_low = attn_t.transpose(0, 2, 1).reshape(batches * tokens, D)
    mixed = hidden + dot(attn_low, out_w, 1, 0)
    normed = layer_norm(mixed, norm_f[:, 0], norm_f[:, 1])
    normed_low = normed.astype(jnp.bfloat16)
    upper = dot(normed_low, up_w, 1, 0)
    act_low = geglu(upper[:, :FF], upper[:, FF:]).astype(jnp.bfloat16)
    second = normed + dot(act_low, down_w, 1, 0)
    result = layer_norm(second, norm_f[:, 2], norm_f[:, 3])
    weights = (qkv_w, out_w, up_w, down_w, norm_f)
    unit_kept = (unit_packed, wide, sums)
    kept = (hidden_low, unit_kept, attn_low, mixed, normed_low, upper, act_low, second)
    return result, weights, kept


def layer_backward(grad_result, weights, kept, exchange, context, collective_id):
    qkv_w, out_w, up_w, down_w, norm_f = weights
    hidden_low, unit_kept, attn_low, mixed, normed_low, upper, act_low, second = kept
    batches = exchange.batches
    tokens = grad_result.shape[0] // batches
    pull_two = jax.vjp(layer_norm, second, norm_f[:, 2], norm_f[:, 3])[1]
    grad_second, grad_gain_two, grad_shift_two = pull_two(grad_result)
    grad_branch = grad_second.astype(jnp.bfloat16)
    grad_act = dot(grad_branch, down_w, 1, 1)
    pull_gate = jax.vjp(geglu, upper[:, :FF], upper[:, FF:])[1]
    grad_gate, grad_upper = pull_gate(grad_act)
    grad_up_low = jnp.concatenate([grad_gate, grad_upper], axis=1).astype(jnp.bfloat16)
    grad_normed = grad_second + dot(grad_up_low, up_w, 1, 1)
    pull_one = jax.vjp(layer_norm, mixed, norm_f[:, 0], norm_f[:, 1])[1]
    grad_mixed, grad_gain_one, grad_shift_one = pull_one(grad_normed)
    grad_attn = grad_mixed.astype(jnp.bfloat16)
    grad_heads = dot(out_w, grad_attn, 1, 1).astype(jnp.bfloat16)
    grad_heads = grad_heads.reshape(HEADS, HEAD_DIM, batches, tokens)
    grad_heads = grad_heads.transpose(2, 0, 1, 3).reshape(batches * HEADS, HEAD_DIM, tokens)
    grad_norm = jnp.stack([grad_gain_one, grad_shift_one, grad_gain_two, grad_shift_two], axis=1)
    grad_out_w = jnp.concatenate(
        [
            dot(attn_low, grad_attn, 0, 0).astype(jnp.bfloat16),
            jnp.pad(grad_norm.astype(jnp.bfloat16), ((0, 0), (0, NORM_PAD - 4))),
        ],
        axis=1,
    )
    grad_up_w = dot(normed_low, grad_up_low, 0, 0).astype(jnp.bfloat16)
    grad_down_w = dot(act_low, grad_branch, 0, 0).astype(jnp.bfloat16)
    flow = Scatter(
        ["down", "up", "out"],
        [grad_down_w, grad_up_w, grad_out_w],
        exchange.sizes,
        BACKWARD_AHEAD,
        BACKWARD_LAG,
    )
    packed_grad, *totals = attention_backward(
        grad_heads,
        unit_kept,
        exchange,
        context,
        collective_id,
        flow,
        BACKWARD_FIRST,
    )
    packed_grad = packed_grad.reshape(batches, HEADS, 3, HEAD_DIM, tokens)
    packed_grad = packed_grad.transpose(0, 4, 2, 1, 3).reshape(batches * tokens, 3 * D)
    grad_hidden = grad_mixed + dot(packed_grad, qkv_w, 1, 1)
    grad_qkv_w = dot(hidden_low, packed_grad, 0, 0).astype(jnp.bfloat16)
    return grad_hidden, grad_qkv_w, totals


def adamw(weight, first, second, grad, rate):
    first_new = beta_one * first + (1.0 - beta_one) * grad
    second_new = beta_two * second + (1.0 - beta_two) * grad * grad
    first_hat = first_new / (1.0 - beta_one**STEP)
    second_hat = second_new / (1.0 - beta_two**STEP)
    weight_new = weight - rate * (first_hat / (jnp.sqrt(second_hat) + adam_eps) + decay * weight)
    return (first_new, second_new, weight_new)


def body(
    inputs,
    cotangent,
    lengths,
    qkv_weight,
    qkv_first,
    qkv_second,
    out_weight,
    out_first,
    out_second,
    up_weight,
    up_first,
    up_second,
    down_weight,
    down_first,
    down_second,
    norm_params,
    norm_first,
    norm_second,
):
    masters = (qkv_weight, out_weight, up_weight, down_weight, norm_params)
    states = (
        (qkv_first, qkv_second),
        (out_first, out_second),
        (up_first, up_second),
        (down_first, down_second),
        (norm_first, norm_second),
    )
    sizes = grid_sizes(lax.axis_size("seq"))
    batches, tokens = inputs.shape[:2]
    exchange = Exchange(sizes, batches, lengths.shape[1])
    context = unit_context(lengths, exchange, exchange.blocks * tokens)
    norm_wide = jnp.pad(norm_params, ((0, 0), (0, 0), (0, NORM_PAD - 4)))
    sources = (qkv_weight, jnp.concatenate([out_weight, norm_wide], axis=2), up_weight, down_weight)
    shards = [[source[layer].astype(jnp.bfloat16) for source in sources] for layer in range(LAYERS)]
    qkv_w = run_flow(Gather(["qkv"], shards[0][:1], sizes, 2, 1), 0, "gather_weights")[0]
    qkv_w = qkv_w.reshape(-1, qkv_w.shape[-1])
    everyone = ("head", "seq")
    later = [lax.all_gather(shard, everyone, axis=0, tiled=True) for shard in shards[1]]

    hidden = inputs.reshape(batches * tokens, D).astype(jnp.float32)
    weights_all, kept_all = [], []
    for layer in range(LAYERS):
        hidden, weights, kept = layer_forward(
            hidden,
            later[0] if layer else qkv_w,
            later[1:] if layer else [],
            [] if layer else ["out", "up", "down"],
            [] if layer else shards[0][1:],
            exchange,
            context,
            1 + layer,
        )
        weights_all.append(weights)
        kept_all.append(kept)
    outputs = hidden.reshape(batches, tokens, D)
    grad_hidden = cotangent.reshape(batches * tokens, D).astype(jnp.float32)
    totals = [[None] * 4 for _ in range(LAYERS)]
    late = []
    for layer in reversed(range(LAYERS)):
        grad_hidden, grad_qkv_w, done = layer_backward(
            grad_hidden,
            weights_all[layer],
            kept_all[layer],
            exchange,
            context,
            1 + LAYERS + layer,
        )
        totals[layer][3], totals[layer][2], totals[layer][1] = done
        late.append(grad_qkv_w)
    last = Scatter(["qkv"] * LAYERS, late, sizes, 4, 2)
    totals[1][0], totals[0][0] = run_flow(last, 1 + 2 * LAYERS, "scatter_grads")
    input_grad = grad_hidden.reshape(batches, tokens, D)

    results = [outputs, input_grad]
    kinds = [
        jnp.stack([totals[layer][0] for layer in range(LAYERS)]),
        jnp.stack([totals[layer][1][:, :D] for layer in range(LAYERS)]),
        jnp.stack([totals[layer][2] for layer in range(LAYERS)]),
        jnp.stack([totals[layer][3] for layer in range(LAYERS)]),
        jnp.stack([totals[layer][1][:, D : D + 4] for layer in range(LAYERS)]),
    ]
    new_weights = []
    for kind in range(5):
        first_new, second_new, weight_new = adamw(
            masters[kind], states[kind][0], states[kind][1], kinds[kind], learn_rates[kind]
        )
        results += [kinds[kind], first_new, second_new, weight_new]
        new_weights.append(weight_new)
    results += [member.astype(jnp.bfloat16) for member in new_weights[:4]]
    return tuple(results)


def solution(mesh):
    tokens = P(None, ("seq", "head"), None)
    rows = P(None, ("head", "seq"), None)
    in_specs = (tokens, tokens, P()) + (rows,) * 15
    out_specs = (tokens, tokens) + (rows,) * 24
    return jax.shard_map(body, mesh=mesh, in_specs=in_specs, out_specs=out_specs, check_vma=False)
```

```python
import functools
import math

import jax
import jax.numpy as jnp
from jax import lax
from jax.experimental import pallas as pl
from jax.experimental.pallas import tpu as pltpu
from jax.sharding import PartitionSpec as P

D = 768
HEADS = 12
HEAD_DIM = 64
FF = 3072
LAYERS = 2
WINDOW = 1024
STEP = 10

beta_one = 0.5
beta_two = 0.5
adam_eps = 1e-08
decay = 0.1
learn_rates = (0.03, 0.15, 0.03, 0.02, 0.2)

MESH = pl.DeviceIdType.MESH
TILE = 256
LOG2E = math.log2(math.e)
NORM_PAD = 128

CORES = 2
AXES = ("x", "z", "y", "c")


def cost_of(microseconds):
    return pl.CostEstimate(flops=0, bytes_accessed=int(microseconds * 3.69e6), transcendentals=0)


def grid_sizes(seq_size):
    rows = 2 if seq_size <= 16 else 4
    return {"x": lax.axis_size("head"), "z": seq_size // (rows * CORES), "y": rows, "c": CORES}


def quotient(value, divisor, count):
    result = 0
    for step in range(1, count):
        result = result + jnp.where(value >= step * divisor, 1, 0)
    return result


def wrapped(value, size):
    return value - jnp.where(value >= size, size, 0)


def own_place(sizes):
    seq = lax.axis_index("seq")
    return {
        "x": lax.axis_index("head"),
        "z": lax.div(seq, sizes["y"] * sizes["c"]),
        "y": lax.rem(lax.div(seq, sizes["c"]), sizes["y"]),
        "c": lax.rem(seq, sizes["c"]),
    }


def device_of(place, sizes):
    seq = (place["z"] * sizes["y"] + place["y"]) * sizes["c"] + place["c"]
    return {"head": place["x"], "seq": seq}


def peer_at(place, axis, step, sizes):
    other = dict(place)
    other[axis] = lax.rem(place[axis] + step, sizes[axis])
    return other


def greet_axes(place, sizes):
    barrier = pltpu.get_barrier_semaphore()
    count = 0
    for axis in AXES:
        for step in range(1, sizes[axis]):
            pl.semaphore_signal(
                barrier,
                inc=1,
                device_id=device_of(peer_at(place, axis, step, sizes), sizes),
                device_id_type=MESH,
            )
            count += 1
    pl.semaphore_wait(barrier, count)


def region(place, full, window):
    return tuple(slice(None) if axis in full else place[axis] for axis in AXES) + window


ZXY = ("z", "x", "y")
ZYX = ("z", "y", "x")

def steps_of(kind, rows):
    def halves(first, second, start=0):
        return ((0, rows, start, first, ZXY), (0, rows, start + first, second, ZYX))

    if kind == "qkv":
        return [halves(384, 384, start) for start in range(0, 3 * D, 768)]
    if kind == "out":
        return [halves(384, 512)]
    if kind == "up":
        return [halves(768, 768, start) for start in range(0, 2 * FF, 1536)]
    if rows % 32:
        return [halves(384, 384)]
    half = rows // 2
    return [
        ((0, half, start, 384, ZXY), (half, half, start, 384, ZYX)) for start in range(0, D, 384)
    ]


HBM = pl.BlockSpec(memory_space=pl.ANY)
VMEM = pl.BlockSpec(memory_space=pltpu.VMEM)
SMEM = pl.BlockSpec(memory_space=pltpu.SMEM)


class Flow:
    def __init__(self, kinds, operands, sizes, ahead, lag):
        self.operands = list(operands)
        self.sizes = sizes
        self.ahead, self.lag = ahead, lag
        self.steps, self.pieces = [], []
        for array, kind in enumerate(kinds):
            for step in steps_of(kind, operands[array].shape[-2]):
                self.steps.append(range(len(self.pieces), len(self.pieces) + len(step)))
                self.pieces += [(array,) + piece for piece in step]
        most = sum(size - 1 for size in sizes.values())
        self.semaphores = [
            pltpu.SemaphoreType.DMA((len(self.pieces), most)),
            pltpu.SemaphoreType.DMA((len(self.pieces), most)),
            pltpu.SemaphoreType.DMA((len(self.pieces),)),
        ]

        if not self.pieces:
            self.ahead, self.semaphores = 0, []

    def bind(self, ins, outs, scratch):
        self.place = own_place(self.sizes)
        if self.pieces:
            self.ins, self.outs, self.buffers = ins, outs, scratch[:-3]
            self.send_sem, self.recv_sem, self.own_sem = scratch[-3:]

    def window(self, number):
        _, row, rows, column, columns, _ = self.pieces[number]
        return (pl.ds(row, rows), pl.ds(column, columns))

    def remote(self, number, axis, step, source, target):
        before = AXES[: AXES.index(axis)]
        slot = sum(self.sizes[one] - 1 for one in before) + step - 1
        return pltpu.make_async_remote_copy(
            src_ref=source,
            dst_ref=target,
            send_sem=self.send_sem.at[number, slot],
            recv_sem=self.recv_sem.at[number, slot],
            device_id=device_of(peer_at(self.place, axis, step, self.sizes), self.sizes),
            device_id_type=MESH,
        )

    def numbers(self, step):
        return self.steps[step] if 0 <= step < len(self.steps) else ()

    def start(self, step, phase):
        for number in self.numbers(step):
            if phase == 0:
                self.own_copy(number).start()
            for copy in self.copies(number, phase):
                copy.start()

    def begin(self):
        for step in range(self.ahead):
            self.start(step, 0)

    def arrive(self, step, phase):
        for number in self.numbers(step):
            if phase == 0:
                self.own_copy(number).wait()
            for copy in self.copies(number, phase):
                copy.wait_recv()
            self.take(number, phase)

    def turns(self):
        def turn(index):
            self.start(index + self.ahead, 0)
            for phase in (3, 2, 1, 0):
                self.arrive(index - self.lag * phase, phase)
                if phase < 3:
                    self.start(index - self.lag * phase, phase + 1)

        count = len(self.steps) + 3 * self.lag if self.steps else 0
        return [functools.partial(turn, index) for index in range(count)]

    def end(self):
        for number in range(len(self.pieces)):
            for phase in range(4):
                for copy in self.copies(number, phase):
                    copy.wait_send()


class Gather(Flow):
    def __init__(self, kinds, shards, sizes, ahead, lag):
        super().__init__(kinds, shards, sizes, ahead, lag)
        lead = tuple(sizes[axis] for axis in AXES)
        self.out_shape = [jax.ShapeDtypeStruct(lead + one.shape, one.dtype) for one in shards]
        self.out_specs = [HBM] * len(shards)
        self.scratch = self.semaphores

    def own_copy(self, number):
        array, window = self.pieces[number][0], self.window(number)
        return pltpu.make_async_copy(
            self.ins[array].at[window],
            self.outs[array].at[region(self.place, (), window)],
            self.own_sem.at[number],
        )

    def copies(self, number, phase):
        array, order, window = self.pieces[number][0], self.pieces[number][-1], self.window(number)
        axis = (order + ("c",))[phase]
        part = self.outs[array].at[region(self.place, order[:phase], window)]
        source = self.ins[array].at[window] if phase == 0 else part
        return [
            self.remote(number, axis, step, source, part) for step in range(1, self.sizes[axis])
        ]

    def take(self, number, phase):
        pass


class Scatter(Flow):
    def __init__(self, kinds, grads, sizes, ahead, lag):
        grads = [
            grad.reshape(tuple(sizes[axis] for axis in AXES) + (-1, grad.shape[-1]))
            for grad in grads
        ]
        super().__init__(kinds, grads, sizes, ahead, lag)
        self.out_shape = [jax.ShapeDtypeStruct(grad.shape[-2:], jnp.float32) for grad in grads]
        self.out_specs = [VMEM] * len(grads)
        self.scratch = []
        for _, _, rows, _, columns, order in self.pieces:

            def shape_of(full, rows=rows, columns=columns):
                return tuple(sizes[axis] for axis in AXES if axis in full) + (rows, columns)

            self.scratch += [pltpu.VMEM(shape_of(order), jnp.bfloat16)] * 2
            for phase in range(3):
                senders = sizes[order[2 - phase]] - 1
                self.scratch.append(
                    pltpu.VMEM((senders,) + shape_of(order[: 2 - phase]), jnp.bfloat16)
                )
        self.scratch += self.semaphores

    def own_copy(self, number):
        array = self.pieces[number][0]
        return pltpu.make_async_copy(
            self.ins[array].at[region(self.place, AXES[:3], self.window(number))],
            self.buffers[5 * number],
            self.own_sem.at[number],
        )

    def copies(self, number, phase):
        array, order = self.pieces[number][0], self.pieces[number][-1]
        axis = "c" if phase == 0 else order[3 - phase]
        found = []
        for step in range(1, self.sizes[axis]):
            peer = peer_at(self.place, axis, step, self.sizes)
            if phase == 0:
                source = self.ins[array].at[region(peer, AXES[:3], self.window(number))]
                target = self.buffers[5 * number + 1]
            else:
                full = order[: 3 - phase]
                where = tuple(slice(None) if one in full else peer[one] for one in AXES[:3])
                source = self.buffers[5 * number].at[where]
                target = self.buffers[5 * number + 1 + phase].at[step - 1]
            found.append(self.remote(number, axis, step, source, target))
        return found

    def take(self, number, phase):
        array, order = self.pieces[number][0], self.pieces[number][-1]
        total = self.buffers[5 * number]
        got = self.buffers[5 * number + 1 + phase]
        if phase == 0:
            total[...] = total[...] + got[...]
            return
        full = order[: 3 - phase]
        where = tuple(slice(None) if axis in full else self.place[axis] for axis in AXES[:3])
        value = total[where]
        senders = self.sizes[order[3 - phase]] - 1
        if phase == 3:
            value = value.astype(jnp.float32)
            for sender in range(senders):
                value = value + got[sender].astype(jnp.float32)
            self.outs[array][self.window(number)] = value
        else:
            for sender in range(senders):
                value = value + got[sender]
            total[where] = value


def run_flow(flow, collective_id, name):
    count = len(flow.operands)

    def kernel(*refs):
        flow.bind(refs[:count], refs[count : 2 * count], refs[2 * count :])
        greet_axes(flow.place, flow.sizes)
        flow.begin()
        for turn in flow.turns():
            turn()
        flow.end()

    return pl.pallas_call(
        kernel,
        out_shape=flow.out_shape,
        in_specs=[HBM] * count,
        out_specs=flow.out_specs,
        scratch_shapes=flow.scratch,
        compiler_params=pltpu.CompilerParams(
            collective_id=collective_id, has_side_effects=True, vmem_limit_bytes=40 << 20
        ),
        cost_estimate=cost_of(30),
        name=name,
    )(*flow.operands)


def unit_place(unit, sizes):
    chips = sizes["x"] * sizes["y"]
    inside = quotient(unit, sizes["z"], chips * sizes["c"])
    row = quotient(inside, sizes["x"], sizes["y"] * sizes["c"])
    core = quotient(inside, chips, sizes["c"])
    x = inside - row * sizes["x"]
    y = wrapped(row - core * sizes["y"] + x, sizes["y"])
    return {"x": x, "z": unit - inside * sizes["z"], "y": y, "c": core}


def own_unit(sizes):
    place = own_place(sizes)
    turned = lax.rem(place["y"] + sizes["y"] * sizes["x"] - place["x"], sizes["y"])
    inside = (place["c"] * sizes["y"] + turned) * sizes["x"] + place["x"]
    return inside * sizes["z"] + place["z"]


class Exchange:
    def __init__(self, sizes, batches, sequences):
        self.sizes = sizes
        self.batches = batches
        self.sequences = sequences
        self.heads = sizes["x"]
        self.devices = math.prod(sizes.values())
        self.units = batches * sequences * HEADS
        self.blocks = self.devices // sequences
        self.held = batches * HEADS
        assert self.units <= self.devices

    def my_block(self):
        return lax.axis_index("seq") * self.heads + lax.axis_index("head")

    def unit_for(self, slot, block):
        batch = quotient(slot, HEADS, self.batches)
        sequence = quotient(block, self.blocks, self.sequences)
        return (batch * self.sequences + sequence) * HEADS + slot - batch * HEADS

    def block_device(self, block):
        return {"head": lax.rem(block, self.heads), "seq": lax.div(block, self.heads)}

    def token_device(self, unit, slot):
        if self.sequences > 1:
            slot = slot + lax.rem(lax.div(unit, HEADS), self.sequences) * self.blocks
        return self.block_device(slot)

    def unit_device(self, slot, block):
        return device_of(unit_place(self.unit_for(slot, block), self.sizes), self.sizes)

    def slot_of(self, unit):
        batch = lax.div(unit, HEADS * self.sequences)
        return lax.min(batch * HEADS + lax.rem(unit, HEADS), self.held - 1)

    def is_me(self, device):
        return jnp.logical_and(
            device["head"] == lax.axis_index("head"), device["seq"] == lax.axis_index("seq")
        )

    def greet_all(self):
        barrier = pltpu.get_barrier_semaphore()

        def greet(step, carry):
            device = self.block_device(lax.rem(self.my_block() + step, self.devices))
            pl.semaphore_signal(barrier, inc=1, device_id=device, device_id_type=MESH)
            return carry

        lax.fori_loop(1, self.devices, greet, 0)
        pl.semaphore_wait(barrier, self.devices - 1)

    def send(self, source, target, send_sem, recv_sem, own_sem, device, wait):
        same = self.is_me(device)
        remote = pltpu.make_async_remote_copy(
            src_ref=source,
            dst_ref=target,
            send_sem=send_sem,
            recv_sem=recv_sem,
            device_id=device,
            device_id_type=MESH,
        )
        if not wait:
            pl.when(same)(pltpu.make_async_copy(source, target, own_sem).start)

        @pl.when(jnp.logical_not(same))
        def _():
            remote.wait_send() if wait else remote.start()

    def receive(self, target, recv_sem, own_sem, device):
        same = self.is_me(device)

        @pl.when(same)
        def _():
            pltpu.make_async_copy(target, target, own_sem).wait()

        @pl.when(jnp.logical_not(same))
        def _():
            pltpu.make_async_copy(target, target, recv_sem).wait()

    def to_units(self, source_at, target_at, send_sem, recv_sem, own_sem, wait, part=0, parts=1):
        block = self.my_block()
        spot = block - quotient(block, self.blocks, self.sequences) * self.blocks
        turned = lax.rem(block, self.held)

        def one(index, carry):
            slot = wrapped(index + turned, self.held)
            self.send(
                source_at(slot),
                target_at(spot),
                send_sem.at[index],
                recv_sem.at[spot],
                own_sem,
                self.unit_device(slot, block),
                wait,
            )
            return carry

        lax.fori_loop(part * self.held // parts, (part + 1) * self.held // parts, one, 0)

    def at_unit(self, target_at, recv_sem, own_sem):
        unit = own_unit(self.sizes)

        def one(spot, carry):
            self.receive(
                target_at(spot), recv_sem.at[spot], own_sem, self.token_device(unit, spot)
            )
            return carry

        lax.fori_loop(0, self.blocks, one, 0)

    def to_token(self, spot, source_at, target_at, send_sem, recv_sem, own_sem, wait):
        unit = own_unit(self.sizes)
        slot = self.slot_of(unit)
        self.send(
            source_at(spot),
            target_at(slot),
            send_sem.at[spot],
            recv_sem.at[slot],
            own_sem,
            self.token_device(unit, spot),
            wait,
        )

    def at_tokens(self, target_at, recv_sem, own_sem):
        block = self.my_block()

        def one(slot, carry):
            self.receive(
                target_at(slot), recv_sem.at[slot], own_sem, self.unit_device(slot, block)
            )
            return carry

        lax.fori_loop(0, self.held, one, 0)


PART = 128
PER = TILE // PART
GUARD = WINDOW // TILE
REACH = 2 * GUARD + 1
DOC_ROWS = 64
FAR = -1e30
FORWARD_AHEAD, FORWARD_FIRST, FORWARD_LAG = 3, 5, 2
BACKWARD_AHEAD, BACKWARD_FIRST, BACKWARD_LAG = 4, 4, 2


def unit_context(lengths, exchange, tokens):
    unit = own_unit(exchange.sizes)
    row = lax.min(lax.div(unit, HEADS), exchange.batches * exchange.sequences - 1)
    head = lax.rem(unit, HEADS)
    own = lax.dynamic_index_in_dim(lengths.reshape(-1, lengths.shape[-1]), row, 0, keepdims=False)
    ends = jnp.cumsum(own)
    place = jnp.arange(tokens, dtype=jnp.int32)
    document = jnp.sum((place[None, :] >= ends[:, None]).astype(jnp.int32), axis=0)
    inside = jnp.arange(DOC_ROWS, dtype=jnp.int32)[:, None] == document[None, :]
    real = jnp.arange(DOC_ROWS, dtype=jnp.int32)[:, None] < lengths.shape[-1]
    of_query = jnp.where(inside, FAR, 0.0)
    of_key = jnp.where(real & ~inside, 1.0, 0.0)
    blocks = tokens // PART
    shape = (DOC_ROWS, blocks, PART)
    slope = jnp.exp2(-8.0 * (head + 1).astype(jnp.float32) / HEADS)
    return (
        (slope * LOG2E).reshape(1),
        of_query.reshape(shape).transpose(1, 0, 2).astype(jnp.bfloat16),
        of_key.reshape(shape).transpose(1, 0, 2).astype(jnp.bfloat16),
    )


def side_by_side(ref, tile, rows):
    return jnp.concatenate([ref[tile * PER + part, rows, :] for part in range(PER)], axis=1)


ROW_Q, ROW_K, ROW_V = slice(0, 64), slice(64, 128), slice(128, 192)


def rows_at(tile):
    return pl.ds(pl.multiple_of(tile * TILE, TILE), TILE)


def part_at(block):
    return pl.ds(pl.multiple_of(block * PART, PART), PART)


def fill_biases(slope_ref, bias_ref):
    key = lax.broadcasted_iota(jnp.int32, (TILE, TILE), 0)
    query = lax.broadcasted_iota(jnp.int32, (TILE, TILE), 1)

    def one(step, carry):
        distance = jnp.abs(key - query + (step - GUARD) * TILE)
        bias = distance.astype(jnp.float32) * -slope_ref[0]
        bias_ref[step] = jnp.where(distance < WINDOW, bias, FAR)
        return carry

    lax.fori_loop(0, REACH, one, 0)


def fill_guards(unit_ref, key_ref, blocks):
    rows = GUARD * TILE
    feature = lax.broadcasted_iota(jnp.int32, (rows, PART), 1)
    away = jnp.where((feature >= 64) & (feature < 72), 1.0, 0.0).astype(jnp.bfloat16)
    for first in (0, rows + blocks * PART):
        key_ref[pl.ds(first, rows), :] = away
    for first in (0, GUARD * PER + blocks):
        unit_ref[pl.ds(first, GUARD * PER)] = jnp.zeros(
            (GUARD * PER,) + unit_ref.shape[1:], unit_ref.dtype
        )


def fill_keys(unit_ref, doc_ref, key_ref, blocks):
    def one(block, carry):
        there = block + GUARD * PER
        features = jnp.concatenate([unit_ref[there, ROW_K, :], doc_ref[block]], axis=0)
        key_ref[part_at(there), :] = features.T
        return carry

    lax.fori_loop(0, blocks, one, 0, unroll=4)


class Service:
    def __init__(self, flow, first, tiles):
        self.turns = flow.turns()
        self.first = first
        self.after = {}
        left = max(len(self.turns) - first, 0)
        for index in range(left):
            self.after.setdefault(index * tiles // left, []).append(self.turns[first + index])

    def begin(self, done=0):
        for turn in self.turns[done : self.first]:
            turn()

    def at(self, tile):
        for index, turns in self.after.items():

            @pl.when(tile == index)
            def _(turns=turns):
                for turn in turns:
                    turn()


def attention_forward(packed, exchange, context, collective_id, flow, first):
    blocks, held = exchange.blocks, exchange.held
    tiles = blocks // PER
    edge = GUARD * PER

    count = len(flow.operands)

    def kernel(slope_ref, query_doc_ref, key_doc_ref, packed_ref, *refs):
        out_ref, keep_ref, wide_ref, sum_ref = refs[count : count + 4]
        flow.bind(refs[:count], refs[count + 4 : 2 * count + 4], refs[2 * count + 14 :])
        (
            unit_ref,
            key_ref,
            bias_ref,
            score_ref,
            result_ref,
            to_sem,
            at_sem,
            back_sem,
            home_sem,
            own_sem,
        ) = refs[2 * count + 4 : 2 * count + 14]
        service = Service(flow, first, tiles)
        has_unit = own_unit(exchange.sizes) < exchange.units
        exchange.greet_all()

        def units(wait, part=0, parts=1):
            exchange.to_units(
                lambda slot: packed_ref.at[slot],
                lambda spot: unit_ref.at[edge + spot],
                to_sem,
                at_sem,
                own_sem.at[0],
                wait,
                part,
                parts,
            )

        def tokens(spot, wait):
            exchange.to_token(
                spot,
                lambda spot: result_ref.at[spot],
                lambda slot: out_ref.at[slot],
                back_sem,
                home_sem,
                own_sem.at[1],
                wait,
            )

        keep = pltpu.make_async_copy(unit_ref.at[pl.ds(edge, blocks)], keep_ref, own_sem.at[2])
        flow.begin()
        parts = 3 if first > 2 else 1
        units(False, 0, parts)

        @pl.when(has_unit)
        def _():
            fill_biases(slope_ref, bias_ref)
            fill_guards(unit_ref, key_ref, blocks)

        for part in range(1, parts):
            service.turns[part - 1]()
            units(False, part, parts)
        service.begin(parts - 1)

        @pl.when(has_unit)
        def _():
            exchange.at_unit(lambda spot: unit_ref.at[edge + spot], at_sem, own_sem.at[0])
            keep.start()
            fill_keys(unit_ref, key_doc_ref, key_ref, blocks)

        def one_tile(tile, carry):
            @pl.when(has_unit)
            def _():
                q_t = jnp.concatenate(
                    [
                        side_by_side(unit_ref, tile + GUARD, ROW_Q),
                        side_by_side(query_doc_ref, tile, slice(0, DOC_ROWS)),
                    ],
                    axis=0,
                )
                top = jnp.full((1, TILE), FAR, jnp.float32)
                for step in range(REACH):
                    raw = jnp.dot(
                        key_ref[rows_at(tile + step), :], q_t, preferred_element_type=jnp.float32
                    )
                    score = raw * (HEAD_DIM ** (-0.5) * LOG2E) + bias_ref[step]
                    score_ref[step] = score
                    top = jnp.maximum(top, jnp.max(score, axis=0, keepdims=True))
                total = jnp.zeros((1, TILE), jnp.float32)
                attended = jnp.zeros((HEAD_DIM, TILE), jnp.float32)
                for step in range(REACH):
                    probs = jnp.exp2(score_ref[step] - top)
                    total = total + jnp.sum(probs, axis=0, keepdims=True)
                    attended = attended + jnp.dot(
                        side_by_side(unit_ref, tile + step, ROW_V),
                        probs.astype(jnp.bfloat16),
                        preferred_element_type=jnp.float32,
                    )
                result = attended / total
                sum_ref[tile] = top + jnp.log2(total)
                for part in range(PER):
                    piece = result[:, part * PART : (part + 1) * PART]
                    wide_ref[tile * PER + part] = piece
                    result_ref[tile * PER + part] = piece.astype(jnp.bfloat16)
                    tokens(tile * PER + part, False)

            service.at(tile)
            return carry

        lax.fori_loop(0, tiles, one_tile, 0)
        units(True)

        exchange.at_tokens(lambda slot: out_ref.at[slot], home_sem, own_sem.at[1])

        @pl.when(has_unit)
        def _():
            def sent(spot, carry):
                tokens(spot, True)
                return carry

            lax.fori_loop(0, blocks, sent, 0)
            keep.wait()

        flow.end()

    return pl.pallas_call(
        kernel,
        out_shape=[
            jax.ShapeDtypeStruct((held, HEAD_DIM, PART), jnp.bfloat16),
            jax.ShapeDtypeStruct((blocks, 3 * HEAD_DIM, PART), jnp.bfloat16),
            jax.ShapeDtypeStruct((blocks, HEAD_DIM, PART), jnp.float32),
            jax.ShapeDtypeStruct((tiles, 1, TILE), jnp.float32),
        ]
        + flow.out_shape,
        in_specs=[SMEM, VMEM, VMEM, HBM] + [HBM] * count,
        out_specs=[HBM, HBM, VMEM, VMEM] + flow.out_specs,
        scratch_shapes=[
            pltpu.VMEM((blocks + 2 * edge, 3 * HEAD_DIM, PART), jnp.bfloat16),
            pltpu.VMEM(((blocks + 2 * edge) * PART, PART), jnp.bfloat16),
            pltpu.VMEM((REACH, TILE, TILE), jnp.float32),
            pltpu.VMEM((REACH, TILE, TILE), jnp.float32),
            pltpu.VMEM((blocks, HEAD_DIM, PART), jnp.bfloat16),
            pltpu.SemaphoreType.DMA((held,)),
            pltpu.SemaphoreType.DMA((blocks,)),
            pltpu.SemaphoreType.DMA((blocks,)),
            pltpu.SemaphoreType.DMA((held,)),
            pltpu.SemaphoreType.DMA((3,)),
        ]
        + flow.scratch,
        compiler_params=pltpu.CompilerParams(
            collective_id=collective_id, has_side_effects=True, vmem_limit_bytes=48 << 20
        ),
        cost_estimate=cost_of(60),
        name="attention_forward",
    )(*context, packed, *flow.operands)


def attention_backward(grad, unit_kept, exchange, context, collective_id, flow, first):
    blocks, held = exchange.blocks, exchange.held
    tiles = blocks // PER
    edge = GUARD * PER

    count = len(flow.operands)

    def kernel(
        slope_ref, query_doc_ref, key_doc_ref, wide_ref, sum_ref, grad_ref, kept_ref, *refs
    ):
        out_ref = refs[count]
        flow.bind(refs[:count], refs[count + 1 : 2 * count + 1], refs[2 * count + 13 :])
        (
            unit_ref,
            got_ref,
            key_ref,
            value_ref,
            bias_ref,
            total_ref,
            result_ref,
            to_sem,
            at_sem,
            back_sem,
            home_sem,
            own_sem,
        ) = refs[2 * count + 1 : 2 * count + 13]
        service = Service(flow, first, tiles)
        has_unit = own_unit(exchange.sizes) < exchange.units
        exchange.greet_all()

        def units(wait):
            exchange.to_units(
                lambda slot: grad_ref.at[slot],
                lambda spot: got_ref.at[spot],
                to_sem,
                at_sem,
                own_sem.at[0],
                wait,
            )

        def tokens(spot, wait):
            exchange.to_token(
                spot,
                lambda spot: result_ref.at[spot],
                lambda slot: out_ref.at[slot],
                back_sem,
                home_sem,
                own_sem.at[1],
                wait,
            )

        load = pltpu.make_async_copy(kept_ref, unit_ref.at[pl.ds(edge, blocks)], own_sem.at[2])
        flow.begin()
        units(False)

        @pl.when(has_unit)
        def _():
            load.start()
            fill_biases(slope_ref, bias_ref)
            fill_guards(unit_ref, key_ref, blocks)
            for first in (0, (edge + blocks) * PART):
                value_ref[pl.ds(first, edge * PART), :] = jnp.zeros(
                    (edge * PART, PART), value_ref.dtype
                )
            total_ref[...] = jnp.zeros_like(total_ref)
            load.wait()
            fill_keys(unit_ref, key_doc_ref, key_ref, blocks)

            def one(block, carry):
                there = block + edge
                value_ref[part_at(there), :] = unit_ref[there, 64:192, :].T
                return carry

            lax.fori_loop(0, blocks, one, 0, unroll=4)

        service.begin()

        @pl.when(has_unit)
        def _():
            exchange.at_unit(lambda spot: got_ref.at[spot], at_sem, own_sem.at[0])

        def finish(tile):
            for part in range(PER):
                block = tile * PER + part
                result_ref[block, 64:192, :] = total_ref[part_at(block + edge), :].T.astype(
                    jnp.bfloat16
                )
                tokens(block, False)

        def one_tile(tile, carry):
            @pl.when(has_unit)
            def _():
                q_part = side_by_side(unit_ref, tile + GUARD, ROW_Q)
                g_part = side_by_side(got_ref, tile, slice(0, 64))
                q_t = jnp.concatenate(
                    [q_part, side_by_side(query_doc_ref, tile, slice(0, DOC_ROWS))], axis=0
                )
                g_small = g_part * jnp.asarray(HEAD_DIM ** (-0.5), jnp.bfloat16)
                g_t = jnp.concatenate([jnp.zeros_like(g_small), g_small], axis=0)
                turned = jnp.concatenate([q_part, g_part], axis=0).T
                lane = lax.broadcasted_iota(jnp.int32, turned.shape, 1)
                none = jnp.zeros_like(turned)
                q_and_g = jnp.concatenate(
                    [jnp.where(lane < 64, turned, none), jnp.where(lane < 64, none, turned)],
                    axis=0,
                )
                wide_t = side_by_side(wide_ref, tile, slice(0, 64))
                mean = jnp.sum(g_small.astype(jnp.float32) * wide_t, axis=0, keepdims=True)
                sum_now = sum_ref[tile]
                grad_q = jnp.zeros((HEAD_DIM, TILE), jnp.float32)
                for step in range(REACH):
                    there = rows_at(tile + step)
                    raw = jnp.dot(key_ref[there, :], q_t, preferred_element_type=jnp.float32)
                    grad_probs = jnp.dot(
                        value_ref[there, :], g_t, preferred_element_type=jnp.float32
                    )
                    score = raw * (HEAD_DIM ** (-0.5) * LOG2E) + bias_ref[step]
                    probs = jnp.exp2(score - sum_now)
                    grad_raw = (probs * (grad_probs - mean)).astype(jnp.bfloat16)
                    total_ref[there, :] += jnp.dot(
                        jnp.concatenate([grad_raw, probs.astype(jnp.bfloat16)], axis=1),
                        q_and_g,
                        preferred_element_type=jnp.float32,
                    )
                    grad_q = grad_q + jnp.dot(
                        side_by_side(unit_ref, tile + step, ROW_K),
                        grad_raw,
                        preferred_element_type=jnp.float32,
                    )
                for part in range(PER):
                    result_ref[tile * PER + part, ROW_Q, :] = grad_q[
                        :, part * PART : (part + 1) * PART
                    ].astype(jnp.bfloat16)

                @pl.when(tile >= GUARD)
                def _():
                    finish(tile - GUARD)

            service.at(tile)
            return carry

        lax.fori_loop(0, tiles, one_tile, 0)
        units(True)

        @pl.when(has_unit)
        def _():
            def rest(tile, carry):
                finish(tile)
                return carry

            lax.fori_loop(max(tiles - GUARD, 0), tiles, rest, 0)

        exchange.at_tokens(lambda slot: out_ref.at[slot], home_sem, own_sem.at[1])

        @pl.when(has_unit)
        def _():
            def sent(spot, carry):
                tokens(spot, True)
                return carry

            lax.fori_loop(0, blocks, sent, 0)

        flow.end()

    return pl.pallas_call(
        kernel,
        out_shape=[jax.ShapeDtypeStruct((held, 3 * HEAD_DIM, PART), jnp.bfloat16)] + flow.out_shape,
        in_specs=[SMEM, VMEM, VMEM, VMEM, VMEM, HBM, HBM] + [HBM] * count,
        out_specs=[HBM] + flow.out_specs,
        scratch_shapes=[
            pltpu.VMEM((blocks + 2 * edge, 3 * HEAD_DIM, PART), jnp.bfloat16),
            pltpu.VMEM((blocks, HEAD_DIM, PART), jnp.bfloat16),
            pltpu.VMEM(((blocks + 2 * edge) * PART, PART), jnp.bfloat16),
            pltpu.VMEM(((blocks + 2 * edge) * PART, PART), jnp.bfloat16),
            pltpu.VMEM((REACH, TILE, TILE), jnp.float32),
            pltpu.VMEM(((blocks + 2 * edge) * PART, PART), jnp.float32),
            pltpu.VMEM((blocks, 3 * HEAD_DIM, PART), jnp.bfloat16),
            pltpu.SemaphoreType.DMA((held,)),
            pltpu.SemaphoreType.DMA((blocks,)),
            pltpu.SemaphoreType.DMA((blocks,)),
            pltpu.SemaphoreType.DMA((held,)),
            pltpu.SemaphoreType.DMA((3,)),
        ]
        + flow.scratch,
        compiler_params=pltpu.CompilerParams(
            collective_id=collective_id, has_side_effects=True, vmem_limit_bytes=60 << 20
        ),
        cost_estimate=cost_of(70),
        name="attention_backward",
    )(*context, *unit_kept[1:], grad, unit_kept[0], *flow.operands)


def layer_norm(summed, gain, shift):
    centre = jnp.mean(summed, axis=-1, keepdims=True)
    centred = summed - centre
    variance = jnp.mean(centred * centred, axis=-1, keepdims=True)
    return centred * lax.rsqrt(variance + 1e-12) * gain + shift


def normal_share(gate):
    return 0.5 * lax.erf(gate * math.sqrt(0.5)) + 0.5


def geglu(gate, upper):
    return gate * normal_share(gate) * upper


def geglu_backward(gate, upper, grad):
    share = normal_share(gate)
    slope = share + gate * jnp.exp(-0.5 * gate * gate) * (1.0 / math.sqrt(2.0 * math.pi))
    return grad * upper * slope, grad * (gate * share)


def dot(a, b, a_axis, b_axis):
    return lax.dot_general(
        a, b, (((a_axis,), (b_axis,)), ((), ())), preferred_element_type=jnp.float32
    )


def layer_forward(hidden, qkv_w, others, kinds, shards, exchange, context, collective_id):
    batches = exchange.batches
    tokens = hidden.shape[0] // batches
    hidden_low = lax.optimization_barrier(hidden.astype(jnp.bfloat16))
    packed = dot(qkv_w, hidden_low, 0, 1).astype(jnp.bfloat16)
    packed = packed.reshape(3, HEADS, HEAD_DIM, batches, tokens)
    packed = packed.transpose(3, 1, 0, 2, 4).reshape(batches * HEADS, 3 * HEAD_DIM, tokens)
    attended, unit_packed, wide, sums, *gathered = attention_forward(
        packed,
        exchange,
        context,
        collective_id,
        Gather(kinds, shards, exchange.sizes, FORWARD_AHEAD, FORWARD_LAG),
        FORWARD_FIRST if len(kinds) > 1 else 1,
    )
    gathered = [one.reshape(-1, one.shape[-1]) for one in gathered]
    out_w, up_w, down_w = gathered + others
    norm_f = out_w[:, D : D + 4].astype(jnp.float32)
    out_w = out_w[:, :D]
    attn_t = attended.reshape(batches, D, tokens)
    attn_low = attn_t.transpose(0, 2, 1).reshape(batches * tokens, D)
    mixed = hidden + dot(attn_low, out_w, 1, 0)
    normed = layer_norm(mixed, norm_f[:, 0], norm_f[:, 1])
    normed_low = normed.astype(jnp.bfloat16)
    upper = dot(normed_low, up_w, 1, 0)
    act_low = geglu(upper[:, :FF], upper[:, FF:]).astype(jnp.bfloat16)
    second = normed + dot(act_low, down_w, 1, 0)
    result = layer_norm(second, norm_f[:, 2], norm_f[:, 3])
    weights = (qkv_w, out_w, up_w, down_w, norm_f)
    unit_kept = (unit_packed, wide, sums)
    kept = (hidden_low, unit_kept, attn_low, mixed, normed_low, upper, act_low, second)
    return result, weights, kept


def layer_backward(grad_result, weights, kept, exchange, context, collective_id):
    qkv_w, out_w, up_w, down_w, norm_f = weights
    hidden_low, unit_kept, attn_low, mixed, normed_low, upper, act_low, second = kept
    batches = exchange.batches
    tokens = grad_result.shape[0] // batches
    pull_two = jax.vjp(layer_norm, second, norm_f[:, 2], norm_f[:, 3])[1]
    grad_second, grad_gain_two, grad_shift_two = pull_two(grad_result)
    grad_branch = grad_second.astype(jnp.bfloat16)
    grad_act = dot(grad_branch, down_w, 1, 1)
    grad_gate, grad_upper = geglu_backward(upper[:, :FF], upper[:, FF:], grad_act)
    grad_up_low = jnp.concatenate([grad_gate, grad_upper], axis=1).astype(jnp.bfloat16)
    grad_normed = grad_second + dot(grad_up_low, up_w, 1, 1)
    pull_one = jax.vjp(layer_norm, mixed, norm_f[:, 0], norm_f[:, 1])[1]
    grad_mixed, grad_gain_one, grad_shift_one = pull_one(grad_normed)
    grad_attn = grad_mixed.astype(jnp.bfloat16)
    grad_heads = dot(out_w, grad_attn, 1, 1).astype(jnp.bfloat16)
    grad_heads = grad_heads.reshape(HEADS, HEAD_DIM, batches, tokens)
    grad_heads = grad_heads.transpose(2, 0, 1, 3).reshape(batches * HEADS, HEAD_DIM, tokens)
    grad_norm = jnp.stack([grad_gain_one, grad_shift_one, grad_gain_two, grad_shift_two], axis=1)
    grad_out_w = jnp.concatenate(
        [
            dot(attn_low, grad_attn, 0, 0).astype(jnp.bfloat16),
            jnp.pad(grad_norm.astype(jnp.bfloat16), ((0, 0), (0, NORM_PAD - 4))),
        ],
        axis=1,
    )
    grad_up_w = dot(normed_low, grad_up_low, 0, 0).astype(jnp.bfloat16)
    grad_down_w = dot(act_low, grad_branch, 0, 0).astype(jnp.bfloat16)
    flow = Scatter(
        ["down", "up", "out"],
        [grad_down_w, grad_up_w, grad_out_w],
        exchange.sizes,
        BACKWARD_AHEAD,
        BACKWARD_LAG,
    )
    packed_grad, *totals = attention_backward(
        grad_heads,
        unit_kept,
        exchange,
        context,
        collective_id,
        flow,
        BACKWARD_FIRST,
    )
    packed_grad = packed_grad.reshape(batches, HEADS, 3, HEAD_DIM, tokens)
    packed_grad = packed_grad.transpose(0, 4, 2, 1, 3).reshape(batches * tokens, 3 * D)
    grad_hidden = grad_mixed + dot(packed_grad, qkv_w, 1, 1)
    grad_qkv_w = dot(hidden_low, packed_grad, 0, 0).astype(jnp.bfloat16)
    return grad_hidden, grad_qkv_w, totals


def adamw(weight, first, second, grad, rate):
    first_new = beta_one * first + (1.0 - beta_one) * grad
    second_new = beta_two * second + (1.0 - beta_two) * grad * grad
    first_hat = first_new / (1.0 - beta_one**STEP)
    second_hat = second_new / (1.0 - beta_two**STEP)
    weight_new = weight - rate * (first_hat / (jnp.sqrt(second_hat) + adam_eps) + decay * weight)
    return (first_new, second_new, weight_new)


def body(
    inputs,
    cotangent,
    lengths,
    qkv_weight,
    qkv_first,
    qkv_second,
    out_weight,
    out_first,
    out_second,
    up_weight,
    up_first,
    up_second,
    down_weight,
    down_first,
    down_second,
    norm_params,
    norm_first,
    norm_second,
):
    masters = (qkv_weight, out_weight, up_weight, down_weight, norm_params)
    states = (
        (qkv_first, qkv_second),
        (out_first, out_second),
        (up_first, up_second),
        (down_first, down_second),
        (norm_first, norm_second),
    )
    sizes = grid_sizes(lax.axis_size("seq"))
    batches, tokens = inputs.shape[:2]
    exchange = Exchange(sizes, batches, lengths.shape[1])
    context = unit_context(lengths, exchange, exchange.blocks * tokens)
    norm_wide = jnp.pad(norm_params, ((0, 0), (0, 0), (0, NORM_PAD - 4)))
    sources = (qkv_weight, jnp.concatenate([out_weight, norm_wide], axis=2), up_weight, down_weight)
    shards = [[source[layer].astype(jnp.bfloat16) for source in sources] for layer in range(LAYERS)]
    qkv_w = run_flow(Gather(["qkv"], shards[0][:1], sizes, 2, 1), 0, "gather_weights")[0]
    qkv_w = qkv_w.reshape(-1, qkv_w.shape[-1])
    everyone = ("head", "seq")
    qkv_w, *later = lax.optimization_barrier((qkv_w, shards[1][0], *shards[1][2:]))
    later = [lax.all_gather(shard, everyone, axis=0, tiled=True) for shard in later]

    hidden = inputs.reshape(batches * tokens, D).astype(jnp.float32)
    weights_all, kept_all = [], []
    for layer in range(LAYERS):
        hidden, weights, kept = layer_forward(
            hidden,
            later[0] if layer else qkv_w,
            later[1:] if layer else [],
            ["out"] if layer else ["out", "up", "down"],
            shards[layer][1:2] if layer else shards[0][1:],
            exchange,
            context,
            1 + layer,
        )
        weights_all.append(weights)
        kept_all.append(kept)
    outputs = hidden.reshape(batches, tokens, D)
    grad_hidden = cotangent.reshape(batches * tokens, D).astype(jnp.float32)
    totals = [[None] * 4 for _ in range(LAYERS)]
    late = []
    for layer in reversed(range(LAYERS)):
        grad_hidden, grad_qkv_w, done = layer_backward(
            grad_hidden,
            weights_all[layer],
            kept_all[layer],
            exchange,
            context,
            1 + LAYERS + layer,
        )
        totals[layer][3], totals[layer][2], totals[layer][1] = done
        late.append(grad_qkv_w)
    last = Scatter(["qkv"] * LAYERS, late, sizes, 4, 2)
    totals[1][0], totals[0][0] = run_flow(last, 1 + 2 * LAYERS, "scatter_grads")
    input_grad = grad_hidden.reshape(batches, tokens, D)

    results = [outputs, input_grad]
    kinds = [
        jnp.stack([totals[layer][0] for layer in range(LAYERS)]),
        jnp.stack([totals[layer][1][:, :D] for layer in range(LAYERS)]),
        jnp.stack([totals[layer][2] for layer in range(LAYERS)]),
        jnp.stack([totals[layer][3] for layer in range(LAYERS)]),
        jnp.stack([totals[layer][1][:, D : D + 4] for layer in range(LAYERS)]),
    ]
    new_weights = []
    for kind in range(5):
        first_new, second_new, weight_new = adamw(
            masters[kind], states[kind][0], states[kind][1], kinds[kind], learn_rates[kind]
        )
        results += [kinds[kind], first_new, second_new, weight_new]
        new_weights.append(weight_new)
    results += [member.astype(jnp.bfloat16) for member in new_weights[:4]]
    return tuple(results)


def solution(mesh):
    tokens = P(None, ("seq", "head"), None)
    rows = P(None, ("head", "seq"), None)
    in_specs = (tokens, tokens, P()) + (rows,) * 15
    out_specs = (tokens, tokens) + (rows,) * 24
    return jax.shard_map(body, mesh=mesh, in_specs=in_specs, out_specs=out_specs, check_vma=False)
```

```python
import functools
import math

import jax
import jax.numpy as jnp
from jax import lax
from jax.experimental import pallas as pl
from jax.experimental.pallas import tpu as pltpu
from jax.sharding import PartitionSpec as P

D = 768
HEADS = 12
HEAD_DIM = 64
FF = 3072
LAYERS = 2
WINDOW = 1024
STEP = 10

beta_one = 0.5
beta_two = 0.5
adam_eps = 1e-08
decay = 0.1
learn_rates = (0.03, 0.15, 0.03, 0.02, 0.2)

MESH = pl.DeviceIdType.MESH
TILE = 256
LOG2E = math.log2(math.e)
NORM_PAD = 128

CORES = 2
AXES = ("x", "z", "y", "c")


def cost_of(microseconds):
    return pl.CostEstimate(flops=0, bytes_accessed=int(microseconds * 3.69e6), transcendentals=0)


def grid_sizes(seq_size):
    rows = 2 if seq_size <= 16 else 4
    return {"x": lax.axis_size("head"), "z": seq_size // (rows * CORES), "y": rows, "c": CORES}


def quotient(value, divisor, count):
    result = 0
    for step in range(1, count):
        result = result + jnp.where(value >= step * divisor, 1, 0)
    return result


def wrapped(value, size):
    return value - jnp.where(value >= size, size, 0)


def own_place(sizes):
    seq = lax.axis_index("seq")
    return {
        "x": lax.axis_index("head"),
        "z": lax.div(seq, sizes["y"] * sizes["c"]),
        "y": lax.rem(lax.div(seq, sizes["c"]), sizes["y"]),
        "c": lax.rem(seq, sizes["c"]),
    }


def device_of(place, sizes):
    seq = (place["z"] * sizes["y"] + place["y"]) * sizes["c"] + place["c"]
    return {"head": place["x"], "seq": seq}


def peer_at(place, axis, step, sizes):
    other = dict(place)
    other[axis] = lax.rem(place[axis] + step, sizes[axis])
    return other


def greet_axes(place, sizes):
    barrier = pltpu.get_barrier_semaphore()
    count = 0
    for axis in AXES:
        for step in range(1, sizes[axis]):
            pl.semaphore_signal(
                barrier,
                inc=1,
                device_id=device_of(peer_at(place, axis, step, sizes), sizes),
                device_id_type=MESH,
            )
            count += 1
    pl.semaphore_wait(barrier, count)


def region(place, full, window):
    return tuple(slice(None) if axis in full else place[axis] for axis in AXES) + window


ZXY = ("z", "x", "y")
ZYX = ("z", "y", "x")

def steps_of(kind, rows):
    def halves(first, second, start=0):
        return ((0, rows, start, first, ZXY), (0, rows, start + first, second, ZYX))

    if kind == "qkv":
        return [halves(384, 384, start) for start in range(0, 3 * D, 768)]
    if kind == "out":
        return [halves(384, 512)]
    if kind == "up":
        return [halves(384, 384, start) for start in range(0, 2 * FF, 768)]
    if rows % 32:
        return [halves(384, 384)]
    return [((row, 16, 0, D, ZXY), (row + 16, 16, 0, D, ZYX)) for row in range(0, rows, 32)]


HBM = pl.BlockSpec(memory_space=pl.ANY)
VMEM = pl.BlockSpec(memory_space=pltpu.VMEM)
SMEM = pl.BlockSpec(memory_space=pltpu.SMEM)


class Flow:
    def __init__(self, kinds, operands, sizes, ahead, lag):
        self.operands = list(operands)
        self.sizes = sizes
        self.ahead, self.lag = ahead, lag
        self.steps, self.pieces = [], []
        for array, kind in enumerate(kinds):
            for step in steps_of(kind, operands[array].shape[-2]):
                self.steps.append(range(len(self.pieces), len(self.pieces) + len(step)))
                self.pieces += [(array,) + piece for piece in step]
        most = sum(size - 1 for size in sizes.values())
        self.semaphores = [
            pltpu.SemaphoreType.DMA((len(self.pieces), most)),
            pltpu.SemaphoreType.DMA((len(self.pieces), most)),
            pltpu.SemaphoreType.DMA((len(self.pieces),)),
        ]

        if not self.pieces:
            self.ahead, self.semaphores = 0, []

    def bind(self, ins, outs, scratch):
        self.place = own_place(self.sizes)
        if self.pieces:
            self.ins, self.outs, self.buffers = ins, outs, scratch[:-3]
            self.send_sem, self.recv_sem, self.own_sem = scratch[-3:]

    def window(self, number):
        _, row, rows, column, columns, _ = self.pieces[number]
        return (pl.ds(row, rows), pl.ds(column, columns))

    def remote(self, number, axis, step, source, target):
        before = AXES[: AXES.index(axis)]
        slot = sum(self.sizes[one] - 1 for one in before) + step - 1
        return pltpu.make_async_remote_copy(
            src_ref=source,
            dst_ref=target,
            send_sem=self.send_sem.at[number, slot],
            recv_sem=self.recv_sem.at[number, slot],
            device_id=device_of(peer_at(self.place, axis, step, self.sizes), self.sizes),
            device_id_type=MESH,
        )

    def numbers(self, step):
        return self.steps[step] if 0 <= step < len(self.steps) else ()

    def start(self, step, phase):
        for number in self.numbers(step):
            if phase == 0:
                self.own_copy(number).start()
            for copy in self.copies(number, phase):
                copy.start()

    def begin(self):
        for step in range(self.ahead):
            self.start(step, 0)

    def arrive(self, step, phase):
        for number in self.numbers(step):
            if phase == 0:
                self.own_copy(number).wait()
            for copy in self.copies(number, phase):
                copy.wait_recv()
            self.take(number, phase)

    def turns(self):
        def turn(index):
            self.start(index + self.ahead, 0)
            for phase in (3, 2, 1, 0):
                self.arrive(index - self.lag * phase, phase)
                if phase < 3:
                    self.start(index - self.lag * phase, phase + 1)

        count = len(self.steps) + 3 * self.lag if self.steps else 0
        return [functools.partial(turn, index) for index in range(count)]

    def end(self):
        for number in range(len(self.pieces)):
            for phase in range(4):
                for copy in self.copies(number, phase):
                    copy.wait_send()


class Gather(Flow):
    def __init__(self, kinds, shards, sizes, ahead, lag):
        super().__init__(kinds, shards, sizes, ahead, lag)
        lead = tuple(sizes[axis] for axis in AXES)
        self.out_shape = [jax.ShapeDtypeStruct(lead + one.shape, one.dtype) for one in shards]
        self.out_specs = [HBM] * len(shards)
        self.scratch = self.semaphores

    def own_copy(self, number):
        array, window = self.pieces[number][0], self.window(number)
        return pltpu.make_async_copy(
            self.ins[array].at[window],
            self.outs[array].at[region(self.place, (), window)],
            self.own_sem.at[number],
        )

    def copies(self, number, phase):
        array, order, window = self.pieces[number][0], self.pieces[number][-1], self.window(number)
        axis = (order + ("c",))[phase]
        part = self.outs[array].at[region(self.place, order[:phase], window)]
        source = self.ins[array].at[window] if phase == 0 else part
        return [
            self.remote(number, axis, step, source, part) for step in range(1, self.sizes[axis])
        ]

    def take(self, number, phase):
        pass


class Scatter(Flow):
    def __init__(self, kinds, grads, sizes, ahead, lag):
        grads = [
            grad.reshape(tuple(sizes[axis] for axis in AXES) + (-1, grad.shape[-1]))
            for grad in grads
        ]
        super().__init__(kinds, grads, sizes, ahead, lag)
        self.out_shape = [jax.ShapeDtypeStruct(grad.shape[-2:], jnp.float32) for grad in grads]
        self.out_specs = [VMEM] * len(grads)
        self.scratch = []
        for _, _, rows, _, columns, order in self.pieces:

            def shape_of(full, rows=rows, columns=columns):
                return tuple(sizes[axis] for axis in AXES if axis in full) + (rows, columns)

            self.scratch += [pltpu.VMEM(shape_of(order), jnp.bfloat16)] * 2
            for phase in range(3):
                senders = sizes[order[2 - phase]] - 1
                self.scratch.append(
                    pltpu.VMEM((senders,) + shape_of(order[: 2 - phase]), jnp.bfloat16)
                )
        self.scratch += self.semaphores

    def own_copy(self, number):
        array = self.pieces[number][0]
        return pltpu.make_async_copy(
            self.ins[array].at[region(self.place, AXES[:3], self.window(number))],
            self.buffers[5 * number],
            self.own_sem.at[number],
        )

    def copies(self, number, phase):
        array, order = self.pieces[number][0], self.pieces[number][-1]
        axis = "c" if phase == 0 else order[3 - phase]
        found = []
        for step in range(1, self.sizes[axis]):
            peer = peer_at(self.place, axis, step, self.sizes)
            if phase == 0:
                source = self.ins[array].at[region(peer, AXES[:3], self.window(number))]
                target = self.buffers[5 * number + 1]
            else:
                full = order[: 3 - phase]
                where = tuple(slice(None) if one in full else peer[one] for one in AXES[:3])
                source = self.buffers[5 * number].at[where]
                target = self.buffers[5 * number + 1 + phase].at[step - 1]
            found.append(self.remote(number, axis, step, source, target))
        return found

    def take(self, number, phase):
        array, order = self.pieces[number][0], self.pieces[number][-1]
        total = self.buffers[5 * number]
        got = self.buffers[5 * number + 1 + phase]
        if phase == 0:
            total[...] = total[...] + got[...]
            return
        full = order[: 3 - phase]
        where = tuple(slice(None) if axis in full else self.place[axis] for axis in AXES[:3])
        value = total[where]
        senders = self.sizes[order[3 - phase]] - 1
        if phase == 3:
            value = value.astype(jnp.float32)
            for sender in range(senders):
                value = value + got[sender].astype(jnp.float32)
            self.outs[array][self.window(number)] = value
        else:
            for sender in range(senders):
                value = value + got[sender]
            total[where] = value


def run_flow(flow, collective_id, name):
    count = len(flow.operands)

    def kernel(*refs):
        flow.bind(refs[:count], refs[count : 2 * count], refs[2 * count :])
        greet_axes(flow.place, flow.sizes)
        flow.begin()
        for turn in flow.turns():
            turn()
        flow.end()

    return pl.pallas_call(
        kernel,
        out_shape=flow.out_shape,
        in_specs=[HBM] * count,
        out_specs=flow.out_specs,
        scratch_shapes=flow.scratch,
        compiler_params=pltpu.CompilerParams(
            collective_id=collective_id, has_side_effects=True, vmem_limit_bytes=40 << 20
        ),
        cost_estimate=cost_of(30),
        name=name,
    )(*flow.operands)


def unit_place(unit, sizes):
    chips = sizes["x"] * sizes["y"]
    inside = quotient(unit, sizes["z"], chips * sizes["c"])
    row = quotient(inside, sizes["x"], sizes["y"] * sizes["c"])
    core = quotient(inside, chips, sizes["c"])
    x = inside - row * sizes["x"]
    y = wrapped(row - core * sizes["y"] + x, sizes["y"])
    return {"x": x, "z": unit - inside * sizes["z"], "y": y, "c": core}


def own_unit(sizes):
    place = own_place(sizes)
    turned = lax.rem(place["y"] + sizes["y"] * sizes["x"] - place["x"], sizes["y"])
    inside = (place["c"] * sizes["y"] + turned) * sizes["x"] + place["x"]
    return inside * sizes["z"] + place["z"]


class Exchange:
    def __init__(self, sizes, batches, sequences):
        self.sizes = sizes
        self.batches = batches
        self.sequences = sequences
        self.heads = sizes["x"]
        self.devices = math.prod(sizes.values())
        self.units = batches * sequences * HEADS
        self.blocks = self.devices // sequences
        self.held = batches * HEADS
        assert self.units <= self.devices

    def my_block(self):
        return lax.axis_index("seq") * self.heads + lax.axis_index("head")

    def unit_for(self, slot, block):
        batch = quotient(slot, HEADS, self.batches)
        sequence = quotient(block, self.blocks, self.sequences)
        return (batch * self.sequences + sequence) * HEADS + slot - batch * HEADS

    def block_device(self, block):
        return {"head": lax.rem(block, self.heads), "seq": lax.div(block, self.heads)}

    def token_device(self, unit, slot):
        if self.sequences > 1:
            slot = slot + lax.rem(lax.div(unit, HEADS), self.sequences) * self.blocks
        return self.block_device(slot)

    def unit_device(self, slot, block):
        return device_of(unit_place(self.unit_for(slot, block), self.sizes), self.sizes)

    def slot_of(self, unit):
        batch = lax.div(unit, HEADS * self.sequences)
        return lax.min(batch * HEADS + lax.rem(unit, HEADS), self.held - 1)

    def is_me(self, device):
        return jnp.logical_and(
            device["head"] == lax.axis_index("head"), device["seq"] == lax.axis_index("seq")
        )

    def greet_all(self):
        barrier = pltpu.get_barrier_semaphore()

        def greet(step, carry):
            device = self.block_device(lax.rem(self.my_block() + step, self.devices))
            pl.semaphore_signal(barrier, inc=1, device_id=device, device_id_type=MESH)
            return carry

        lax.fori_loop(1, self.devices, greet, 0)
        pl.semaphore_wait(barrier, self.devices - 1)

    def send(self, source, target, send_sem, recv_sem, own_sem, device, wait):
        same = self.is_me(device)
        remote = pltpu.make_async_remote_copy(
            src_ref=source,
            dst_ref=target,
            send_sem=send_sem,
            recv_sem=recv_sem,
            device_id=device,
            device_id_type=MESH,
        )
        if not wait:
            pl.when(same)(pltpu.make_async_copy(source, target, own_sem).start)

        @pl.when(jnp.logical_not(same))
        def _():
            remote.wait_send() if wait else remote.start()

    def receive(self, target, recv_sem, own_sem, device):
        same = self.is_me(device)

        @pl.when(same)
        def _():
            pltpu.make_async_copy(target, target, own_sem).wait()

        @pl.when(jnp.logical_not(same))
        def _():
            pltpu.make_async_copy(target, target, recv_sem).wait()

    def to_units(self, source_at, target_at, send_sem, recv_sem, own_sem, wait, part=0, parts=1):
        block = self.my_block()
        spot = block - quotient(block, self.blocks, self.sequences) * self.blocks
        turned = lax.rem(block, self.held)

        def one(index, carry):
            slot = wrapped(index + turned, self.held)
            self.send(
                source_at(slot),
                target_at(spot),
                send_sem.at[index],
                recv_sem.at[spot],
                own_sem,
                self.unit_device(slot, block),
                wait,
            )
            return carry

        lax.fori_loop(part * self.held // parts, (part + 1) * self.held // parts, one, 0)

    def at_unit(self, target_at, recv_sem, own_sem):
        unit = own_unit(self.sizes)

        def one(spot, carry):
            self.receive(
                target_at(spot), recv_sem.at[spot], own_sem, self.token_device(unit, spot)
            )
            return carry

        lax.fori_loop(0, self.blocks, one, 0)

    def to_token(self, spot, source_at, target_at, send_sem, recv_sem, own_sem, wait):
        unit = own_unit(self.sizes)
        slot = self.slot_of(unit)
        self.send(
            source_at(spot),
            target_at(slot),
            send_sem.at[spot],
            recv_sem.at[slot],
            own_sem,
            self.token_device(unit, spot),
            wait,
        )

    def at_tokens(self, target_at, recv_sem, own_sem):
        block = self.my_block()

        def one(slot, carry):
            self.receive(
                target_at(slot), recv_sem.at[slot], own_sem, self.unit_device(slot, block)
            )
            return carry

        lax.fori_loop(0, self.held, one, 0)


PART = 128
PER = TILE // PART
GUARD = WINDOW // TILE
REACH = 2 * GUARD + 1
DOC_ROWS = 64
FAR = -1e30
FORWARD_AHEAD, FORWARD_FIRST, FORWARD_LAG = 4, 8, 2
BACKWARD_AHEAD, BACKWARD_FIRST, BACKWARD_LAG = 5, 5, 2


def unit_context(lengths, exchange, tokens):
    unit = own_unit(exchange.sizes)
    row = lax.min(lax.div(unit, HEADS), exchange.batches * exchange.sequences - 1)
    head = lax.rem(unit, HEADS)
    own = lax.dynamic_index_in_dim(lengths.reshape(-1, lengths.shape[-1]), row, 0, keepdims=False)
    ends = jnp.cumsum(own)
    place = jnp.arange(tokens, dtype=jnp.int32)
    document = jnp.sum((place[None, :] >= ends[:, None]).astype(jnp.int32), axis=0)
    inside = jnp.arange(DOC_ROWS, dtype=jnp.int32)[:, None] == document[None, :]
    real = jnp.arange(DOC_ROWS, dtype=jnp.int32)[:, None] < lengths.shape[-1]
    of_query = jnp.where(inside, FAR, 0.0)
    of_key = jnp.where(real & ~inside, 1.0, 0.0)
    blocks = tokens // PART
    shape = (DOC_ROWS, blocks, PART)
    slope = jnp.exp2(-8.0 * (head + 1).astype(jnp.float32) / HEADS)
    return (
        (slope * LOG2E).reshape(1),
        of_query.reshape(shape).transpose(1, 0, 2).astype(jnp.bfloat16),
        of_key.reshape(shape).transpose(1, 0, 2).astype(jnp.bfloat16),
    )


def side_by_side(ref, tile, rows):
    return jnp.concatenate([ref[tile * PER + part, rows, :] for part in range(PER)], axis=1)


ROW_Q, ROW_K, ROW_V = slice(0, 64), slice(64, 128), slice(128, 192)


def rows_at(tile):
    return pl.ds(pl.multiple_of(tile * TILE, TILE), TILE)


def part_at(block):
    return pl.ds(pl.multiple_of(block * PART, PART), PART)


def fill_biases(slope_ref, bias_ref):
    key = lax.broadcasted_iota(jnp.int32, (TILE, TILE), 0)
    query = lax.broadcasted_iota(jnp.int32, (TILE, TILE), 1)

    def one(step, carry):
        distance = jnp.abs(key - query + (step - GUARD) * TILE)
        bias = distance.astype(jnp.float32) * -slope_ref[0]
        bias_ref[step] = jnp.where(distance < WINDOW, bias, FAR)
        return carry

    lax.fori_loop(0, REACH, one, 0)


def fill_guards(unit_ref, key_ref, blocks):
    rows = GUARD * TILE
    feature = lax.broadcasted_iota(jnp.int32, (rows, PART), 1)
    away = jnp.where((feature >= 64) & (feature < 72), 1.0, 0.0).astype(jnp.bfloat16)
    for first in (0, rows + blocks * PART):
        key_ref[pl.ds(first, rows), :] = away
    for first in (0, GUARD * PER + blocks):
        unit_ref[pl.ds(first, GUARD * PER)] = jnp.zeros(
            (GUARD * PER,) + unit_ref.shape[1:], unit_ref.dtype
        )


def fill_keys(unit_ref, doc_ref, key_ref, blocks):
    def one(block, carry):
        there = block + GUARD * PER
        features = jnp.concatenate([unit_ref[there, ROW_K, :], doc_ref[block]], axis=0)
        key_ref[part_at(there), :] = features.T
        return carry

    lax.fori_loop(0, blocks, one, 0, unroll=4)


class Service:
    def __init__(self, flow, first, tiles):
        self.turns = flow.turns()
        self.first = first
        self.after = {}
        left = max(len(self.turns) - first, 0)
        for index in range(left):
            self.after.setdefault(index * tiles // left, []).append(self.turns[first + index])

    def begin(self, done=0):
        for turn in self.turns[done : self.first]:
            turn()

    def at(self, tile):
        for index, turns in self.after.items():

            @pl.when(tile == index)
            def _(turns=turns):
                for turn in turns:
                    turn()


def attention_forward(packed, exchange, context, collective_id, flow, first):
    blocks, held = exchange.blocks, exchange.held
    tiles = blocks // PER
    edge = GUARD * PER

    count = len(flow.operands)

    def kernel(slope_ref, query_doc_ref, key_doc_ref, packed_ref, *refs):
        out_ref, keep_ref, wide_ref, sum_ref = refs[count : count + 4]
        flow.bind(refs[:count], refs[count + 4 : 2 * count + 4], refs[2 * count + 14 :])
        (
            unit_ref,
            key_ref,
            bias_ref,
            score_ref,
            result_ref,
            to_sem,
            at_sem,
            back_sem,
            home_sem,
            own_sem,
        ) = refs[2 * count + 4 : 2 * count + 14]
        service = Service(flow, first, tiles)
        has_unit = own_unit(exchange.sizes) < exchange.units
        exchange.greet_all()

        def units(wait, part=0, parts=1):
            exchange.to_units(
                lambda slot: packed_ref.at[slot],
                lambda spot: unit_ref.at[edge + spot],
                to_sem,
                at_sem,
                own_sem.at[0],
                wait,
                part,
                parts,
            )

        def tokens(spot, wait):
            exchange.to_token(
                spot,
                lambda spot: result_ref.at[spot],
                lambda slot: out_ref.at[slot],
                back_sem,
                home_sem,
                own_sem.at[1],
                wait,
            )

        keep = pltpu.make_async_copy(unit_ref.at[pl.ds(edge, blocks)], keep_ref, own_sem.at[2])
        flow.begin()
        parts = 3 if first > 2 else 1
        units(False, 0, parts)

        @pl.when(has_unit)
        def _():
            fill_biases(slope_ref, bias_ref)
            fill_guards(unit_ref, key_ref, blocks)

        for part in range(1, parts):
            service.turns[part - 1]()
            units(False, part, parts)
        service.begin(parts - 1)

        @pl.when(has_unit)
        def _():
            exchange.at_unit(lambda spot: unit_ref.at[edge + spot], at_sem, own_sem.at[0])
            keep.start()
            fill_keys(unit_ref, key_doc_ref, key_ref, blocks)

        def one_tile(tile, carry):
            @pl.when(has_unit)
            def _():
                q_t = jnp.concatenate(
                    [
                        side_by_side(unit_ref, tile + GUARD, ROW_Q),
                        side_by_side(query_doc_ref, tile, slice(0, DOC_ROWS)),
                    ],
                    axis=0,
                )
                top = jnp.full((1, TILE), FAR, jnp.float32)
                for step in range(REACH):
                    raw = jnp.dot(
                        key_ref[rows_at(tile + step), :], q_t, preferred_element_type=jnp.float32
                    )
                    score = raw * (HEAD_DIM ** (-0.5) * LOG2E) + bias_ref[step]
                    score_ref[step] = score
                    top = jnp.maximum(top, jnp.max(score, axis=0, keepdims=True))
                total = jnp.zeros((1, TILE), jnp.float32)
                attended = jnp.zeros((HEAD_DIM, TILE), jnp.float32)
                for step in range(REACH):
                    probs = jnp.exp2(score_ref[step] - top)
                    total = total + jnp.sum(probs, axis=0, keepdims=True)
                    attended = attended + jnp.dot(
                        side_by_side(unit_ref, tile + step, ROW_V),
                        probs.astype(jnp.bfloat16),
                        preferred_element_type=jnp.float32,
                    )
                result = attended / total
                sum_ref[tile] = top + jnp.log2(total)
                for part in range(PER):
                    piece = result[:, part * PART : (part + 1) * PART]
                    wide_ref[tile * PER + part] = piece
                    result_ref[tile * PER + part] = piece.astype(jnp.bfloat16)
                    tokens(tile * PER + part, False)

            service.at(tile)
            return carry

        lax.fori_loop(0, tiles, one_tile, 0)
        units(True)

        exchange.at_tokens(lambda slot: out_ref.at[slot], home_sem, own_sem.at[1])

        @pl.when(has_unit)
        def _():
            def sent(spot, carry):
                tokens(spot, True)
                return carry

            lax.fori_loop(0, blocks, sent, 0)
            keep.wait()

        flow.end()

    return pl.pallas_call(
        kernel,
        out_shape=[
            jax.ShapeDtypeStruct((held, HEAD_DIM, PART), jnp.bfloat16),
            jax.ShapeDtypeStruct((blocks, 3 * HEAD_DIM, PART), jnp.bfloat16),
            jax.ShapeDtypeStruct((blocks, HEAD_DIM, PART), jnp.float32),
            jax.ShapeDtypeStruct((tiles, 1, TILE), jnp.float32),
        ]
        + flow.out_shape,
        in_specs=[SMEM, VMEM, VMEM, HBM] + [HBM] * count,
        out_specs=[HBM, HBM, VMEM, VMEM] + flow.out_specs,
        scratch_shapes=[
            pltpu.VMEM((blocks + 2 * edge, 3 * HEAD_DIM, PART), jnp.bfloat16),
            pltpu.VMEM(((blocks + 2 * edge) * PART, PART), jnp.bfloat16),
            pltpu.VMEM((REACH, TILE, TILE), jnp.float32),
            pltpu.VMEM((REACH, TILE, TILE), jnp.float32),
            pltpu.VMEM((blocks, HEAD_DIM, PART), jnp.bfloat16),
            pltpu.SemaphoreType.DMA((held,)),
            pltpu.SemaphoreType.DMA((blocks,)),
            pltpu.SemaphoreType.DMA((blocks,)),
            pltpu.SemaphoreType.DMA((held,)),
            pltpu.SemaphoreType.DMA((3,)),
        ]
        + flow.scratch,
        compiler_params=pltpu.CompilerParams(
            collective_id=collective_id, has_side_effects=True, vmem_limit_bytes=48 << 20
        ),
        cost_estimate=cost_of(60),
        name="attention_forward",
    )(*context, packed, *flow.operands)


def attention_backward(grad, unit_kept, exchange, context, collective_id, flow, first):
    blocks, held = exchange.blocks, exchange.held
    tiles = blocks // PER
    edge = GUARD * PER

    count = len(flow.operands)

    def kernel(
        slope_ref, query_doc_ref, key_doc_ref, wide_ref, sum_ref, grad_ref, kept_ref, *refs
    ):
        out_ref = refs[count]
        flow.bind(refs[:count], refs[count + 1 : 2 * count + 1], refs[2 * count + 13 :])
        (
            unit_ref,
            got_ref,
            key_ref,
            value_ref,
            bias_ref,
            total_ref,
            result_ref,
            to_sem,
            at_sem,
            back_sem,
            home_sem,
            own_sem,
        ) = refs[2 * count + 1 : 2 * count + 13]
        service = Service(flow, first, tiles)
        has_unit = own_unit(exchange.sizes) < exchange.units
        exchange.greet_all()

        def units(wait):
            exchange.to_units(
                lambda slot: grad_ref.at[slot],
                lambda spot: got_ref.at[spot],
                to_sem,
                at_sem,
                own_sem.at[0],
                wait,
            )

        def tokens(spot, wait):
            exchange.to_token(
                spot,
                lambda spot: result_ref.at[spot],
                lambda slot: out_ref.at[slot],
                back_sem,
                home_sem,
                own_sem.at[1],
                wait,
            )

        load = pltpu.make_async_copy(kept_ref, unit_ref.at[pl.ds(edge, blocks)], own_sem.at[2])
        flow.begin()
        units(False)

        @pl.when(has_unit)
        def _():
            load.start()
            fill_biases(slope_ref, bias_ref)
            fill_guards(unit_ref, key_ref, blocks)
            for first in (0, (edge + blocks) * PART):
                value_ref[pl.ds(first, edge * PART), :] = jnp.zeros(
                    (edge * PART, PART), value_ref.dtype
                )
            total_ref[...] = jnp.zeros_like(total_ref)
            load.wait()
            fill_keys(unit_ref, key_doc_ref, key_ref, blocks)

            def one(block, carry):
                there = block + edge
                value_ref[part_at(there), :] = unit_ref[there, 64:192, :].T
                return carry

            lax.fori_loop(0, blocks, one, 0, unroll=4)

        service.begin()

        @pl.when(has_unit)
        def _():
            exchange.at_unit(lambda spot: got_ref.at[spot], at_sem, own_sem.at[0])

        def finish(tile):
            for part in range(PER):
                block = tile * PER + part
                result_ref[block, 64:192, :] = total_ref[part_at(block + edge), :].T.astype(
                    jnp.bfloat16
                )
                tokens(block, False)

        def one_tile(tile, carry):
            @pl.when(has_unit)
            def _():
                q_part = side_by_side(unit_ref, tile + GUARD, ROW_Q)
                g_part = side_by_side(got_ref, tile, slice(0, 64))
                q_t = jnp.concatenate(
                    [q_part, side_by_side(query_doc_ref, tile, slice(0, DOC_ROWS))], axis=0
                )
                g_small = g_part * jnp.asarray(HEAD_DIM ** (-0.5), jnp.bfloat16)
                g_t = jnp.concatenate([jnp.zeros_like(g_small), g_small], axis=0)
                turned = jnp.concatenate([q_part, g_part], axis=0).T
                lane = lax.broadcasted_iota(jnp.int32, turned.shape, 1)
                none = jnp.zeros_like(turned)
                q_and_g = jnp.concatenate(
                    [jnp.where(lane < 64, turned, none), jnp.where(lane < 64, none, turned)],
                    axis=0,
                )
                wide_t = side_by_side(wide_ref, tile, slice(0, 64))
                mean = jnp.sum(g_small.astype(jnp.float32) * wide_t, axis=0, keepdims=True)
                sum_now = sum_ref[tile]
                grad_q = jnp.zeros((HEAD_DIM, TILE), jnp.float32)
                for step in range(REACH):
                    there = rows_at(tile + step)
                    raw = jnp.dot(key_ref[there, :], q_t, preferred_element_type=jnp.float32)
                    grad_probs = jnp.dot(
                        value_ref[there, :], g_t, preferred_element_type=jnp.float32
                    )
                    score = raw * (HEAD_DIM ** (-0.5) * LOG2E) + bias_ref[step]
                    probs = jnp.exp2(score - sum_now)
                    grad_raw = (probs * (grad_probs - mean)).astype(jnp.bfloat16)
                    total_ref[there, :] += jnp.dot(
                        jnp.concatenate([grad_raw, probs.astype(jnp.bfloat16)], axis=1),
                        q_and_g,
                        preferred_element_type=jnp.float32,
                    )
                    grad_q = grad_q + jnp.dot(
                        side_by_side(unit_ref, tile + step, ROW_K),
                        grad_raw,
                        preferred_element_type=jnp.float32,
                    )
                for part in range(PER):
                    result_ref[tile * PER + part, ROW_Q, :] = grad_q[
                        :, part * PART : (part + 1) * PART
                    ].astype(jnp.bfloat16)

                @pl.when(tile >= GUARD)
                def _():
                    finish(tile - GUARD)

            service.at(tile)
            return carry

        lax.fori_loop(0, tiles, one_tile, 0)
        units(True)

        @pl.when(has_unit)
        def _():
            def rest(tile, carry):
                finish(tile)
                return carry

            lax.fori_loop(max(tiles - GUARD, 0), tiles, rest, 0)

        exchange.at_tokens(lambda slot: out_ref.at[slot], home_sem, own_sem.at[1])

        @pl.when(has_unit)
        def _():
            def sent(spot, carry):
                tokens(spot, True)
                return carry

            lax.fori_loop(0, blocks, sent, 0)

        flow.end()

    return pl.pallas_call(
        kernel,
        out_shape=[jax.ShapeDtypeStruct((held, 3 * HEAD_DIM, PART), jnp.bfloat16)] + flow.out_shape,
        in_specs=[SMEM, VMEM, VMEM, VMEM, VMEM, HBM, HBM] + [HBM] * count,
        out_specs=[HBM] + flow.out_specs,
        scratch_shapes=[
            pltpu.VMEM((blocks + 2 * edge, 3 * HEAD_DIM, PART), jnp.bfloat16),
            pltpu.VMEM((blocks, HEAD_DIM, PART), jnp.bfloat16),
            pltpu.VMEM(((blocks + 2 * edge) * PART, PART), jnp.bfloat16),
            pltpu.VMEM(((blocks + 2 * edge) * PART, PART), jnp.bfloat16),
            pltpu.VMEM((REACH, TILE, TILE), jnp.float32),
            pltpu.VMEM(((blocks + 2 * edge) * PART, PART), jnp.float32),
            pltpu.VMEM((blocks, 3 * HEAD_DIM, PART), jnp.bfloat16),
            pltpu.SemaphoreType.DMA((held,)),
            pltpu.SemaphoreType.DMA((blocks,)),
            pltpu.SemaphoreType.DMA((blocks,)),
            pltpu.SemaphoreType.DMA((held,)),
            pltpu.SemaphoreType.DMA((3,)),
        ]
        + flow.scratch,
        compiler_params=pltpu.CompilerParams(
            collective_id=collective_id, has_side_effects=True, vmem_limit_bytes=60 << 20
        ),
        cost_estimate=cost_of(70),
        name="attention_backward",
    )(*context, *unit_kept[1:], grad, unit_kept[0], *flow.operands)


def layer_norm(summed, gain, shift):
    centre = jnp.mean(summed, axis=-1, keepdims=True)
    centred = summed - centre
    variance = jnp.mean(centred * centred, axis=-1, keepdims=True)
    return centred * lax.rsqrt(variance + 1e-12) * gain + shift


def normal_share(gate):
    return 0.5 * lax.erf(gate * math.sqrt(0.5)) + 0.5


def geglu(gate, upper):
    return gate * normal_share(gate) * upper


def geglu_backward(gate, upper, grad):
    share = normal_share(gate)
    slope = share + gate * jnp.exp(-0.5 * gate * gate) * (1.0 / math.sqrt(2.0 * math.pi))
    return grad * upper * slope, grad * (gate * share)


def dot(a, b, a_axis, b_axis):
    return lax.dot_general(
        a, b, (((a_axis,), (b_axis,)), ((), ())), preferred_element_type=jnp.float32
    )


def layer_forward(hidden, qkv_w, others, kinds, shards, exchange, context, collective_id):
    batches = exchange.batches
    tokens = hidden.shape[0] // batches
    hidden_low = hidden.astype(jnp.bfloat16)
    if others:
        hidden_low = lax.optimization_barrier(hidden_low)
    packed = dot(qkv_w, hidden_low, 0, 1).astype(jnp.bfloat16)
    packed = packed.reshape(3, HEADS, HEAD_DIM, batches, tokens)
    packed = packed.transpose(3, 1, 0, 2, 4).reshape(batches * HEADS, 3 * HEAD_DIM, tokens)
    attended, unit_packed, wide, sums, *gathered = attention_forward(
        packed,
        exchange,
        context,
        collective_id,
        Gather(kinds, shards, exchange.sizes, FORWARD_AHEAD, FORWARD_LAG),
        FORWARD_FIRST if kinds else 0,
    )
    gathered = [one.reshape(-1, one.shape[-1]) for one in gathered]
    out_w, up_w, down_w = others + gathered
    norm_f = out_w[:, D : D + 4].astype(jnp.float32)
    out_w = out_w[:, :D]
    attn_t = attended.reshape(batches, D, tokens)
    attn_low = attn_t.transpose(0, 2, 1).reshape(batches * tokens, D)
    mixed = hidden + dot(attn_low, out_w, 1, 0)
    normed = layer_norm(mixed, norm_f[:, 0], norm_f[:, 1])
    normed_low = normed.astype(jnp.bfloat16)
    upper = dot(normed_low, up_w, 1, 0)
    act_low = geglu(upper[:, :FF], upper[:, FF:]).astype(jnp.bfloat16)
    second = normed + dot(act_low, down_w, 1, 0)
    result = layer_norm(second, norm_f[:, 2], norm_f[:, 3])
    weights = (qkv_w, out_w, up_w, down_w, norm_f)
    unit_kept = (unit_packed, wide, sums)
    kept = (hidden_low, unit_kept, attn_low, mixed, normed_low, upper, act_low, second)
    return result, weights, kept


def layer_backward(grad_result, weights, kept, exchange, context, collective_id):
    qkv_w, out_w, up_w, down_w, norm_f = weights
    hidden_low, unit_kept, attn_low, mixed, normed_low, upper, act_low, second = kept
    batches = exchange.batches
    tokens = grad_result.shape[0] // batches
    pull_two = jax.vjp(layer_norm, second, norm_f[:, 2], norm_f[:, 3])[1]
    grad_second, grad_gain_two, grad_shift_two = pull_two(grad_result)
    grad_branch = grad_second.astype(jnp.bfloat16)
    grad_act = dot(grad_branch, down_w, 1, 1)
    grad_gate, grad_upper = geglu_backward(upper[:, :FF], upper[:, FF:], grad_act)
    grad_up_low = jnp.concatenate([grad_gate, grad_upper], axis=1).astype(jnp.bfloat16)
    grad_normed = grad_second + dot(grad_up_low, up_w, 1, 1)
    pull_one = jax.vjp(layer_norm, mixed, norm_f[:, 0], norm_f[:, 1])[1]
    grad_mixed, grad_gain_one, grad_shift_one = pull_one(grad_normed)
    grad_attn = grad_mixed.astype(jnp.bfloat16)
    grad_heads = dot(out_w, grad_attn, 1, 1).astype(jnp.bfloat16)
    grad_heads = grad_heads.reshape(HEADS, HEAD_DIM, batches, tokens)
    grad_heads = grad_heads.transpose(2, 0, 1, 3).reshape(batches * HEADS, HEAD_DIM, tokens)
    grad_norm = jnp.stack([grad_gain_one, grad_shift_one, grad_gain_two, grad_shift_two], axis=1)
    grad_out_w = jnp.concatenate(
        [
            dot(attn_low, grad_attn, 0, 0).astype(jnp.bfloat16),
            jnp.pad(grad_norm.astype(jnp.bfloat16), ((0, 0), (0, NORM_PAD - 4))),
        ],
        axis=1,
    )
    grad_up_w = dot(normed_low, grad_up_low, 0, 0).astype(jnp.bfloat16)
    grad_down_w = dot(act_low, grad_branch, 0, 0).astype(jnp.bfloat16)
    flow = Scatter(
        ["down", "up", "out"],
        [grad_down_w, grad_up_w, grad_out_w],
        exchange.sizes,
        BACKWARD_AHEAD,
        BACKWARD_LAG,
    )
    packed_grad, *totals = attention_backward(
        grad_heads,
        unit_kept,
        exchange,
        context,
        collective_id,
        flow,
        BACKWARD_FIRST,
    )
    packed_grad = packed_grad.reshape(batches, HEADS, 3, HEAD_DIM, tokens)
    packed_grad = packed_grad.transpose(0, 4, 2, 1, 3).reshape(batches * tokens, 3 * D)
    grad_hidden = grad_mixed + dot(packed_grad, qkv_w, 1, 1)
    grad_qkv_w = dot(hidden_low, packed_grad, 0, 0).astype(jnp.bfloat16)
    return grad_hidden, grad_qkv_w, totals


def adamw(weight, first, second, grad, rate):
    first_new = beta_one * first + (1.0 - beta_one) * grad
    second_new = beta_two * second + (1.0 - beta_two) * grad * grad
    first_hat = first_new / (1.0 - beta_one**STEP)
    second_hat = second_new / (1.0 - beta_two**STEP)
    weight_new = weight - rate * (first_hat / (jnp.sqrt(second_hat) + adam_eps) + decay * weight)
    return (first_new, second_new, weight_new)


def body(
    inputs,
    cotangent,
    lengths,
    qkv_weight,
    qkv_first,
    qkv_second,
    out_weight,
    out_first,
    out_second,
    up_weight,
    up_first,
    up_second,
    down_weight,
    down_first,
    down_second,
    norm_params,
    norm_first,
    norm_second,
):
    masters = (qkv_weight, out_weight, up_weight, down_weight, norm_params)
    states = (
        (qkv_first, qkv_second),
        (out_first, out_second),
        (up_first, up_second),
        (down_first, down_second),
        (norm_first, norm_second),
    )
    sizes = grid_sizes(lax.axis_size("seq"))
    batches, tokens = inputs.shape[:2]
    exchange = Exchange(sizes, batches, lengths.shape[1])
    context = unit_context(lengths, exchange, exchange.blocks * tokens)
    norm_wide = jnp.pad(norm_params, ((0, 0), (0, 0), (0, NORM_PAD - 4)))
    sources = (qkv_weight, jnp.concatenate([out_weight, norm_wide], axis=2), up_weight, down_weight)
    shards = [[source[layer].astype(jnp.bfloat16) for source in sources] for layer in range(LAYERS)]
    qkv_w = run_flow(Gather(["qkv"], shards[0][:1], sizes, 2, 1), 0, "gather_weights")[0]
    qkv_w = qkv_w.reshape(-1, qkv_w.shape[-1])
    everyone = ("head", "seq")
    later = [lax.all_gather(shard, everyone, axis=0, tiled=True) for shard in shards[1]]

    hidden = inputs.reshape(batches * tokens, D).astype(jnp.float32)
    weights_all, kept_all = [], []
    for layer in range(LAYERS):
        hidden, weights, kept = layer_forward(
            hidden,
            later[0] if layer else qkv_w,
            later[1:] if layer else [],
            [] if layer else ["out", "up", "down"],
            [] if layer else shards[0][1:],
            exchange,
            context,
            1 + layer,
        )
        weights_all.append(weights)
        kept_all.append(kept)
    outputs = hidden.reshape(batches, tokens, D)
    grad_hidden = cotangent.reshape(batches * tokens, D).astype(jnp.float32)
    totals = [[None] * 4 for _ in range(LAYERS)]
    late = []
    for layer in reversed(range(LAYERS)):
        grad_hidden, grad_qkv_w, done = layer_backward(
            grad_hidden,
            weights_all[layer],
            kept_all[layer],
            exchange,
            context,
            1 + LAYERS + layer,
        )
        totals[layer][3], totals[layer][2], totals[layer][1] = done
        late.append(grad_qkv_w)
    last = Scatter(["qkv"] * LAYERS, late, sizes, 4, 2)
    totals[1][0], totals[0][0] = run_flow(last, 1 + 2 * LAYERS, "scatter_grads")
    input_grad = grad_hidden.reshape(batches, tokens, D)

    results = [outputs, input_grad]
    kinds = [
        jnp.stack([totals[layer][0] for layer in range(LAYERS)]),
        jnp.stack([totals[layer][1][:, :D] for layer in range(LAYERS)]),
        jnp.stack([totals[layer][2] for layer in range(LAYERS)]),
        jnp.stack([totals[layer][3] for layer in range(LAYERS)]),
        jnp.stack([totals[layer][1][:, D : D + 4] for layer in range(LAYERS)]),
    ]
    new_weights = []
    for kind in range(5):
        first_new, second_new, weight_new = adamw(
            masters[kind], states[kind][0], states[kind][1], kinds[kind], learn_rates[kind]
        )
        results += [kinds[kind], first_new, second_new, weight_new]
        new_weights.append(weight_new)
    results += [member.astype(jnp.bfloat16) for member in new_weights[:4]]
    return tuple(results)


def solution(mesh):
    tokens = P(None, ("seq", "head"), None)
    rows = P(None, ("head", "seq"), None)
    in_specs = (tokens, tokens, P()) + (rows,) * 15
    out_specs = (tokens, tokens) + (rows,) * 24
    return jax.shard_map(body, mesh=mesh, in_specs=in_specs, out_specs=out_specs, check_vma=False)
```

```python
import functools
import math

import jax
import jax.numpy as jnp
from jax import lax
from jax.experimental import pallas as pl
from jax.experimental.layout import Layout, with_layout_constraint
from jax.experimental.pallas import tpu as pltpu
from jax.sharding import PartitionSpec as P

D = 768
HEADS = 12
HEAD_DIM = 64
FF = 3072
LAYERS = 2
WINDOW = 1024
STEP = 10

beta_one = 0.5
beta_two = 0.5
adam_eps = 1e-08
decay = 0.1
learn_rates = (0.03, 0.15, 0.03, 0.02, 0.2)

MESH = pl.DeviceIdType.MESH
TILE = 256
LOG2E = math.log2(math.e)
NORM_PAD = 128

CORES = 2
AXES = ("x", "z", "y", "c")


def cost_of(microseconds):
    return pl.CostEstimate(flops=0, bytes_accessed=int(microseconds * 3.69e6), transcendentals=0)


def grid_sizes(seq_size):
    rows = 2 if seq_size <= 16 else 4
    return {"x": lax.axis_size("head"), "z": seq_size // (rows * CORES), "y": rows, "c": CORES}


def quotient(value, divisor, count):
    result = 0
    for step in range(1, count):
        result = result + jnp.where(value >= step * divisor, 1, 0)
    return result


def wrapped(value, size):
    return value - jnp.where(value >= size, size, 0)


def own_place(sizes):
    seq = lax.axis_index("seq")
    return {
        "x": lax.axis_index("head"),
        "z": lax.div(seq, sizes["y"] * sizes["c"]),
        "y": lax.rem(lax.div(seq, sizes["c"]), sizes["y"]),
        "c": lax.rem(seq, sizes["c"]),
    }


def device_of(place, sizes):
    seq = (place["z"] * sizes["y"] + place["y"]) * sizes["c"] + place["c"]
    return {"head": place["x"], "seq": seq}


def peer_at(place, axis, step, sizes):
    other = dict(place)
    other[axis] = lax.rem(place[axis] + step, sizes[axis])
    return other


def greet_axes(place, sizes):
    barrier = pltpu.get_barrier_semaphore()
    count = 0
    for axis in AXES:
        for step in range(1, sizes[axis]):
            pl.semaphore_signal(
                barrier,
                inc=1,
                device_id=device_of(peer_at(place, axis, step, sizes), sizes),
                device_id_type=MESH,
            )
            count += 1
    pl.semaphore_wait(barrier, count)


def region(place, full, window):
    return tuple(slice(None) if axis in full else place[axis] for axis in AXES) + window


ZXY = ("z", "x", "y")
ZYX = ("z", "y", "x")

def steps_of(kind, rows):
    def halves(first, second, start=0):
        return ((0, rows, start, first, ZXY), (0, rows, start + first, second, ZYX))

    if kind == "qkv":
        return [halves(384, 384, start) for start in range(0, 3 * D, 768)]
    if kind == "out":
        return [halves(384, 512)]
    if kind == "up":
        return [halves(384, 384, start) for start in range(0, 2 * FF, 768)]
    if rows % 32:
        return [halves(384, 384)]
    return [((row, 16, 0, D, ZXY), (row + 16, 16, 0, D, ZYX)) for row in range(0, rows, 32)]


HBM = pl.BlockSpec(memory_space=pl.ANY)
VMEM = pl.BlockSpec(memory_space=pltpu.VMEM)
SMEM = pl.BlockSpec(memory_space=pltpu.SMEM)


class Flow:
    def __init__(self, kinds, operands, sizes, ahead, lag):
        self.operands = list(operands)
        self.sizes = sizes
        self.ahead, self.lag = ahead, lag
        self.steps, self.pieces = [], []
        for array, kind in enumerate(kinds):
            for step in steps_of(kind, operands[array].shape[-2]):
                self.steps.append(range(len(self.pieces), len(self.pieces) + len(step)))
                self.pieces += [(array,) + piece for piece in step]
        most = sum(size - 1 for size in sizes.values())
        self.semaphores = [
            pltpu.SemaphoreType.DMA((len(self.pieces), most)),
            pltpu.SemaphoreType.DMA((len(self.pieces), most)),
            pltpu.SemaphoreType.DMA((len(self.pieces),)),
        ]

        if not self.pieces:
            self.ahead, self.semaphores = 0, []

    def bind(self, ins, outs, scratch):
        self.place = own_place(self.sizes)
        if self.pieces:
            self.ins, self.outs, self.buffers = ins, outs, scratch[:-3]
            self.send_sem, self.recv_sem, self.own_sem = scratch[-3:]

    def window(self, number):
        _, row, rows, column, columns, _ = self.pieces[number]
        return (pl.ds(row, rows), pl.ds(column, columns))

    def remote(self, number, axis, step, source, target):
        before = AXES[: AXES.index(axis)]
        slot = sum(self.sizes[one] - 1 for one in before) + step - 1
        return pltpu.make_async_remote_copy(
            src_ref=source,
            dst_ref=target,
            send_sem=self.send_sem.at[number, slot],
            recv_sem=self.recv_sem.at[number, slot],
            device_id=device_of(peer_at(self.place, axis, step, self.sizes), self.sizes),
            device_id_type=MESH,
        )

    def numbers(self, step):
        return self.steps[step] if 0 <= step < len(self.steps) else ()

    def start(self, step, phase):
        for number in self.numbers(step):
            if phase == 0:
                self.own_copy(number).start()
            for copy in self.copies(number, phase):
                copy.start()

    def begin(self):
        for step in range(self.ahead):
            self.start(step, 0)

    def arrive(self, step, phase):
        for number in self.numbers(step):
            if phase == 0:
                self.own_copy(number).wait()
            for copy in self.copies(number, phase):
                copy.wait_recv()
            self.take(number, phase)

    def turns(self):
        def turn(index):
            self.start(index + self.ahead, 0)
            for phase in (3, 2, 1, 0):
                self.arrive(index - self.lag * phase, phase)
                if phase < 3:
                    self.start(index - self.lag * phase, phase + 1)

        count = len(self.steps) + 3 * self.lag if self.steps else 0
        return [functools.partial(turn, index) for index in range(count)]

    def end(self):
        for number in range(len(self.pieces)):
            for phase in range(4):
                for copy in self.copies(number, phase):
                    copy.wait_send()


class Gather(Flow):
    def __init__(self, kinds, shards, sizes, ahead, lag):
        super().__init__(kinds, shards, sizes, ahead, lag)
        lead = tuple(sizes[axis] for axis in AXES)
        self.out_shape = [jax.ShapeDtypeStruct(lead + one.shape, one.dtype) for one in shards]
        self.out_specs = [HBM] * len(shards)
        self.scratch = self.semaphores

    def own_copy(self, number):
        array, window = self.pieces[number][0], self.window(number)
        return pltpu.make_async_copy(
            self.ins[array].at[window],
            self.outs[array].at[region(self.place, (), window)],
            self.own_sem.at[number],
        )

    def copies(self, number, phase):
        array, order, window = self.pieces[number][0], self.pieces[number][-1], self.window(number)
        axis = (order + ("c",))[phase]
        part = self.outs[array].at[region(self.place, order[:phase], window)]
        source = self.ins[array].at[window] if phase == 0 else part
        return [
            self.remote(number, axis, step, source, part) for step in range(1, self.sizes[axis])
        ]

    def take(self, number, phase):
        pass


class Scatter(Flow):
    def __init__(self, kinds, grads, sizes, ahead, lag):
        grads = [
            grad.reshape(tuple(sizes[axis] for axis in AXES) + (-1, grad.shape[-1]))
            for grad in grads
        ]
        super().__init__(kinds, grads, sizes, ahead, lag)
        self.out_shape = [jax.ShapeDtypeStruct(grad.shape[-2:], jnp.float32) for grad in grads]
        self.out_specs = [VMEM] * len(grads)
        self.scratch = []
        for _, _, rows, _, columns, order in self.pieces:

            def shape_of(full, rows=rows, columns=columns):
                return tuple(sizes[axis] for axis in AXES if axis in full) + (rows, columns)

            self.scratch += [pltpu.VMEM(shape_of(order), jnp.bfloat16)] * 2
            for phase in range(3):
                senders = sizes[order[2 - phase]] - 1
                self.scratch.append(
                    pltpu.VMEM((senders,) + shape_of(order[: 2 - phase]), jnp.bfloat16)
                )
        self.scratch += self.semaphores

    def own_copy(self, number):
        array = self.pieces[number][0]
        return pltpu.make_async_copy(
            self.ins[array].at[region(self.place, AXES[:3], self.window(number))],
            self.buffers[5 * number],
            self.own_sem.at[number],
        )

    def copies(self, number, phase):
        array, order = self.pieces[number][0], self.pieces[number][-1]
        axis = "c" if phase == 0 else order[3 - phase]
        found = []
        for step in range(1, self.sizes[axis]):
            peer = peer_at(self.place, axis, step, self.sizes)
            if phase == 0:
                source = self.ins[array].at[region(peer, AXES[:3], self.window(number))]
                target = self.buffers[5 * number + 1]
            else:
                full = order[: 3 - phase]
                where = tuple(slice(None) if one in full else peer[one] for one in AXES[:3])
                source = self.buffers[5 * number].at[where]
                target = self.buffers[5 * number + 1 + phase].at[step - 1]
            found.append(self.remote(number, axis, step, source, target))
        return found

    def take(self, number, phase):
        array, order = self.pieces[number][0], self.pieces[number][-1]
        total = self.buffers[5 * number]
        got = self.buffers[5 * number + 1 + phase]
        if phase == 0:
            total[...] = total[...] + got[...]
            return
        full = order[: 3 - phase]
        where = tuple(slice(None) if axis in full else self.place[axis] for axis in AXES[:3])
        value = total[where]
        senders = self.sizes[order[3 - phase]] - 1
        if phase == 3:
            value = value.astype(jnp.float32)
            for sender in range(senders):
                value = value + got[sender].astype(jnp.float32)
            self.outs[array][self.window(number)] = value
        else:
            for sender in range(senders):
                value = value + got[sender]
            total[where] = value


def run_flow(flow, collective_id, name):
    count = len(flow.operands)

    def kernel(*refs):
        flow.bind(refs[:count], refs[count : 2 * count], refs[2 * count :])
        greet_axes(flow.place, flow.sizes)
        flow.begin()
        for turn in flow.turns():
            turn()
        flow.end()

    return pl.pallas_call(
        kernel,
        out_shape=flow.out_shape,
        in_specs=[HBM] * count,
        out_specs=flow.out_specs,
        scratch_shapes=flow.scratch,
        compiler_params=pltpu.CompilerParams(
            collective_id=collective_id, has_side_effects=True, vmem_limit_bytes=40 << 20
        ),
        cost_estimate=cost_of(30),
        name=name,
    )(*flow.operands)


def unit_place(unit, sizes):
    chips = sizes["x"] * sizes["y"]
    inside = quotient(unit, sizes["z"], chips * sizes["c"])
    row = quotient(inside, sizes["x"], sizes["y"] * sizes["c"])
    core = quotient(inside, chips, sizes["c"])
    x = inside - row * sizes["x"]
    y = wrapped(row - core * sizes["y"] + x, sizes["y"])
    return {"x": x, "z": unit - inside * sizes["z"], "y": y, "c": core}


def own_unit(sizes):
    place = own_place(sizes)
    turned = lax.rem(place["y"] + sizes["y"] * sizes["x"] - place["x"], sizes["y"])
    inside = (place["c"] * sizes["y"] + turned) * sizes["x"] + place["x"]
    return inside * sizes["z"] + place["z"]


class Exchange:
    def __init__(self, sizes, batches, sequences):
        self.sizes = sizes
        self.batches = batches
        self.sequences = sequences
        self.heads = sizes["x"]
        self.devices = math.prod(sizes.values())
        self.units = batches * sequences * HEADS
        self.blocks = self.devices // sequences
        self.held = batches * HEADS
        assert self.units <= self.devices

    def my_block(self):
        return lax.axis_index("seq") * self.heads + lax.axis_index("head")

    def unit_for(self, slot, block):
        batch = quotient(slot, HEADS, self.batches)
        sequence = quotient(block, self.blocks, self.sequences)
        return (batch * self.sequences + sequence) * HEADS + slot - batch * HEADS

    def block_device(self, block):
        return {"head": lax.rem(block, self.heads), "seq": lax.div(block, self.heads)}

    def token_device(self, unit, slot):
        if self.sequences > 1:
            slot = slot + lax.rem(lax.div(unit, HEADS), self.sequences) * self.blocks
        return self.block_device(slot)

    def unit_device(self, slot, block):
        return device_of(unit_place(self.unit_for(slot, block), self.sizes), self.sizes)

    def slot_of(self, unit):
        batch = lax.div(unit, HEADS * self.sequences)
        return lax.min(batch * HEADS + lax.rem(unit, HEADS), self.held - 1)

    def is_me(self, device):
        return jnp.logical_and(
            device["head"] == lax.axis_index("head"), device["seq"] == lax.axis_index("seq")
        )

    def greet_all(self):
        barrier = pltpu.get_barrier_semaphore()

        def greet(step, carry):
            device = self.block_device(lax.rem(self.my_block() + step, self.devices))
            pl.semaphore_signal(barrier, inc=1, device_id=device, device_id_type=MESH)
            return carry

        lax.fori_loop(1, self.devices, greet, 0)
        pl.semaphore_wait(barrier, self.devices - 1)

    def send(self, source, target, send_sem, recv_sem, own_sem, device, wait):
        same = self.is_me(device)
        remote = pltpu.make_async_remote_copy(
            src_ref=source,
            dst_ref=target,
            send_sem=send_sem,
            recv_sem=recv_sem,
            device_id=device,
            device_id_type=MESH,
        )
        if not wait:
            pl.when(same)(pltpu.make_async_copy(source, target, own_sem).start)

        @pl.when(jnp.logical_not(same))
        def _():
            remote.wait_send() if wait else remote.start()

    def receive(self, target, recv_sem, own_sem, device):
        same = self.is_me(device)

        @pl.when(same)
        def _():
            pltpu.make_async_copy(target, target, own_sem).wait()

        @pl.when(jnp.logical_not(same))
        def _():
            pltpu.make_async_copy(target, target, recv_sem).wait()

    def to_units(self, source_at, target_at, send_sem, recv_sem, own_sem, wait, part=0, parts=1):
        block = self.my_block()
        spot = block - quotient(block, self.blocks, self.sequences) * self.blocks
        turned = lax.rem(block, self.held)

        def one(index, carry):
            slot = wrapped(index + turned, self.held)
            self.send(
                source_at(slot),
                target_at(spot),
                send_sem.at[index],
                recv_sem.at[spot],
                own_sem,
                self.unit_device(slot, block),
                wait,
            )
            return carry

        lax.fori_loop(part * self.held // parts, (part + 1) * self.held // parts, one, 0)

    def at_unit(self, target_at, recv_sem, own_sem):
        unit = own_unit(self.sizes)

        def one(spot, carry):
            self.receive(
                target_at(spot), recv_sem.at[spot], own_sem, self.token_device(unit, spot)
            )
            return carry

        lax.fori_loop(0, self.blocks, one, 0)

    def to_token(self, spot, source_at, target_at, send_sem, recv_sem, own_sem, wait):
        unit = own_unit(self.sizes)
        slot = self.slot_of(unit)
        self.send(
            source_at(spot),
            target_at(slot),
            send_sem.at[spot],
            recv_sem.at[slot],
            own_sem,
            self.token_device(unit, spot),
            wait,
        )

    def at_tokens(self, target_at, recv_sem, own_sem):
        block = self.my_block()

        def one(slot, carry):
            self.receive(
                target_at(slot), recv_sem.at[slot], own_sem, self.unit_device(slot, block)
            )
            return carry

        lax.fori_loop(0, self.held, one, 0)


PART = 128
PER = TILE // PART
GUARD = WINDOW // TILE
REACH = 2 * GUARD + 1
DOC_ROWS = 64
FAR = -1e30
FORWARD_AHEAD, FORWARD_FIRST, FORWARD_LAG = 4, 8, 2
BACKWARD_AHEAD, BACKWARD_FIRST, BACKWARD_LAG = 8, 5, 2


def unit_context(lengths, exchange, tokens):
    unit = own_unit(exchange.sizes)
    row = lax.min(lax.div(unit, HEADS), exchange.batches * exchange.sequences - 1)
    head = lax.rem(unit, HEADS)
    own = lax.dynamic_index_in_dim(lengths.reshape(-1, lengths.shape[-1]), row, 0, keepdims=False)
    ends = jnp.cumsum(own)
    place = jnp.arange(tokens, dtype=jnp.int32)
    document = jnp.sum((place[None, :] >= ends[:, None]).astype(jnp.int32), axis=0)
    inside = jnp.arange(DOC_ROWS, dtype=jnp.int32)[:, None] == document[None, :]
    real = jnp.arange(DOC_ROWS, dtype=jnp.int32)[:, None] < lengths.shape[-1]
    of_query = jnp.where(inside, FAR, 0.0)
    of_key = jnp.where(real & ~inside, 1.0, 0.0)
    blocks = tokens // PART
    shape = (DOC_ROWS, blocks, PART)
    slope = jnp.exp2(-8.0 * (head + 1).astype(jnp.float32) / HEADS)
    return (
        (slope * LOG2E).reshape(1),
        of_query.reshape(shape).transpose(1, 0, 2).astype(jnp.bfloat16),
        of_key.reshape(shape).transpose(1, 0, 2).astype(jnp.bfloat16),
    )


def side_by_side(ref, tile, rows):
    return jnp.concatenate([ref[tile * PER + part, rows, :] for part in range(PER)], axis=1)


ROW_Q, ROW_K, ROW_V = slice(0, 64), slice(64, 128), slice(128, 192)


def rows_at(tile):
    return pl.ds(pl.multiple_of(tile * TILE, TILE), TILE)


def part_at(block):
    return pl.ds(pl.multiple_of(block * PART, PART), PART)


def fill_biases(slope_ref, bias_ref):
    key = lax.broadcasted_iota(jnp.int32, (TILE, TILE), 0)
    query = lax.broadcasted_iota(jnp.int32, (TILE, TILE), 1)

    def one(step, carry):
        distance = jnp.abs(key - query + (step - GUARD) * TILE)
        bias = distance.astype(jnp.float32) * -slope_ref[0]
        bias_ref[step] = jnp.where(distance < WINDOW, bias, FAR)
        return carry

    lax.fori_loop(0, REACH, one, 0)


def fill_guards(unit_ref, key_ref, blocks):
    rows = GUARD * TILE
    feature = lax.broadcasted_iota(jnp.int32, (rows, PART), 1)
    away = jnp.where((feature >= 64) & (feature < 72), 1.0, 0.0).astype(jnp.bfloat16)
    for first in (0, rows + blocks * PART):
        key_ref[pl.ds(first, rows), :] = away
    for first in (0, GUARD * PER + blocks):
        unit_ref[pl.ds(first, GUARD * PER)] = jnp.zeros(
            (GUARD * PER,) + unit_ref.shape[1:], unit_ref.dtype
        )


def fill_keys(unit_ref, doc_ref, key_ref, blocks):
    def one(block, carry):
        there = block + GUARD * PER
        features = jnp.concatenate([unit_ref[there, ROW_K, :], doc_ref[block]], axis=0)
        key_ref[part_at(there), :] = features.T
        return carry

    lax.fori_loop(0, blocks, one, 0, unroll=4)


class Service:
    def __init__(self, flow, first, tiles):
        self.turns = flow.turns()
        self.first = first
        self.after = {}
        left = max(len(self.turns) - first, 0)
        for index in range(left):
            self.after.setdefault(index * tiles // left, []).append(self.turns[first + index])

    def begin(self, done=0):
        for turn in self.turns[done : self.first]:
            turn()

    def at(self, tile):
        for index, turns in self.after.items():

            @pl.when(tile == index)
            def _(turns=turns):
                for turn in turns:
                    turn()


def attention_forward(packed, exchange, context, collective_id, flow, first):
    blocks, held = exchange.blocks, exchange.held
    tiles = blocks // PER
    edge = GUARD * PER

    count = len(flow.operands)

    def kernel(slope_ref, query_doc_ref, key_doc_ref, packed_ref, *refs):
        out_ref, keep_ref, wide_ref, sum_ref = refs[count : count + 4]
        flow.bind(refs[:count], refs[count + 4 : 2 * count + 4], refs[2 * count + 14 :])
        (
            unit_ref,
            key_ref,
            bias_ref,
            score_ref,
            result_ref,
            to_sem,
            at_sem,
            back_sem,
            home_sem,
            own_sem,
        ) = refs[2 * count + 4 : 2 * count + 14]
        service = Service(flow, first, tiles)
        has_unit = own_unit(exchange.sizes) < exchange.units
        exchange.greet_all()

        def units(wait, part=0, parts=1):
            exchange.to_units(
                lambda slot: packed_ref.at[slot],
                lambda spot: unit_ref.at[edge + spot],
                to_sem,
                at_sem,
                own_sem.at[0],
                wait,
                part,
                parts,
            )

        def tokens(spot, wait):
            exchange.to_token(
                spot,
                lambda spot: result_ref.at[spot],
                lambda slot: out_ref.at[slot],
                back_sem,
                home_sem,
                own_sem.at[1],
                wait,
            )

        keep = pltpu.make_async_copy(unit_ref.at[pl.ds(edge, blocks)], keep_ref, own_sem.at[2])
        flow.begin()
        parts = 3 if first > 2 else 1
        units(False, 0, parts)

        @pl.when(has_unit)
        def _():
            fill_biases(slope_ref, bias_ref)
            fill_guards(unit_ref, key_ref, blocks)

        for part in range(1, parts):
            service.turns[part - 1]()
            units(False, part, parts)
        service.begin(parts - 1)

        @pl.when(has_unit)
        def _():
            exchange.at_unit(lambda spot: unit_ref.at[edge + spot], at_sem, own_sem.at[0])
            keep.start()
            fill_keys(unit_ref, key_doc_ref, key_ref, blocks)

        def one_tile(tile, carry):
            @pl.when(has_unit)
            def _():
                q_t = jnp.concatenate(
                    [
                        side_by_side(unit_ref, tile + GUARD, ROW_Q),
                        side_by_side(query_doc_ref, tile, slice(0, DOC_ROWS)),
                    ],
                    axis=0,
                )
                top = jnp.full((1, TILE), FAR, jnp.float32)
                for step in range(REACH):
                    raw = jnp.dot(
                        key_ref[rows_at(tile + step), :], q_t, preferred_element_type=jnp.float32
                    )
                    score = raw * (HEAD_DIM ** (-0.5) * LOG2E) + bias_ref[step]
                    score_ref[step] = score
                    top = jnp.maximum(top, jnp.max(score, axis=0, keepdims=True))
                total = jnp.zeros((1, TILE), jnp.float32)
                attended = jnp.zeros((HEAD_DIM, TILE), jnp.float32)
                for step in range(REACH):
                    probs = jnp.exp2(score_ref[step] - top)
                    total = total + jnp.sum(probs, axis=0, keepdims=True)
                    attended = attended + jnp.dot(
                        side_by_side(unit_ref, tile + step, ROW_V),
                        probs.astype(jnp.bfloat16),
                        preferred_element_type=jnp.float32,
                    )
                result = attended / total
                sum_ref[tile] = top + jnp.log2(total)
                for part in range(PER):
                    piece = result[:, part * PART : (part + 1) * PART]
                    wide_ref[tile * PER + part] = piece
                    result_ref[tile * PER + part] = piece.astype(jnp.bfloat16)
                    tokens(tile * PER + part, False)

            service.at(tile)
            return carry

        lax.fori_loop(0, tiles, one_tile, 0)
        units(True)

        exchange.at_tokens(lambda slot: out_ref.at[slot], home_sem, own_sem.at[1])

        @pl.when(has_unit)
        def _():
            def sent(spot, carry):
                tokens(spot, True)
                return carry

            lax.fori_loop(0, blocks, sent, 0)
            keep.wait()

        flow.end()

    return pl.pallas_call(
        kernel,
        out_shape=[
            jax.ShapeDtypeStruct((held, HEAD_DIM, PART), jnp.bfloat16),
            jax.ShapeDtypeStruct((blocks, 3 * HEAD_DIM, PART), jnp.bfloat16),
            jax.ShapeDtypeStruct((blocks, HEAD_DIM, PART), jnp.float32),
            jax.ShapeDtypeStruct((tiles, 1, TILE), jnp.float32),
        ]
        + flow.out_shape,
        in_specs=[SMEM, VMEM, VMEM, HBM] + [HBM] * count,
        out_specs=[HBM, HBM, VMEM, VMEM] + flow.out_specs,
        scratch_shapes=[
            pltpu.VMEM((blocks + 2 * edge, 3 * HEAD_DIM, PART), jnp.bfloat16),
            pltpu.VMEM(((blocks + 2 * edge) * PART, PART), jnp.bfloat16),
            pltpu.VMEM((REACH, TILE, TILE), jnp.float32),
            pltpu.VMEM((REACH, TILE, TILE), jnp.float32),
            pltpu.VMEM((blocks, HEAD_DIM, PART), jnp.bfloat16),
            pltpu.SemaphoreType.DMA((held,)),
            pltpu.SemaphoreType.DMA((blocks,)),
            pltpu.SemaphoreType.DMA((blocks,)),
            pltpu.SemaphoreType.DMA((held,)),
            pltpu.SemaphoreType.DMA((3,)),
        ]
        + flow.scratch,
        compiler_params=pltpu.CompilerParams(
            collective_id=collective_id, has_side_effects=True, vmem_limit_bytes=48 << 20
        ),
        cost_estimate=cost_of(60),
        name="attention_forward",
    )(*context, packed, *flow.operands)


def attention_backward(grad, unit_kept, exchange, context, collective_id, flow, first):
    blocks, held = exchange.blocks, exchange.held
    tiles = blocks // PER
    edge = GUARD * PER

    count = len(flow.operands)

    def kernel(
        slope_ref, query_doc_ref, key_doc_ref, wide_ref, sum_ref, grad_ref, kept_ref, *refs
    ):
        out_ref = refs[count]
        flow.bind(refs[:count], refs[count + 1 : 2 * count + 1], refs[2 * count + 13 :])
        (
            unit_ref,
            got_ref,
            key_ref,
            value_ref,
            bias_ref,
            total_ref,
            result_ref,
            to_sem,
            at_sem,
            back_sem,
            home_sem,
            own_sem,
        ) = refs[2 * count + 1 : 2 * count + 13]
        service = Service(flow, first, tiles)
        has_unit = own_unit(exchange.sizes) < exchange.units
        exchange.greet_all()

        def units(wait):
            exchange.to_units(
                lambda slot: grad_ref.at[slot],
                lambda spot: got_ref.at[spot],
                to_sem,
                at_sem,
                own_sem.at[0],
                wait,
            )

        def tokens(spot, wait):
            exchange.to_token(
                spot,
                lambda spot: result_ref.at[spot],
                lambda slot: out_ref.at[slot],
                back_sem,
                home_sem,
                own_sem.at[1],
                wait,
            )

        load = pltpu.make_async_copy(kept_ref, unit_ref.at[pl.ds(edge, blocks)], own_sem.at[2])
        flow.begin()
        units(False)

        @pl.when(has_unit)
        def _():
            load.start()
            fill_biases(slope_ref, bias_ref)
            fill_guards(unit_ref, key_ref, blocks)
            for first in (0, (edge + blocks) * PART):
                value_ref[pl.ds(first, edge * PART), :] = jnp.zeros(
                    (edge * PART, PART), value_ref.dtype
                )
            total_ref[...] = jnp.zeros_like(total_ref)
            load.wait()
            fill_keys(unit_ref, key_doc_ref, key_ref, blocks)

            def one(block, carry):
                there = block + edge
                value_ref[part_at(there), :] = unit_ref[there, 64:192, :].T
                return carry

            lax.fori_loop(0, blocks, one, 0, unroll=4)

        service.begin()

        @pl.when(has_unit)
        def _():
            exchange.at_unit(lambda spot: got_ref.at[spot], at_sem, own_sem.at[0])

        def finish(tile):
            for part in range(PER):
                block = tile * PER + part
                result_ref[block, 64:192, :] = total_ref[part_at(block + edge), :].T.astype(
                    jnp.bfloat16
                )
                tokens(block, False)

        def one_tile(tile, carry):
            @pl.when(has_unit)
            def _():
                q_part = side_by_side(unit_ref, tile + GUARD, ROW_Q)
                g_part = side_by_side(got_ref, tile, slice(0, 64))
                q_t = jnp.concatenate(
                    [q_part, side_by_side(query_doc_ref, tile, slice(0, DOC_ROWS))], axis=0
                )
                g_small = g_part * jnp.asarray(HEAD_DIM ** (-0.5), jnp.bfloat16)
                g_t = jnp.concatenate([jnp.zeros_like(g_small), g_small], axis=0)
                turned = jnp.concatenate([q_part, g_part], axis=0).T
                lane = lax.broadcasted_iota(jnp.int32, turned.shape, 1)
                none = jnp.zeros_like(turned)
                q_and_g = jnp.concatenate(
                    [jnp.where(lane < 64, turned, none), jnp.where(lane < 64, none, turned)],
                    axis=0,
                )
                wide_t = side_by_side(wide_ref, tile, slice(0, 64))
                mean = jnp.sum(g_small.astype(jnp.float32) * wide_t, axis=0, keepdims=True)
                sum_now = sum_ref[tile]
                grad_q = jnp.zeros((HEAD_DIM, TILE), jnp.float32)
                for step in range(REACH):
                    there = rows_at(tile + step)
                    raw = jnp.dot(key_ref[there, :], q_t, preferred_element_type=jnp.float32)
                    grad_probs = jnp.dot(
                        value_ref[there, :], g_t, preferred_element_type=jnp.float32
                    )
                    score = raw * (HEAD_DIM ** (-0.5) * LOG2E) + bias_ref[step]
                    probs = jnp.exp2(score - sum_now)
                    grad_raw = (probs * (grad_probs - mean)).astype(jnp.bfloat16)
                    total_ref[there, :] += jnp.dot(
                        jnp.concatenate([grad_raw, probs.astype(jnp.bfloat16)], axis=1),
                        q_and_g,
                        preferred_element_type=jnp.float32,
                    )
                    grad_q = grad_q + jnp.dot(
                        side_by_side(unit_ref, tile + step, ROW_K),
                        grad_raw,
                        preferred_element_type=jnp.float32,
                    )
                for part in range(PER):
                    result_ref[tile * PER + part, ROW_Q, :] = grad_q[
                        :, part * PART : (part + 1) * PART
                    ].astype(jnp.bfloat16)

                @pl.when(tile >= GUARD)
                def _():
                    finish(tile - GUARD)

            service.at(tile)
            return carry

        lax.fori_loop(0, tiles, one_tile, 0)
        units(True)

        @pl.when(has_unit)
        def _():
            def rest(tile, carry):
                finish(tile)
                return carry

            lax.fori_loop(max(tiles - GUARD, 0), tiles, rest, 0)

        exchange.at_tokens(lambda slot: out_ref.at[slot], home_sem, own_sem.at[1])

        @pl.when(has_unit)
        def _():
            def sent(spot, carry):
                tokens(spot, True)
                return carry

            lax.fori_loop(0, blocks, sent, 0)

        flow.end()

    return pl.pallas_call(
        kernel,
        out_shape=[jax.ShapeDtypeStruct((held, 3 * HEAD_DIM, PART), jnp.bfloat16)] + flow.out_shape,
        in_specs=[SMEM, VMEM, VMEM, VMEM, VMEM, HBM, HBM] + [HBM] * count,
        out_specs=[HBM] + flow.out_specs,
        scratch_shapes=[
            pltpu.VMEM((blocks + 2 * edge, 3 * HEAD_DIM, PART), jnp.bfloat16),
            pltpu.VMEM((blocks, HEAD_DIM, PART), jnp.bfloat16),
            pltpu.VMEM(((blocks + 2 * edge) * PART, PART), jnp.bfloat16),
            pltpu.VMEM(((blocks + 2 * edge) * PART, PART), jnp.bfloat16),
            pltpu.VMEM((REACH, TILE, TILE), jnp.float32),
            pltpu.VMEM(((blocks + 2 * edge) * PART, PART), jnp.float32),
            pltpu.VMEM((blocks, 3 * HEAD_DIM, PART), jnp.bfloat16),
            pltpu.SemaphoreType.DMA((held,)),
            pltpu.SemaphoreType.DMA((blocks,)),
            pltpu.SemaphoreType.DMA((blocks,)),
            pltpu.SemaphoreType.DMA((held,)),
            pltpu.SemaphoreType.DMA((3,)),
        ]
        + flow.scratch,
        compiler_params=pltpu.CompilerParams(
            collective_id=collective_id, has_side_effects=True, vmem_limit_bytes=60 << 20
        ),
        cost_estimate=cost_of(70),
        name="attention_backward",
    )(*context, *unit_kept[1:], grad, unit_kept[0], *flow.operands)


def layer_norm(summed, gain, shift):
    centre = jnp.mean(summed, axis=-1, keepdims=True)
    centred = summed - centre
    variance = jnp.mean(centred * centred, axis=-1, keepdims=True)
    return centred * lax.rsqrt(variance + 1e-12) * gain + shift


def normal_share(gate):
    return 0.5 * lax.erf(gate * math.sqrt(0.5)) + 0.5


def geglu(gate, upper):
    return gate * normal_share(gate) * upper


def geglu_backward(gate, upper, grad):
    share = normal_share(gate)
    slope = share + gate * jnp.exp(-0.5 * gate * gate) * (1.0 / math.sqrt(2.0 * math.pi))
    return grad * upper * slope, grad * (gate * share)


def dot(a, b, a_axis, b_axis):
    return lax.dot_general(
        a, b, (((a_axis,), (b_axis,)), ((), ())), preferred_element_type=jnp.float32
    )


def layer_forward(hidden, qkv_w, others, kinds, shards, exchange, context, collective_id):
    batches = exchange.batches
    tokens = hidden.shape[0] // batches
    hidden_low = hidden.astype(jnp.bfloat16)
    packed = dot(qkv_w, hidden_low, 0, 1).astype(jnp.bfloat16)
    packed = with_layout_constraint(packed, Layout((0, 1)))
    packed = packed.reshape(3, HEADS, HEAD_DIM, batches, tokens)
    packed = packed.transpose(3, 1, 0, 2, 4).reshape(batches * HEADS, 3 * HEAD_DIM, tokens)
    attended, unit_packed, wide, sums, *gathered = attention_forward(
        packed,
        exchange,
        context,
        collective_id,
        Gather(kinds, shards, exchange.sizes, FORWARD_AHEAD, FORWARD_LAG),
        FORWARD_FIRST if kinds else 0,
    )
    gathered = [one.reshape(-1, one.shape[-1]) for one in gathered]
    out_w, up_w, down_w = others + gathered
    norm_f = out_w[:, D : D + 4].astype(jnp.float32)
    out_w = out_w[:, :D]
    attn_t = attended.reshape(batches, D, tokens)
    attn_low = attn_t.transpose(0, 2, 1).reshape(batches * tokens, D)
    mixed = hidden + dot(attn_low, out_w, 1, 0)
    normed = layer_norm(mixed, norm_f[:, 0], norm_f[:, 1])
    normed_low = normed.astype(jnp.bfloat16)
    upper = dot(normed_low, up_w, 1, 0)
    act_low = geglu(upper[:, :FF], upper[:, FF:]).astype(jnp.bfloat16)
    second = normed + dot(act_low, down_w, 1, 0)
    result = layer_norm(second, norm_f[:, 2], norm_f[:, 3])
    weights = (qkv_w, out_w, up_w, down_w, norm_f)
    unit_kept = (unit_packed, wide, sums)
    kept = (hidden_low, unit_kept, attn_low, mixed, normed_low, upper, act_low, second)
    return result, weights, kept


def layer_backward(grad_result, weights, kept, exchange, context, collective_id):
    qkv_w, out_w, up_w, down_w, norm_f = weights
    hidden_low, unit_kept, attn_low, mixed, normed_low, upper, act_low, second = kept
    batches = exchange.batches
    tokens = grad_result.shape[0] // batches
    pull_two = jax.vjp(layer_norm, second, norm_f[:, 2], norm_f[:, 3])[1]
    grad_second, grad_gain_two, grad_shift_two = pull_two(grad_result)
    grad_branch = grad_second.astype(jnp.bfloat16)
    grad_act = dot(grad_branch, down_w, 1, 1)
    grad_gate, grad_upper = geglu_backward(upper[:, :FF], upper[:, FF:], grad_act)
    grad_up_low = jnp.concatenate([grad_gate, grad_upper], axis=1).astype(jnp.bfloat16)
    grad_normed = grad_second + dot(grad_up_low, up_w, 1, 1)
    pull_one = jax.vjp(layer_norm, mixed, norm_f[:, 0], norm_f[:, 1])[1]
    grad_mixed, grad_gain_one, grad_shift_one = pull_one(grad_normed)
    grad_attn = grad_mixed.astype(jnp.bfloat16)
    grad_heads = dot(out_w, grad_attn, 1, 1).astype(jnp.bfloat16)
    grad_heads = grad_heads.reshape(HEADS, HEAD_DIM, batches, tokens)
    grad_heads = grad_heads.transpose(2, 0, 1, 3).reshape(batches * HEADS, HEAD_DIM, tokens)
    grad_norm = jnp.stack([grad_gain_one, grad_shift_one, grad_gain_two, grad_shift_two], axis=1)
    grad_out_w = jnp.concatenate(
        [
            dot(attn_low, grad_attn, 0, 0).astype(jnp.bfloat16),
            jnp.pad(grad_norm.astype(jnp.bfloat16), ((0, 0), (0, NORM_PAD - 4))),
        ],
        axis=1,
    )
    grad_up_w = dot(normed_low, grad_up_low, 0, 0).astype(jnp.bfloat16)
    grad_down_w = dot(act_low, grad_branch, 0, 0).astype(jnp.bfloat16)
    flow = Scatter(
        ["down", "up", "out"],
        [grad_down_w, grad_up_w, grad_out_w],
        exchange.sizes,
        BACKWARD_AHEAD,
        BACKWARD_LAG,
    )
    packed_grad, *totals = attention_backward(
        grad_heads,
        unit_kept,
        exchange,
        context,
        collective_id,
        flow,
        BACKWARD_FIRST,
    )
    packed_grad = packed_grad.reshape(batches, HEADS, 3, HEAD_DIM, tokens)
    packed_grad = packed_grad.transpose(0, 4, 2, 1, 3).reshape(batches * tokens, 3 * D)
    grad_hidden = grad_mixed + dot(packed_grad, qkv_w, 1, 1)
    grad_qkv_w = dot(hidden_low, packed_grad, 0, 0).astype(jnp.bfloat16)
    return grad_hidden, grad_qkv_w, totals


def adamw(weight, first, second, grad, rate):
    first_new = beta_one * first + (1.0 - beta_one) * grad
    second_new = beta_two * second + (1.0 - beta_two) * grad * grad
    first_hat = first_new / (1.0 - beta_one**STEP)
    second_hat = second_new / (1.0 - beta_two**STEP)
    weight_new = weight - rate * (first_hat / (jnp.sqrt(second_hat) + adam_eps) + decay * weight)
    return (first_new, second_new, weight_new)


def body(
    inputs,
    cotangent,
    lengths,
    qkv_weight,
    qkv_first,
    qkv_second,
    out_weight,
    out_first,
    out_second,
    up_weight,
    up_first,
    up_second,
    down_weight,
    down_first,
    down_second,
    norm_params,
    norm_first,
    norm_second,
):
    masters = (qkv_weight, out_weight, up_weight, down_weight, norm_params)
    states = (
        (qkv_first, qkv_second),
        (out_first, out_second),
        (up_first, up_second),
        (down_first, down_second),
        (norm_first, norm_second),
    )
    sizes = grid_sizes(lax.axis_size("seq"))
    batches, tokens = inputs.shape[:2]
    exchange = Exchange(sizes, batches, lengths.shape[1])
    context = unit_context(lengths, exchange, exchange.blocks * tokens)
    norm_wide = jnp.pad(norm_params, ((0, 0), (0, 0), (0, NORM_PAD - 4)))
    sources = (qkv_weight, jnp.concatenate([out_weight, norm_wide], axis=2), up_weight, down_weight)
    shards = [[source[layer].astype(jnp.bfloat16) for source in sources] for layer in range(LAYERS)]
    qkv_w = run_flow(Gather(["qkv"], shards[0][:1], sizes, 2, 1), 0, "gather_weights")[0]
    qkv_w = qkv_w.reshape(-1, qkv_w.shape[-1])
    everyone = ("head", "seq")
    later = [jnp.concatenate(shards[1][:2], axis=1)] + shards[1][2:]
    later = [lax.all_gather(shard, everyone, axis=0, tiled=True) for shard in later]
    later = [later[0][:, : 3 * D], later[0][:, 3 * D :]] + later[1:]

    hidden = inputs.reshape(batches * tokens, D).astype(jnp.float32)
    weights_all, kept_all = [], []
    for layer in range(LAYERS):
        hidden, weights, kept = layer_forward(
            hidden,
            later[0] if layer else qkv_w,
            later[1:] if layer else [],
            [] if layer else ["out", "up", "down"],
            [] if layer else shards[0][1:],
            exchange,
            context,
            1 + layer,
        )
        weights_all.append(weights)
        kept_all.append(kept)
    outputs = hidden.reshape(batches, tokens, D)
    grad_hidden = cotangent.reshape(batches * tokens, D).astype(jnp.float32)
    totals = [[None] * 4 for _ in range(LAYERS)]
    late = []
    for layer in reversed(range(LAYERS)):
        grad_hidden, grad_qkv_w, done = layer_backward(
            grad_hidden,
            weights_all[layer],
            kept_all[layer],
            exchange,
            context,
            1 + LAYERS + layer,
        )
        totals[layer][3], totals[layer][2], totals[layer][1] = done
        late.append(grad_qkv_w)
    last = Scatter(["qkv"] * LAYERS, late, sizes, 6, 2)
    totals[1][0], totals[0][0] = run_flow(last, 1 + 2 * LAYERS, "scatter_grads")
    input_grad = grad_hidden.reshape(batches, tokens, D)

    results = [outputs, input_grad]
    kinds = [
        jnp.stack([totals[layer][0] for layer in range(LAYERS)]),
        jnp.stack([totals[layer][1][:, :D] for layer in range(LAYERS)]),
        jnp.stack([totals[layer][2] for layer in range(LAYERS)]),
        jnp.stack([totals[layer][3] for layer in range(LAYERS)]),
        jnp.stack([totals[layer][1][:, D : D + 4] for layer in range(LAYERS)]),
    ]
    new_weights = []
    for kind in range(5):
        first_new, second_new, weight_new = adamw(
            masters[kind], states[kind][0], states[kind][1], kinds[kind], learn_rates[kind]
        )
        results += [kinds[kind], first_new, second_new, weight_new]
        new_weights.append(weight_new)
    results += [member.astype(jnp.bfloat16) for member in new_weights[:4]]
    return tuple(results)


def solution(mesh):
    tokens = P(None, ("seq", "head"), None)
    rows = P(None, ("head", "seq"), None)
    in_specs = (tokens, tokens, P()) + (rows,) * 15
    out_specs = (tokens, tokens) + (rows,) * 24
    return jax.shard_map(body, mesh=mesh, in_specs=in_specs, out_specs=out_specs, check_vma=False)
```

```python
import functools
import math

import jax
import jax.numpy as jnp
from jax import lax
from jax.experimental import pallas as pl
from jax.experimental.layout import Layout, with_layout_constraint
from jax.experimental.pallas import tpu as pltpu
from jax.sharding import PartitionSpec as P

D = 768
HEADS = 12
HEAD_DIM = 64
FF = 3072
LAYERS = 2
WINDOW = 1024
STEP = 10

beta_one = 0.5
beta_two = 0.5
adam_eps = 1e-08
decay = 0.1
learn_rates = (0.03, 0.15, 0.03, 0.02, 0.2)

MESH = pl.DeviceIdType.MESH
TILE = 256
LOG2E = math.log2(math.e)
NORM_PAD = 128

CORES = 2
AXES = ("x", "z", "y", "c")


def cost_of(microseconds):
    return pl.CostEstimate(flops=0, bytes_accessed=int(microseconds * 3.69e6), transcendentals=0)


def grid_sizes(seq_size):
    rows = 2 if seq_size <= 16 else 4
    return {"x": lax.axis_size("head"), "z": seq_size // (rows * CORES), "y": rows, "c": CORES}


def quotient(value, divisor, count):
    result = 0
    for step in range(1, count):
        result = result + jnp.where(value >= step * divisor, 1, 0)
    return result


def wrapped(value, size):
    return value - jnp.where(value >= size, size, 0)


def own_place(sizes):
    seq = lax.axis_index("seq")
    return {
        "x": lax.axis_index("head"),
        "z": lax.div(seq, sizes["y"] * sizes["c"]),
        "y": lax.rem(lax.div(seq, sizes["c"]), sizes["y"]),
        "c": lax.rem(seq, sizes["c"]),
    }


def device_of(place, sizes):
    seq = (place["z"] * sizes["y"] + place["y"]) * sizes["c"] + place["c"]
    return {"head": place["x"], "seq": seq}


def peer_at(place, axis, step, sizes):
    other = dict(place)
    other[axis] = lax.rem(place[axis] + step, sizes[axis])
    return other


def greet_axes(place, sizes):
    barrier = pltpu.get_barrier_semaphore()
    count = 0
    for axis in AXES:
        for step in range(1, sizes[axis]):
            pl.semaphore_signal(
                barrier,
                inc=1,
                device_id=device_of(peer_at(place, axis, step, sizes), sizes),
                device_id_type=MESH,
            )
            count += 1
    pl.semaphore_wait(barrier, count)


def region(place, full, window):
    return tuple(slice(None) if axis in full else place[axis] for axis in AXES) + window


ZXY = ("z", "x", "y")
ZYX = ("z", "y", "x")

def steps_of(kind, rows):
    def halves(first, second, start=0):
        return ((0, rows, start, first, ZXY), (0, rows, start + first, second, ZYX))

    if kind == "qkv":
        return [halves(384, 384, start) for start in range(0, 3 * D, 768)]
    if kind == "out":
        return [halves(384, 512)]
    if kind == "up":
        return [halves(384, 384, start) for start in range(0, 2 * FF, 768)]
    if rows % 32:
        return [halves(384, 384)]
    return [((row, 16, 0, D, ZXY), (row + 16, 16, 0, D, ZYX)) for row in range(0, rows, 32)]


HBM = pl.BlockSpec(memory_space=pl.ANY)
VMEM = pl.BlockSpec(memory_space=pltpu.VMEM)
SMEM = pl.BlockSpec(memory_space=pltpu.SMEM)


class Flow:
    def __init__(self, kinds, operands, sizes, ahead, lag):
        self.operands = list(operands)
        self.sizes = sizes
        self.ahead, self.lag = ahead, lag
        self.steps, self.pieces = [], []
        for array, kind in enumerate(kinds):
            for step in steps_of(kind, operands[array].shape[-2]):
                self.steps.append(range(len(self.pieces), len(self.pieces) + len(step)))
                self.pieces += [(array,) + piece for piece in step]
        most = sum(size - 1 for size in sizes.values())
        self.semaphores = [
            pltpu.SemaphoreType.DMA((len(self.pieces), most)),
            pltpu.SemaphoreType.DMA((len(self.pieces), most)),
            pltpu.SemaphoreType.DMA((len(self.pieces),)),
        ]

        if not self.pieces:
            self.ahead, self.semaphores = 0, []

    def bind(self, ins, outs, scratch):
        self.place = own_place(self.sizes)
        if self.pieces:
            self.ins, self.outs, self.buffers = ins, outs, scratch[:-3]
            self.send_sem, self.recv_sem, self.own_sem = scratch[-3:]

    def window(self, number):
        _, row, rows, column, columns, _ = self.pieces[number]
        return (pl.ds(row, rows), pl.ds(column, columns))

    def remote(self, number, axis, step, source, target):
        before = AXES[: AXES.index(axis)]
        slot = sum(self.sizes[one] - 1 for one in before) + step - 1
        return pltpu.make_async_remote_copy(
            src_ref=source,
            dst_ref=target,
            send_sem=self.send_sem.at[number, slot],
            recv_sem=self.recv_sem.at[number, slot],
            device_id=device_of(peer_at(self.place, axis, step, self.sizes), self.sizes),
            device_id_type=MESH,
        )

    def numbers(self, step):
        return self.steps[step] if 0 <= step < len(self.steps) else ()

    def start(self, step, phase):
        for number in self.numbers(step):
            if phase == 0:
                self.own_copy(number).start()
            for copy in self.copies(number, phase):
                copy.start()

    def begin(self):
        for step in range(self.ahead):
            self.start(step, 0)

    def arrive(self, step, phase):
        for number in self.numbers(step):
            if phase == 0:
                self.own_copy(number).wait()
            for copy in self.copies(number, phase):
                copy.wait_recv()
            self.take(number, phase)

    def turns(self):
        def turn(index):
            self.start(index + self.ahead, 0)
            for phase in (3, 2, 1, 0):
                self.arrive(index - self.lag * phase, phase)
                if phase < 3:
                    self.start(index - self.lag * phase, phase + 1)

        count = len(self.steps) + 3 * self.lag if self.steps else 0
        return [functools.partial(turn, index) for index in range(count)]

    def end(self):
        for number in range(len(self.pieces)):
            for phase in range(4):
                for copy in self.copies(number, phase):
                    copy.wait_send()


class Gather(Flow):
    def __init__(self, kinds, shards, sizes, ahead, lag):
        super().__init__(kinds, shards, sizes, ahead, lag)
        lead = tuple(sizes[axis] for axis in AXES)
        self.out_shape = [jax.ShapeDtypeStruct(lead + one.shape, one.dtype) for one in shards]
        self.out_specs = [HBM] * len(shards)
        self.scratch = self.semaphores

    def own_copy(self, number):
        array, window = self.pieces[number][0], self.window(number)
        return pltpu.make_async_copy(
            self.ins[array].at[window],
            self.outs[array].at[region(self.place, (), window)],
            self.own_sem.at[number],
        )

    def copies(self, number, phase):
        array, order, window = self.pieces[number][0], self.pieces[number][-1], self.window(number)
        axis = (order + ("c",))[phase]
        part = self.outs[array].at[region(self.place, order[:phase], window)]
        source = self.ins[array].at[window] if phase == 0 else part
        return [
            self.remote(number, axis, step, source, part) for step in range(1, self.sizes[axis])
        ]

    def take(self, number, phase):
        pass


class Scatter(Flow):
    def __init__(self, kinds, grads, sizes, ahead, lag):
        grads = [
            grad.reshape(tuple(sizes[axis] for axis in AXES) + (-1, grad.shape[-1]))
            for grad in grads
        ]
        super().__init__(kinds, grads, sizes, ahead, lag)
        self.out_shape = [jax.ShapeDtypeStruct(grad.shape[-2:], jnp.float32) for grad in grads]
        self.out_specs = [VMEM] * len(grads)
        self.scratch = []
        for _, _, rows, _, columns, order in self.pieces:

            def shape_of(full, rows=rows, columns=columns):
                return tuple(sizes[axis] for axis in AXES if axis in full) + (rows, columns)

            self.scratch += [pltpu.VMEM(shape_of(order), jnp.bfloat16)] * 2
            for phase in range(3):
                senders = sizes[order[2 - phase]] - 1
                self.scratch.append(
                    pltpu.VMEM((senders,) + shape_of(order[: 2 - phase]), jnp.bfloat16)
                )
        self.scratch += self.semaphores

    def own_copy(self, number):
        array = self.pieces[number][0]
        return pltpu.make_async_copy(
            self.ins[array].at[region(self.place, AXES[:3], self.window(number))],
            self.buffers[5 * number],
            self.own_sem.at[number],
        )

    def copies(self, number, phase):
        array, order = self.pieces[number][0], self.pieces[number][-1]
        axis = "c" if phase == 0 else order[3 - phase]
        found = []
        for step in range(1, self.sizes[axis]):
            peer = peer_at(self.place, axis, step, self.sizes)
            if phase == 0:
                source = self.ins[array].at[region(peer, AXES[:3], self.window(number))]
                target = self.buffers[5 * number + 1]
            else:
                full = order[: 3 - phase]
                where = tuple(slice(None) if one in full else peer[one] for one in AXES[:3])
                source = self.buffers[5 * number].at[where]
                target = self.buffers[5 * number + 1 + phase].at[step - 1]
            found.append(self.remote(number, axis, step, source, target))
        return found

    def take(self, number, phase):
        array, order = self.pieces[number][0], self.pieces[number][-1]
        total = self.buffers[5 * number]
        got = self.buffers[5 * number + 1 + phase]
        if phase == 0:
            total[...] = total[...] + got[...]
            return
        full = order[: 3 - phase]
        where = tuple(slice(None) if axis in full else self.place[axis] for axis in AXES[:3])
        value = total[where]
        senders = self.sizes[order[3 - phase]] - 1
        if phase == 3:
            value = value.astype(jnp.float32)
            for sender in range(senders):
                value = value + got[sender].astype(jnp.float32)
            self.outs[array][self.window(number)] = value
        else:
            for sender in range(senders):
                value = value + got[sender]
            total[where] = value


def run_flow(flow, collective_id, name):
    count = len(flow.operands)

    def kernel(*refs):
        flow.bind(refs[:count], refs[count : 2 * count], refs[2 * count :])
        greet_axes(flow.place, flow.sizes)
        flow.begin()
        for turn in flow.turns():
            turn()
        flow.end()

    return pl.pallas_call(
        kernel,
        out_shape=flow.out_shape,
        in_specs=[HBM] * count,
        out_specs=flow.out_specs,
        scratch_shapes=flow.scratch,
        compiler_params=pltpu.CompilerParams(
            collective_id=collective_id, has_side_effects=True, vmem_limit_bytes=40 << 20
        ),
        cost_estimate=cost_of(30),
        name=name,
    )(*flow.operands)


def unit_place(unit, sizes):
    chips = sizes["x"] * sizes["y"]
    inside = quotient(unit, sizes["z"], chips * sizes["c"])
    row = quotient(inside, sizes["x"], sizes["y"] * sizes["c"])
    core = quotient(inside, chips, sizes["c"])
    x = inside - row * sizes["x"]
    y = wrapped(row - core * sizes["y"] + x, sizes["y"])
    return {"x": x, "z": unit - inside * sizes["z"], "y": y, "c": core}


def own_unit(sizes):
    place = own_place(sizes)
    turned = lax.rem(place["y"] + sizes["y"] * sizes["x"] - place["x"], sizes["y"])
    inside = (place["c"] * sizes["y"] + turned) * sizes["x"] + place["x"]
    return inside * sizes["z"] + place["z"]


class Exchange:
    def __init__(self, sizes, batches, sequences):
        self.sizes = sizes
        self.batches = batches
        self.sequences = sequences
        self.heads = sizes["x"]
        self.devices = math.prod(sizes.values())
        self.units = batches * sequences * HEADS
        self.blocks = self.devices // sequences
        self.held = batches * HEADS
        assert self.units <= self.devices

    def my_block(self):
        return lax.axis_index("seq") * self.heads + lax.axis_index("head")

    def unit_for(self, slot, block):
        batch = quotient(slot, HEADS, self.batches)
        sequence = quotient(block, self.blocks, self.sequences)
        return (batch * self.sequences + sequence) * HEADS + slot - batch * HEADS

    def block_device(self, block):
        return {"head": lax.rem(block, self.heads), "seq": lax.div(block, self.heads)}

    def token_device(self, unit, slot):
        if self.sequences > 1:
            slot = slot + lax.rem(lax.div(unit, HEADS), self.sequences) * self.blocks
        return self.block_device(slot)

    def unit_device(self, slot, block):
        return device_of(unit_place(self.unit_for(slot, block), self.sizes), self.sizes)

    def slot_of(self, unit):
        batch = lax.div(unit, HEADS * self.sequences)
        return lax.min(batch * HEADS + lax.rem(unit, HEADS), self.held - 1)

    def is_me(self, device):
        return jnp.logical_and(
            device["head"] == lax.axis_index("head"), device["seq"] == lax.axis_index("seq")
        )

    def greet_all(self):
        barrier = pltpu.get_barrier_semaphore()

        def greet(step, carry):
            device = self.block_device(lax.rem(self.my_block() + step, self.devices))
            pl.semaphore_signal(barrier, inc=1, device_id=device, device_id_type=MESH)
            return carry

        lax.fori_loop(1, self.devices, greet, 0)
        pl.semaphore_wait(barrier, self.devices - 1)

    def send(self, source, target, send_sem, recv_sem, own_sem, device, wait):
        same = self.is_me(device)
        remote = pltpu.make_async_remote_copy(
            src_ref=source,
            dst_ref=target,
            send_sem=send_sem,
            recv_sem=recv_sem,
            device_id=device,
            device_id_type=MESH,
        )
        if not wait:
            pl.when(same)(pltpu.make_async_copy(source, target, own_sem).start)

        @pl.when(jnp.logical_not(same))
        def _():
            remote.wait_send() if wait else remote.start()

    def receive(self, target, recv_sem, own_sem, device):
        same = self.is_me(device)

        @pl.when(same)
        def _():
            pltpu.make_async_copy(target, target, own_sem).wait()

        @pl.when(jnp.logical_not(same))
        def _():
            pltpu.make_async_copy(target, target, recv_sem).wait()

    def to_units(self, source_at, target_at, send_sem, recv_sem, own_sem, wait, part=0, parts=1):
        block = self.my_block()
        spot = block - quotient(block, self.blocks, self.sequences) * self.blocks
        turned = lax.rem(block, self.held)

        def one(index, carry):
            slot = wrapped(index + turned, self.held)
            self.send(
                source_at(slot),
                target_at(spot),
                send_sem.at[index],
                recv_sem.at[spot],
                own_sem,
                self.unit_device(slot, block),
                wait,
            )
            return carry

        lax.fori_loop(part * self.held // parts, (part + 1) * self.held // parts, one, 0)

    def at_unit(self, target_at, recv_sem, own_sem):
        unit = own_unit(self.sizes)

        def one(spot, carry):
            self.receive(
                target_at(spot), recv_sem.at[spot], own_sem, self.token_device(unit, spot)
            )
            return carry

        lax.fori_loop(0, self.blocks, one, 0)

    def to_token(self, spot, source_at, target_at, send_sem, recv_sem, own_sem, wait):
        unit = own_unit(self.sizes)
        slot = self.slot_of(unit)
        self.send(
            source_at(spot),
            target_at(slot),
            send_sem.at[spot],
            recv_sem.at[slot],
            own_sem,
            self.token_device(unit, spot),
            wait,
        )

    def at_tokens(self, target_at, recv_sem, own_sem):
        block = self.my_block()

        def one(slot, carry):
            self.receive(
                target_at(slot), recv_sem.at[slot], own_sem, self.unit_device(slot, block)
            )
            return carry

        lax.fori_loop(0, self.held, one, 0)


PART = 128
PER = TILE // PART
GUARD = WINDOW // TILE
REACH = 2 * GUARD + 1
DOC_ROWS = 64
FAR = -1e30
FORWARD_AHEAD, FORWARD_FIRST, FORWARD_LAG = 2, 8, 2
BACKWARD_AHEAD, BACKWARD_FIRST, BACKWARD_LAG = 2, 5, 2


def unit_context(lengths, exchange, tokens):
    unit = own_unit(exchange.sizes)
    row = lax.min(lax.div(unit, HEADS), exchange.batches * exchange.sequences - 1)
    head = lax.rem(unit, HEADS)
    own = lax.dynamic_index_in_dim(lengths.reshape(-1, lengths.shape[-1]), row, 0, keepdims=False)
    ends = jnp.cumsum(own)
    place = jnp.arange(tokens, dtype=jnp.int32)
    document = jnp.sum((place[None, :] >= ends[:, None]).astype(jnp.int32), axis=0)
    inside = jnp.arange(DOC_ROWS, dtype=jnp.int32)[:, None] == document[None, :]
    real = jnp.arange(DOC_ROWS, dtype=jnp.int32)[:, None] < lengths.shape[-1]
    of_query = jnp.where(inside, FAR, 0.0)
    of_key = jnp.where(real & ~inside, 1.0, 0.0)
    blocks = tokens // PART
    shape = (DOC_ROWS, blocks, PART)
    slope = jnp.exp2(-8.0 * (head + 1).astype(jnp.float32) / HEADS)
    return (
        (slope * LOG2E).reshape(1),
        of_query.reshape(shape).transpose(1, 0, 2).astype(jnp.bfloat16),
        of_key.reshape(shape).transpose(1, 0, 2).astype(jnp.bfloat16),
    )


def side_by_side(ref, tile, rows):
    return jnp.concatenate([ref[tile * PER + part, rows, :] for part in range(PER)], axis=1)


ROW_Q, ROW_K, ROW_V = slice(0, 64), slice(64, 128), slice(128, 192)


def rows_at(tile):
    return pl.ds(pl.multiple_of(tile * TILE, TILE), TILE)


def part_at(block):
    return pl.ds(pl.multiple_of(block * PART, PART), PART)


def fill_biases(slope_ref, bias_ref):
    key = lax.broadcasted_iota(jnp.int32, (TILE, TILE), 0)
    query = lax.broadcasted_iota(jnp.int32, (TILE, TILE), 1)

    def one(step, carry):
        distance = jnp.abs(key - query + (step - GUARD) * TILE)
        bias = distance.astype(jnp.float32) * -slope_ref[0]
        bias_ref[step] = jnp.where(distance < WINDOW, bias, FAR)
        return carry

    lax.fori_loop(0, REACH, one, 0)


def fill_guards(unit_ref, key_ref, blocks):
    rows = GUARD * TILE
    feature = lax.broadcasted_iota(jnp.int32, (rows, PART), 1)
    away = jnp.where((feature >= 64) & (feature < 72), 1.0, 0.0).astype(jnp.bfloat16)
    for first in (0, rows + blocks * PART):
        key_ref[pl.ds(first, rows), :] = away
    for first in (0, GUARD * PER + blocks):
        unit_ref[pl.ds(first, GUARD * PER)] = jnp.zeros(
            (GUARD * PER,) + unit_ref.shape[1:], unit_ref.dtype
        )


def fill_keys(unit_ref, doc_ref, key_ref, blocks):
    def one(block, carry):
        there = block + GUARD * PER
        features = jnp.concatenate([unit_ref[there, ROW_K, :], doc_ref[block]], axis=0)
        key_ref[part_at(there), :] = features.T
        return carry

    lax.fori_loop(0, blocks, one, 0, unroll=4)


class Service:
    def __init__(self, flow, first, tiles):
        self.turns = flow.turns()
        self.first = first
        self.after = {}
        left = max(len(self.turns) - first, 0)
        for index in range(left):
            self.after.setdefault(index * tiles // left, []).append(self.turns[first + index])

    def begin(self, done=0):
        for turn in self.turns[done : self.first]:
            turn()

    def at(self, tile):
        for index, turns in self.after.items():

            @pl.when(tile == index)
            def _(turns=turns):
                for turn in turns:
                    turn()


def attention_forward(packed, exchange, context, collective_id, flow, first):
    blocks, held = exchange.blocks, exchange.held
    tiles = blocks // PER
    edge = GUARD * PER

    count = len(flow.operands)

    def kernel(slope_ref, query_doc_ref, key_doc_ref, packed_ref, *refs):
        out_ref, keep_ref, wide_ref, sum_ref = refs[count : count + 4]
        flow.bind(refs[:count], refs[count + 4 : 2 * count + 4], refs[2 * count + 14 :])
        (
            unit_ref,
            key_ref,
            bias_ref,
            score_ref,
            result_ref,
            to_sem,
            at_sem,
            back_sem,
            home_sem,
            own_sem,
        ) = refs[2 * count + 4 : 2 * count + 14]
        service = Service(flow, first, tiles)
        has_unit = own_unit(exchange.sizes) < exchange.units
        exchange.greet_all()

        def units(wait, part=0, parts=1):
            exchange.to_units(
                lambda slot: packed_ref.at[slot],
                lambda spot: unit_ref.at[edge + spot],
                to_sem,
                at_sem,
                own_sem.at[0],
                wait,
                part,
                parts,
            )

        def tokens(spot, wait):
            exchange.to_token(
                spot,
                lambda spot: result_ref.at[spot],
                lambda slot: out_ref.at[slot],
                back_sem,
                home_sem,
                own_sem.at[1],
                wait,
            )

        keep = pltpu.make_async_copy(unit_ref.at[pl.ds(edge, blocks)], keep_ref, own_sem.at[2])
        flow.begin()
        parts = 3 if first > 2 else 1
        units(False, 0, parts)

        @pl.when(has_unit)
        def _():
            fill_biases(slope_ref, bias_ref)
            fill_guards(unit_ref, key_ref, blocks)

        for part in range(1, parts):
            service.turns[part - 1]()
            units(False, part, parts)
        service.begin(parts - 1)

        @pl.when(has_unit)
        def _():
            exchange.at_unit(lambda spot: unit_ref.at[edge + spot], at_sem, own_sem.at[0])
            keep.start()
            fill_keys(unit_ref, key_doc_ref, key_ref, blocks)

        def one_tile(tile, carry):
            @pl.when(has_unit)
            def _():
                q_t = jnp.concatenate(
                    [
                        side_by_side(unit_ref, tile + GUARD, ROW_Q),
                        side_by_side(query_doc_ref, tile, slice(0, DOC_ROWS)),
                    ],
                    axis=0,
                )
                top = jnp.full((1, TILE), FAR, jnp.float32)
                for step in range(REACH):
                    raw = jnp.dot(
                        key_ref[rows_at(tile + step), :], q_t, preferred_element_type=jnp.float32
                    )
                    score = raw * (HEAD_DIM ** (-0.5) * LOG2E) + bias_ref[step]
                    score_ref[step] = score
                    top = jnp.maximum(top, jnp.max(score, axis=0, keepdims=True))
                total = jnp.zeros((1, TILE), jnp.float32)
                attended = jnp.zeros((HEAD_DIM, TILE), jnp.float32)
                for step in range(REACH):
                    probs = jnp.exp2(score_ref[step] - top)
                    total = total + jnp.sum(probs, axis=0, keepdims=True)
                    attended = attended + jnp.dot(
                        side_by_side(unit_ref, tile + step, ROW_V),
                        probs.astype(jnp.bfloat16),
                        preferred_element_type=jnp.float32,
                    )
                result = attended / total
                sum_ref[tile] = top + jnp.log2(total)
                for part in range(PER):
                    piece = result[:, part * PART : (part + 1) * PART]
                    wide_ref[tile * PER + part] = piece
                    result_ref[tile * PER + part] = piece.astype(jnp.bfloat16)
                    tokens(tile * PER + part, False)

            service.at(tile)
            return carry

        lax.fori_loop(0, tiles, one_tile, 0)
        units(True)

        exchange.at_tokens(lambda slot: out_ref.at[slot], home_sem, own_sem.at[1])

        @pl.when(has_unit)
        def _():
            def sent(spot, carry):
                tokens(spot, True)
                return carry

            lax.fori_loop(0, blocks, sent, 0)
            keep.wait()

        flow.end()

    return pl.pallas_call(
        kernel,
        out_shape=[
            jax.ShapeDtypeStruct((held, HEAD_DIM, PART), jnp.bfloat16),
            jax.ShapeDtypeStruct((blocks, 3 * HEAD_DIM, PART), jnp.bfloat16),
            jax.ShapeDtypeStruct((blocks, HEAD_DIM, PART), jnp.float32),
            jax.ShapeDtypeStruct((tiles, 1, TILE), jnp.float32),
        ]
        + flow.out_shape,
        in_specs=[SMEM, VMEM, VMEM, HBM] + [HBM] * count,
        out_specs=[HBM, HBM, VMEM, VMEM] + flow.out_specs,
        scratch_shapes=[
            pltpu.VMEM((blocks + 2 * edge, 3 * HEAD_DIM, PART), jnp.bfloat16),
            pltpu.VMEM(((blocks + 2 * edge) * PART, PART), jnp.bfloat16),
            pltpu.VMEM((REACH, TILE, TILE), jnp.float32),
            pltpu.VMEM((REACH, TILE, TILE), jnp.float32),
            pltpu.VMEM((blocks, HEAD_DIM, PART), jnp.bfloat16),
            pltpu.SemaphoreType.DMA((held,)),
            pltpu.SemaphoreType.DMA((blocks,)),
            pltpu.SemaphoreType.DMA((blocks,)),
            pltpu.SemaphoreType.DMA((held,)),
            pltpu.SemaphoreType.DMA((3,)),
        ]
        + flow.scratch,
        compiler_params=pltpu.CompilerParams(
            collective_id=collective_id, has_side_effects=True, vmem_limit_bytes=48 << 20
        ),
        cost_estimate=cost_of(60),
        name="attention_forward",
    )(*context, packed, *flow.operands)


def attention_backward(grad, unit_kept, exchange, context, collective_id, flow, first):
    blocks, held = exchange.blocks, exchange.held
    tiles = blocks // PER
    edge = GUARD * PER

    count = len(flow.operands)

    def kernel(
        slope_ref, query_doc_ref, key_doc_ref, wide_ref, sum_ref, grad_ref, kept_ref, *refs
    ):
        out_ref = refs[count]
        flow.bind(refs[:count], refs[count + 1 : 2 * count + 1], refs[2 * count + 13 :])
        (
            unit_ref,
            got_ref,
            key_ref,
            value_ref,
            bias_ref,
            total_ref,
            result_ref,
            to_sem,
            at_sem,
            back_sem,
            home_sem,
            own_sem,
        ) = refs[2 * count + 1 : 2 * count + 13]
        service = Service(flow, first, tiles)
        has_unit = own_unit(exchange.sizes) < exchange.units
        exchange.greet_all()

        def units(wait):
            exchange.to_units(
                lambda slot: grad_ref.at[slot],
                lambda spot: got_ref.at[spot],
                to_sem,
                at_sem,
                own_sem.at[0],
                wait,
            )

        def tokens(spot, wait):
            exchange.to_token(
                spot,
                lambda spot: result_ref.at[spot],
                lambda slot: out_ref.at[slot],
                back_sem,
                home_sem,
                own_sem.at[1],
                wait,
            )

        load = pltpu.make_async_copy(kept_ref, unit_ref.at[pl.ds(edge, blocks)], own_sem.at[2])
        flow.begin()
        units(False)

        @pl.when(has_unit)
        def _():
            load.start()
            fill_biases(slope_ref, bias_ref)
            fill_guards(unit_ref, key_ref, blocks)
            for first in (0, (edge + blocks) * PART):
                value_ref[pl.ds(first, edge * PART), :] = jnp.zeros(
                    (edge * PART, PART), value_ref.dtype
                )
            total_ref[...] = jnp.zeros_like(total_ref)
            load.wait()
            fill_keys(unit_ref, key_doc_ref, key_ref, blocks)

            def one(block, carry):
                there = block + edge
                value_ref[part_at(there), :] = unit_ref[there, 64:192, :].T
                return carry

            lax.fori_loop(0, blocks, one, 0, unroll=4)

        service.begin()

        @pl.when(has_unit)
        def _():
            exchange.at_unit(lambda spot: got_ref.at[spot], at_sem, own_sem.at[0])

        def finish(tile):
            for part in range(PER):
                block = tile * PER + part
                result_ref[block, 64:192, :] = total_ref[part_at(block + edge), :].T.astype(
                    jnp.bfloat16
                )
                tokens(block, False)

        def one_tile(tile, carry):
            @pl.when(has_unit)
            def _():
                q_part = side_by_side(unit_ref, tile + GUARD, ROW_Q)
                g_part = side_by_side(got_ref, tile, slice(0, 64))
                q_t = jnp.concatenate(
                    [q_part, side_by_side(query_doc_ref, tile, slice(0, DOC_ROWS))], axis=0
                )
                g_small = g_part * jnp.asarray(HEAD_DIM ** (-0.5), jnp.bfloat16)
                g_t = jnp.concatenate([jnp.zeros_like(g_small), g_small], axis=0)
                turned = jnp.concatenate([q_part, g_part], axis=0).T
                lane = lax.broadcasted_iota(jnp.int32, turned.shape, 1)
                none = jnp.zeros_like(turned)
                q_and_g = jnp.concatenate(
                    [jnp.where(lane < 64, turned, none), jnp.where(lane < 64, none, turned)],
                    axis=0,
                )
                wide_t = side_by_side(wide_ref, tile, slice(0, 64))
                mean = jnp.sum(g_small.astype(jnp.float32) * wide_t, axis=0, keepdims=True)
                sum_now = sum_ref[tile]
                grad_q = jnp.zeros((HEAD_DIM, TILE), jnp.float32)
                for step in range(REACH):
                    there = rows_at(tile + step)
                    raw = jnp.dot(key_ref[there, :], q_t, preferred_element_type=jnp.float32)
                    grad_probs = jnp.dot(
                        value_ref[there, :], g_t, preferred_element_type=jnp.float32
                    )
                    score = raw * (HEAD_DIM ** (-0.5) * LOG2E) + bias_ref[step]
                    probs = jnp.exp2(score - sum_now)
                    grad_raw = (probs * (grad_probs - mean)).astype(jnp.bfloat16)
                    total_ref[there, :] += jnp.dot(
                        jnp.concatenate([grad_raw, probs.astype(jnp.bfloat16)], axis=1),
                        q_and_g,
                        preferred_element_type=jnp.float32,
                    )
                    grad_q = grad_q + jnp.dot(
                        side_by_side(unit_ref, tile + step, ROW_K),
                        grad_raw,
                        preferred_element_type=jnp.float32,
                    )
                for part in range(PER):
                    result_ref[tile * PER + part, ROW_Q, :] = grad_q[
                        :, part * PART : (part + 1) * PART
                    ].astype(jnp.bfloat16)

                @pl.when(tile >= GUARD)
                def _():
                    finish(tile - GUARD)

            service.at(tile)
            return carry

        lax.fori_loop(0, tiles, one_tile, 0)
        units(True)

        @pl.when(has_unit)
        def _():
            def rest(tile, carry):
                finish(tile)
                return carry

            lax.fori_loop(max(tiles - GUARD, 0), tiles, rest, 0)

        exchange.at_tokens(lambda slot: out_ref.at[slot], home_sem, own_sem.at[1])

        @pl.when(has_unit)
        def _():
            def sent(spot, carry):
                tokens(spot, True)
                return carry

            lax.fori_loop(0, blocks, sent, 0)

        flow.end()

    return pl.pallas_call(
        kernel,
        out_shape=[jax.ShapeDtypeStruct((held, 3 * HEAD_DIM, PART), jnp.bfloat16)] + flow.out_shape,
        in_specs=[SMEM, VMEM, VMEM, VMEM, VMEM, HBM, HBM] + [HBM] * count,
        out_specs=[HBM] + flow.out_specs,
        scratch_shapes=[
            pltpu.VMEM((blocks + 2 * edge, 3 * HEAD_DIM, PART), jnp.bfloat16),
            pltpu.VMEM((blocks, HEAD_DIM, PART), jnp.bfloat16),
            pltpu.VMEM(((blocks + 2 * edge) * PART, PART), jnp.bfloat16),
            pltpu.VMEM(((blocks + 2 * edge) * PART, PART), jnp.bfloat16),
            pltpu.VMEM((REACH, TILE, TILE), jnp.float32),
            pltpu.VMEM(((blocks + 2 * edge) * PART, PART), jnp.float32),
            pltpu.VMEM((blocks, 3 * HEAD_DIM, PART), jnp.bfloat16),
            pltpu.SemaphoreType.DMA((held,)),
            pltpu.SemaphoreType.DMA((blocks,)),
            pltpu.SemaphoreType.DMA((blocks,)),
            pltpu.SemaphoreType.DMA((held,)),
            pltpu.SemaphoreType.DMA((3,)),
        ]
        + flow.scratch,
        compiler_params=pltpu.CompilerParams(
            collective_id=collective_id, has_side_effects=True, vmem_limit_bytes=60 << 20
        ),
        cost_estimate=cost_of(70),
        name="attention_backward",
    )(*context, *unit_kept[1:], grad, unit_kept[0], *flow.operands)


def layer_norm(summed, gain, shift):
    centre = jnp.mean(summed, axis=-1, keepdims=True)
    centred = summed - centre
    variance = jnp.mean(centred * centred, axis=-1, keepdims=True)
    return centred * lax.rsqrt(variance + 1e-12) * gain + shift


def normal_share(gate):
    return 0.5 * lax.erf(gate * math.sqrt(0.5)) + 0.5


def geglu(gate, upper):
    return gate * normal_share(gate) * upper


def geglu_backward(gate, upper, grad):
    share = normal_share(gate)
    slope = share + gate * jnp.exp(-0.5 * gate * gate) * (1.0 / math.sqrt(2.0 * math.pi))
    return grad * upper * slope, grad * (gate * share)


def dot(a, b, a_axis, b_axis):
    return lax.dot_general(
        a, b, (((a_axis,), (b_axis,)), ((), ())), preferred_element_type=jnp.float32
    )


def layer_forward(hidden, qkv_w, others, kinds, shards, exchange, context, collective_id):
    batches = exchange.batches
    tokens = hidden.shape[0] // batches
    hidden_low = hidden.astype(jnp.bfloat16)
    packed = dot(qkv_w, hidden_low, 0, 1).astype(jnp.bfloat16)
    packed = with_layout_constraint(packed, Layout((0, 1)))
    packed = packed.reshape(3, HEADS, HEAD_DIM, batches, tokens)
    packed = packed.transpose(3, 1, 0, 2, 4).reshape(batches * HEADS, 3 * HEAD_DIM, tokens)
    attended, unit_packed, wide, sums, *gathered = attention_forward(
        packed,
        exchange,
        context,
        collective_id,
        Gather(kinds, shards, exchange.sizes, FORWARD_AHEAD, FORWARD_LAG),
        FORWARD_FIRST if kinds else 0,
    )
    gathered = [one.reshape(-1, one.shape[-1]) for one in gathered]
    out_w, up_w, down_w = others + gathered
    norm_f = out_w[:, D : D + 4].astype(jnp.float32)
    out_w = out_w[:, :D]
    attn_t = attended.reshape(batches, D, tokens)
    attn_low = attn_t.transpose(0, 2, 1).reshape(batches * tokens, D)
    mixed = hidden + dot(attn_low, out_w, 1, 0)
    normed = layer_norm(mixed, norm_f[:, 0], norm_f[:, 1])
    normed_low = normed.astype(jnp.bfloat16)
    upper = dot(normed_low, up_w, 1, 0)
    act_low = geglu(upper[:, :FF], upper[:, FF:]).astype(jnp.bfloat16)
    second = normed + dot(act_low, down_w, 1, 0)
    result = layer_norm(second, norm_f[:, 2], norm_f[:, 3])
    weights = (qkv_w, out_w, up_w, down_w, norm_f)
    unit_kept = (unit_packed, wide, sums)
    kept = (hidden_low, unit_kept, attn_low, mixed, normed_low, upper, act_low, second)
    return result, weights, kept


def layer_backward(grad_result, weights, kept, exchange, context, collective_id):
    qkv_w, out_w, up_w, down_w, norm_f = weights
    hidden_low, unit_kept, attn_low, mixed, normed_low, upper, act_low, second = kept
    batches = exchange.batches
    tokens = grad_result.shape[0] // batches
    pull_two = jax.vjp(layer_norm, second, norm_f[:, 2], norm_f[:, 3])[1]
    grad_second, grad_gain_two, grad_shift_two = pull_two(grad_result)
    grad_branch = grad_second.astype(jnp.bfloat16)
    grad_act = dot(grad_branch, down_w, 1, 1)
    grad_gate, grad_upper = geglu_backward(upper[:, :FF], upper[:, FF:], grad_act)
    grad_up_low = jnp.concatenate([grad_gate, grad_upper], axis=1).astype(jnp.bfloat16)
    grad_normed = grad_second + dot(grad_up_low, up_w, 1, 1)
    pull_one = jax.vjp(layer_norm, mixed, norm_f[:, 0], norm_f[:, 1])[1]
    grad_mixed, grad_gain_one, grad_shift_one = pull_one(grad_normed)
    grad_attn = grad_mixed.astype(jnp.bfloat16)
    grad_heads = dot(out_w, grad_attn, 1, 1).astype(jnp.bfloat16)
    grad_heads = grad_heads.reshape(HEADS, HEAD_DIM, batches, tokens)
    grad_heads = grad_heads.transpose(2, 0, 1, 3).reshape(batches * HEADS, HEAD_DIM, tokens)
    grad_norm = jnp.stack([grad_gain_one, grad_shift_one, grad_gain_two, grad_shift_two], axis=1)
    grad_out_w = jnp.concatenate(
        [
            dot(attn_low, grad_attn, 0, 0).astype(jnp.bfloat16),
            jnp.pad(grad_norm.astype(jnp.bfloat16), ((0, 0), (0, NORM_PAD - 4))),
        ],
        axis=1,
    )
    grad_up_w = dot(normed_low, grad_up_low, 0, 0).astype(jnp.bfloat16)
    grad_down_w = dot(act_low, grad_branch, 0, 0).astype(jnp.bfloat16)
    flow = Scatter(
        ["down", "up", "out"],
        [grad_down_w, grad_up_w, grad_out_w],
        exchange.sizes,
        BACKWARD_AHEAD,
        BACKWARD_LAG,
    )
    packed_grad, *totals = attention_backward(
        grad_heads,
        unit_kept,
        exchange,
        context,
        collective_id,
        flow,
        BACKWARD_FIRST,
    )
    packed_grad = packed_grad.reshape(batches, HEADS, 3, HEAD_DIM, tokens)
    packed_grad = packed_grad.transpose(0, 4, 2, 1, 3).reshape(batches * tokens, 3 * D)
    grad_hidden = grad_mixed + dot(packed_grad, qkv_w, 1, 1)
    grad_qkv_w = dot(hidden_low, packed_grad, 0, 0).astype(jnp.bfloat16)
    return grad_hidden, grad_qkv_w, totals


def adamw(weight, first, second, grad, rate):
    first_new = beta_one * first + (1.0 - beta_one) * grad
    second_new = beta_two * second + (1.0 - beta_two) * grad * grad
    first_hat = first_new / (1.0 - beta_one**STEP)
    second_hat = second_new / (1.0 - beta_two**STEP)
    weight_new = weight - rate * (first_hat / (jnp.sqrt(second_hat) + adam_eps) + decay * weight)
    return (first_new, second_new, weight_new)


def body(
    inputs,
    cotangent,
    lengths,
    qkv_weight,
    qkv_first,
    qkv_second,
    out_weight,
    out_first,
    out_second,
    up_weight,
    up_first,
    up_second,
    down_weight,
    down_first,
    down_second,
    norm_params,
    norm_first,
    norm_second,
):
    masters = (qkv_weight, out_weight, up_weight, down_weight, norm_params)
    states = (
        (qkv_first, qkv_second),
        (out_first, out_second),
        (up_first, up_second),
        (down_first, down_second),
        (norm_first, norm_second),
    )
    sizes = grid_sizes(lax.axis_size("seq"))
    batches, tokens = inputs.shape[:2]
    exchange = Exchange(sizes, batches, lengths.shape[1])
    context = unit_context(lengths, exchange, exchange.blocks * tokens)
    norm_wide = jnp.pad(norm_params, ((0, 0), (0, 0), (0, NORM_PAD - 4)))
    sources = (qkv_weight, jnp.concatenate([out_weight, norm_wide], axis=2), up_weight, down_weight)
    shards = [[source[layer].astype(jnp.bfloat16) for source in sources] for layer in range(LAYERS)]
    qkv_w = run_flow(Gather(["qkv"], shards[0][:1], sizes, 2, 1), 0, "gather_weights")[0]
    qkv_w = qkv_w.reshape(-1, qkv_w.shape[-1])
    everyone = ("head", "seq")
    later = [lax.all_gather(shard, everyone, axis=0, tiled=True) for shard in shards[1]]

    hidden = inputs.reshape(batches * tokens, D).astype(jnp.float32)
    weights_all, kept_all = [], []
    for layer in range(LAYERS):
        hidden, weights, kept = layer_forward(
            hidden,
            later[0] if layer else qkv_w,
            later[1:] if layer else [],
            [] if layer else ["out", "up", "down"],
            [] if layer else shards[0][1:],
            exchange,
            context,
            1 + layer,
        )
        weights_all.append(weights)
        kept_all.append(kept)
    outputs = hidden.reshape(batches, tokens, D)
    grad_hidden = cotangent.reshape(batches * tokens, D).astype(jnp.float32)
    totals = [[None] * 4 for _ in range(LAYERS)]
    late = []
    for layer in reversed(range(LAYERS)):
        grad_hidden, grad_qkv_w, done = layer_backward(
            grad_hidden,
            weights_all[layer],
            kept_all[layer],
            exchange,
            context,
            1 + LAYERS + layer,
        )
        totals[layer][3], totals[layer][2], totals[layer][1] = done
        late.append(grad_qkv_w)
    last = Scatter(["qkv"] * LAYERS, late, sizes, 2, 2)
    totals[1][0], totals[0][0] = run_flow(last, 1 + 2 * LAYERS, "scatter_grads")
    input_grad = grad_hidden.reshape(batches, tokens, D)

    results = [outputs, input_grad]
    kinds = [
        jnp.stack([totals[layer][0] for layer in range(LAYERS)]),
        jnp.stack([totals[layer][1][:, :D] for layer in range(LAYERS)]),
        jnp.stack([totals[layer][2] for layer in range(LAYERS)]),
        jnp.stack([totals[layer][3] for layer in range(LAYERS)]),
        jnp.stack([totals[layer][1][:, D : D + 4] for layer in range(LAYERS)]),
    ]
    new_weights = []
    for kind in range(5):
        first_new, second_new, weight_new = adamw(
            masters[kind], states[kind][0], states[kind][1], kinds[kind], learn_rates[kind]
        )
        results += [kinds[kind], first_new, second_new, weight_new]
        new_weights.append(weight_new)
    results += [member.astype(jnp.bfloat16) for member in new_weights[:4]]
    return tuple(results)


def solution(mesh):
    tokens = P(None, ("seq", "head"), None)
    rows = P(None, ("head", "seq"), None)
    in_specs = (tokens, tokens, P()) + (rows,) * 15
    out_specs = (tokens, tokens) + (rows,) * 24
    return jax.shard_map(body, mesh=mesh, in_specs=in_specs, out_specs=out_specs, check_vma=False)
```
